32 devices in a mesh: shot: 4 (over y, x), dom: 8 (over z, core).
Axes of the slice: x: 2, y: 2, z: 4, core: 2. Of those that a mesh axis runs over, the one named last changes fastest.
Arguments:
- forward: float32 [8, 9, 125, 2048], P('shot', None, None, 'dom'), may hold values from -6 to 6
- adjoint: float32 [8, 9, 125, 2048], P('shot', None, None, 'dom'), may hold values from -6 to 6
- material: float32 [3, 125, 2048], P(None, None, 'dom'), may hold values from 0.5 to 2
- counts: int32 [8], P('dom'), may hold values from 64 to 256, as said below
- send_list: int32 [8, 4, 32], P('dom'), may hold values from 0 to 256, as said below
- neighbours: int32 [8, 1536], P('dom'), may hold values from 0 to 1665, as said below
Outputs:
- forward_next: float32 [8, 9, 125, 2048], P('shot', None, None, 'dom')
- adjoint_next: float32 [8, 9, 125, 2048], P('shot', None, None, 'dom')
- gradient: float32 [3, 125, 2048], P(None, None, 'dom')
The draws below stay inside these ranges and needn't reach their ends.
Inputs may be any that keep to these rules, and one draw needn't show every extreme that they name: Device d holds counts[d] octants in its first slots, in Morton order of its tree; some device holds 256 and some device holds only one layer, 64. `send_list`: entry [d, s, p] is the slot of device d's octant on lateral side s (-x, +x, -y, +y) at position p = (horizontal coordinate along the side) * 4 + layer, or 256 where the position holds no octant; every listed slot is live. `neighbours`: codes as in the reference program: a code below 1536 names a live local face; a ghost code names a position whose octant the neighbouring tree lists; 1665 marks an absorbing boundary and is also given for every face of a slot that is not live.
All inputs are finite; a program needn't handle non-finite values.
Results may differ from the reference program's by a relative error of at most 0.0003.
Values sent between devices are 32-bit elements; how exact they have to be, the bound alone decides.
No kernel may reach another device: no remote copies, remote signals or barrier semaphores. Data moves between devices by JAX's collectives and lax.ppermute only.
A program may use at most 192 MiB of HBM per device.

```python
import math
import jax
import jax.numpy as jnp
import numpy as np
from jax import lax

BOX = 8
EZ = 4
DEV_Y = 4
NODES = 125
FIELDS = 9
OCT_DEV = 256
SHOTS = 8
OCTANTS = 2048
N_DOM = 8


def forest_layout(key):
    layers = EZ
    devices = N_DOM
    slot_count = BOX * BOX * layers
    side_length = BOX * layers
    rows_of_trees = devices // DEV_Y
    layout_key = jax.random.fold_in(key, 4242)
    key_level, key_vary, key_full, key_low = jax.random.split(layout_key, 4)
    device_ids = jnp.arange(devices, dtype=jnp.int32)
    tall_tree = jax.random.randint(key_level, (devices,), 0, 5) == 0
    full_device = jax.random.randint(key_full, (), 0, devices)
    low_device = (full_device + 1 + jax.random.randint(key_low, (), 0, devices - 1)) % devices
    levels = jnp.where(tall_tree, layers, 1)
    variation = jax.random.randint(key_vary, (devices, BOX, BOX), -1, 2)
    heights = jnp.clip(levels[:, None, None] + variation, 1, layers)
    heights = jnp.where((device_ids == full_device)[:, None, None], layers, heights)
    heights = jnp.where((device_ids == low_device)[:, None, None], 1, heights)
    grid_x, grid_y, grid_z = jnp.meshgrid(jnp.arange(BOX, dtype=jnp.int32), jnp.arange(BOX, dtype=jnp.int32), jnp.arange(layers, dtype=jnp.int32), indexing='ij')
    morton = jnp.zeros_like(grid_x)
    for bit_number in range(5):
        morton = morton + ((grid_x >> bit_number & 1) << 3 * bit_number + 2)
        morton = morton + ((grid_y >> bit_number & 1) << 3 * bit_number + 1)
        morton = morton + ((grid_z >> bit_number & 1) << 3 * bit_number)
    live_cells = grid_z[None] < heights[:, :, :, None]
    sort_key = morton[None] + jnp.where(live_cells, 0, 65536)
    position_of = jnp.argsort(sort_key.reshape(devices, slot_count), axis=1).astype(jnp.int32)
    slot_of = jnp.argsort(position_of, axis=1).astype(jnp.int32)
    slot_cells = slot_of.reshape(devices, BOX, BOX, layers)
    counts = jnp.sum(live_cells.reshape(devices, slot_count).astype(jnp.int32), axis=1).astype(jnp.int32)
    free_code = 6 * slot_count + 4 * side_length
    absorb_code = free_code + 1
    tree_x = device_ids // DEV_Y
    tree_y = device_ids % DEV_Y
    grids = (grid_x, grid_y, grid_z)
    extents = (BOX, BOX, layers)
    per_face = []
    for face_id in range(6):
        direction = face_id // 2
        sign = 1 if face_id % 2 == 1 else -1
        opposite = face_id + 1 if face_id % 2 == 0 else face_id - 1
        moved_coord = grids[direction] + sign
        inside = (moved_coord >= 0) & (moved_coord < extents[direction])
        next_live = jnp.roll(live_cells, -sign, axis=1 + direction)
        next_slot = jnp.roll(slot_cells, -sign, axis=1 + direction)
        local_value = jnp.where(next_live, opposite * slot_count + next_slot, free_code)
        edge = 0 if sign > 0 else BOX - 1
        if direction == 2:
            outside_value = jnp.full(live_cells.shape, absorb_code if sign < 0 else free_code, jnp.int32)
        elif direction == 0:
            exists = (tree_x + sign >= 0) & (tree_x + sign < rows_of_trees)
            column = jnp.roll(heights, -sign * DEV_Y, axis=0)[:, edge, :]
            ghost_live = grid_z[None] < column[:, None, :, None]
            ghost_value = 6 * slot_count + face_id * side_length + grid_y * layers + grid_z
            outside_value = jnp.where(exists[:, None, None, None], jnp.where(ghost_live, ghost_value[None], free_code), absorb_code)
        else:
            exists = (tree_y + sign >= 0) & (tree_y + sign < DEV_Y)
            column = jnp.roll(heights, -sign, axis=0)[:, :, edge]
            ghost_live = grid_z[None] < column[:, :, None, None]
            ghost_value = 6 * slot_count + face_id * side_length + grid_x * layers + grid_z
            outside_value = jnp.where(exists[:, None, None, None], jnp.where(ghost_live, ghost_value[None], free_code), absorb_code)
        combined = jnp.where(inside[None], local_value, outside_value)
        combined = jnp.where(live_cells, combined, absorb_code)
        per_face.append(combined.reshape(devices, slot_count))
    stacked = jnp.stack(per_face, axis=1)
    gather_index = jnp.broadcast_to(position_of[:, None, :], stacked.shape)
    neighbours = jnp.take_along_axis(stacked, gather_index, axis=2).reshape(devices, 6 * slot_count).astype(jnp.int32)
    side_slots = (slot_cells[:, 0], slot_cells[:, BOX - 1], slot_cells[:, :, 0], slot_cells[:, :, BOX - 1])
    side_lives = (live_cells[:, 0], live_cells[:, BOX - 1], live_cells[:, :, 0], live_cells[:, :, BOX - 1])
    send_list = jnp.stack([jnp.where(alive, slots_here, slot_count).reshape(devices, side_length) for alive, slots_here in zip(side_lives, side_slots)], axis=1).astype(jnp.int32)
    return (counts, send_list, neighbours)


def draw_counts(key, part):
    return forest_layout(key)[0]


def draw_send_list(key, part):
    return forest_layout(key)[1]


def draw_neighbours(key, part):
    return forest_layout(key)[2]


def block_scale(stream_key, shape, cuts, low, top_value):
    factor_of = 1.0
    for dim, shards_of in cuts:
        steps = jax.random.uniform(jax.random.fold_in(jax.random.fold_in(stream_key, 6), dim), (shards_of,), jnp.float32, low / len(cuts), top_value / len(cuts))
        factor_of = factor_of * jnp.repeat(jnp.exp(steps), shape[dim] // shards_of).reshape((-1,) + (1,) * (len(shape) - 1 - dim))
    return factor_of


def centred(own_key, extent, scale, bound, cuts=(), kind=jnp.bfloat16):
    drawn = scale * jax.random.normal(own_key, extent, jnp.float32)
    if cuts:
        drawn = drawn * block_scale(own_key, extent, cuts, -0.22, 0.18)
    return jnp.clip(drawn, -bound, bound).astype(kind)


def setup_inputs(seed: int = 0) -> dict:
    key_list = jax.random.split(jax.random.key(seed), 7)
    forward = centred(key_list[0], (SHOTS, FIELDS, NODES, OCTANTS), 1.0, 6.0, ((0, 4), (3, 8)), jnp.float32)
    adjoint = centred(key_list[1], (SHOTS, FIELDS, NODES, OCTANTS), 1.0, 6.0, ((0, 4), (3, 8)), jnp.float32)
    material = jnp.clip(jnp.exp(math.log(2.0) - 1.3862944 * jax.random.uniform(key_list[2], (3, NODES, OCTANTS), jnp.float32) ** block_scale(key_list[2], (3, NODES, OCTANTS), ((2, 8),), -0.2, 0.2)), 0.5, 2.0)
    counts = draw_counts(jax.random.fold_in(key_list[6], 71), 0)
    send_list = draw_send_list(jax.random.fold_in(key_list[6], 71), 0)
    neighbours = draw_neighbours(jax.random.fold_in(key_list[6], 71), 0)
    return {"forward": forward, "adjoint": adjoint, "material": material, "counts": counts, "send_list": send_list, "neighbours": neighbours}


step_size = 0.01
lift_weight = 10.0
highest = lax.Precision.HIGHEST
stress_slots = ((3, 8, 7), (8, 4, 6), (7, 6, 5))
symmetric_pairs = ((0, 0), (1, 1), (2, 2), (1, 2), (0, 2), (0, 1))

def derivative_matrix():
    points = np.array([-1.0, -np.sqrt(3.0 / 7.0), 0.0, np.sqrt(3.0 / 7.0), 1.0])
    barycentric = np.array([1.0 / np.prod([points[a] - points[b] for b in range(5) if b != a]) for a in range(5)])
    matrix = np.zeros((5, 5))
    for a in range(5):
        for b in range(5):
            if a != b:
                matrix[a, b] = barycentric[b] / barycentric[a] / (points[a] - points[b])
        matrix[a, a] = -np.sum(matrix[a])
    return jnp.asarray(matrix, dtype=jnp.float32)

def split_nodes(values):
    return values.reshape(values.shape[:2] + (5, 5, 5) + values.shape[3:])

def derivative_parts(states):
    matrix = derivative_matrix()
    shaped = split_nodes(states)
    along_x = jnp.einsum('ai,sfijk...->sfajk...', matrix, shaped, precision=highest)
    along_y = jnp.einsum('aj,sfijk...->sfiak...', matrix, shaped, precision=highest)
    along_z = jnp.einsum('ak,sfijk...->sfija...', matrix, shaped, precision=highest)
    return tuple((part.reshape(states.shape) for part in (along_x, along_y, along_z)))

def volume_terms(derivs, medium):
    lame_first = medium[:, 0]
    shear_modulus = medium[:, 1]
    buoyancy = medium[:, 2]
    divergence = derivs[0][:, 0] + derivs[1][:, 1] + derivs[2][:, 2]
    stress_div = [sum((derivs[d][:, stress_slots[a][d]] for d in range(3))) for a in range(3)]
    rates = [derivs[a][:, b] + derivs[b][:, a] for a, b in symmetric_pairs]
    flux_rows = [buoyancy * part for part in stress_div]
    for pair_id, (a, b) in enumerate(symmetric_pairs):
        stress_row = shear_modulus * rates[pair_id]
        if a == b:
            stress_row = stress_row + lame_first * divergence
        flux_rows.append(stress_row)
    return (jnp.stack(flux_rows, axis=1), (divergence, rates, stress_div))

def material_partials(rate_parts, dual):
    divergence, rates, stress_div = rate_parts
    pressure_part = divergence * (dual[:, 3] + dual[:, 4] + dual[:, 5])
    shear_part = sum((rates[n] * dual[:, 3 + n] for n in range(6)))
    buoyancy_part = sum((stress_div[a] * dual[:, a] for a in range(3)))
    return jnp.stack([pressure_part, shear_part, buoyancy_part], axis=1)

def face_of(values, face_id):
    shaped = split_nodes(values)
    position = 0 if face_id % 2 == 0 else 4
    picked = lax.index_in_dim(shaped, position, axis=2 + face_id // 2, keepdims=False)
    return picked.reshape(values.shape[:2] + (25,) + values.shape[3:])

def face_traces(values):
    return jnp.concatenate([face_of(values, face_id) for face_id in range(6)], axis=-1)

def add_face(tendency, face_id, values):
    shaped = values.reshape(values.shape[:2] + (5, 5) + values.shape[3:])
    selector = [slice(None)] * tendency.ndim
    selector[2 + face_id // 2] = 0 if face_id % 2 == 0 else 4
    return tendency.at[tuple(selector)].add(shaped)

def surface_terms(volume, jump_all, medium_faces, slot_count):
    tendency = split_nodes(volume)
    for face_id in range(6):
        direction = face_id // 2
        normal = -1.0 if face_id % 2 == 0 else 1.0
        window = slice(face_id * slot_count, (face_id + 1) * slot_count)
        jump_piece = jump_all[..., window]
        lame_first = medium_faces[:, 0, :, window]
        shear_modulus = medium_faces[:, 1, :, window]
        buoyancy = medium_faces[:, 2, :, window]
        wave_speed = jnp.sqrt((lame_first + 2.0 * shear_modulus) * buoyancy)
        flux_rows = [buoyancy * jump_piece[:, stress_slots[a][direction]] for a in range(3)]
        for a, b in symmetric_pairs:
            flux_terms = []
            if a == b:
                flux_terms.append(lame_first * jump_piece[:, direction])
            if direction == a:
                flux_terms.append(shear_modulus * jump_piece[:, b])
            if direction == b:
                flux_terms.append(shear_modulus * jump_piece[:, a])
            flux_rows.append(sum(flux_terms) if flux_terms else None)
        corrections = []
        for field_id in range(9):
            amount = wave_speed * jump_piece[:, field_id]
            if flux_rows[field_id] is not None:
                amount = amount + normal * flux_rows[field_id]
            corrections.append(0.5 * lift_weight * amount)
        tendency = add_face(tendency, face_id, jnp.stack(corrections, axis=1))
    return tendency.reshape(volume.shape)

def shift_devices(values, offset):
    padding = jnp.zeros((abs(offset),) + values.shape[1:], values.dtype)
    if offset > 0:
        return jnp.concatenate([padding, values[:-offset]], axis=0)
    return jnp.concatenate([values[-offset:], padding], axis=0)

def ghost_reference(traces, send_list, slot_count):
    sent = []
    for side_id in range(4):
        listed = send_list[:, side_id]
        target = jnp.where(listed < slot_count, side_id * slot_count + listed, 6 * slot_count)
        target = jnp.broadcast_to(target[:, None, None, :], traces.shape[:3] + (listed.shape[1],))
        sent.append(jnp.take_along_axis(traces, target, axis=3, mode='fill', fill_value=0.0))
    pieces = [shift_devices(sent[side_id], offset) for offset, side_id in ((DEV_Y, 1), (-DEV_Y, 0), (1, 3), (-1, 2))]
    return jnp.concatenate(pieces, axis=3)

def tendency_reference(states, medium, medium_faces, send_list, neighbours):
    slot_count = states.shape[3]
    derivs = derivative_parts(states)
    volume, rate_parts = volume_terms(derivs, medium)
    traces = face_traces(states)
    sources = jnp.concatenate([traces, ghost_reference(traces, send_list, slot_count)], axis=3)
    free_code = sources.shape[3]
    target = jnp.broadcast_to(neighbours[:, None, None, :], traces.shape)
    exterior = jnp.take_along_axis(sources, target, axis=3, mode='fill', fill_value=0.0)
    free_mask = (neighbours == free_code).astype(jnp.float32)[:, None, None, :]
    jump_all = exterior - traces
    jump_all = jnp.concatenate([jump_all[:, :3] * (1.0 - free_mask), jump_all[:, 3:] * (1.0 + free_mask)], axis=1)
    return (surface_terms(volume, jump_all, medium_faces, slot_count), rate_parts)

def reference(forward, adjoint, material, counts, send_list, neighbours):
    slot_count = OCT_DEV
    devices = N_DOM
    live_mask = (jnp.arange(slot_count, dtype=jnp.int32)[None, :] < counts[:, None]).astype(jnp.float32)
    medium = jnp.transpose(material.reshape(3, 125, devices, slot_count), (2, 0, 1, 3))
    medium_faces = face_traces(medium)

    def per_device(values):
        shaped = jnp.transpose(values.reshape(9, 125, devices, slot_count), (2, 0, 1, 3))
        return shaped * live_mask[:, None, None, :]

    def restore(values):
        return jnp.transpose(values, (1, 2, 0, 3)).reshape(values.shape[1], 125, devices * slot_count)

    def advance(states):
        return tendency_reference(states, medium, medium_faces, send_list, neighbours)

    def one_shot(pair):
        states = per_device(pair[0])
        duals = per_device(pair[1])
        forward_rate, forward_parts = advance(states)
        adjoint_rate, unused_parts = advance(duals)
        forward_mid = states + step_size * forward_rate
        adjoint_mid = duals + step_size * adjoint_rate
        forward_rate2, forward_parts2 = advance(forward_mid)
        adjoint_rate2, unused_parts2 = advance(adjoint_mid)
        forward_end = 0.5 * states + 0.5 * (forward_mid + step_size * forward_rate2)
        adjoint_end = 0.5 * duals + 0.5 * (adjoint_mid + step_size * adjoint_rate2)
        partial_value = material_partials(forward_parts, duals) + material_partials(forward_parts2, adjoint_mid)
        return (restore(forward_end), restore(adjoint_end), partial_value)
    forward_next, adjoint_next, partials = lax.map(one_shot, (forward, adjoint))
    gradient = 0.5 * step_size * lax.optimization_barrier(jnp.sum(partials, axis=0))
    gradient = jnp.transpose(gradient, (1, 2, 0, 3)).reshape(3, 125, devices * slot_count)
    return (forward_next, adjoint_next, gradient)
```

```python
import functools

import jax
import jax.numpy as jnp
import numpy as np
from jax import lax
from jax.experimental import pallas as pl
from jax.experimental.pallas import tpu as pltpu
from jax.sharding import PartitionSpec as P

DEV_Y = 4
ORDER = 5
NODES = ORDER**3
FACE = ORDER * ORDER
FIELDS = 9
LANES = 128
SUBS = 8
step_size = 0.01
lift_weight = 10.0
VMEM_BYTES = 16 * 1024 * 1024

FACE_OFF = (0, 100, 0, 20, 0, 4)
FACE_U = (5, 5, 25, 25, 25, 25)
FACE_V = (1, 1, 1, 1, 5, 5)


def derivative_matrix():
    points = np.array([-1.0, -np.sqrt(3.0 / 7.0), 0.0, np.sqrt(3.0 / 7.0), 1.0])
    barycentric = np.array(
        [1.0 / np.prod([points[a] - points[b] for b in range(5) if b != a]) for a in range(5)]
    )
    matrix = np.zeros((5, 5))
    for a in range(5):
        for b in range(5):
            if a != b:
                matrix[a, b] = barycentric[b] / barycentric[a] / (points[a] - points[b])
        matrix[a, a] = -np.sum(matrix[a])
    return matrix


MAT = derivative_matrix()


def derivative(u):
    e0, e1 = u[0] + u[4], u[1] + u[3]
    o0, o1 = u[0] - u[4], u[1] - u[3]
    mid = u[2] + u[2]
    e0, e1 = e0 - mid, e1 - mid
    out = [None] * 5
    for a in range(2):
        even = float(0.5 * (MAT[a, 0] + MAT[a, 4])) * e0 + float(0.5 * (MAT[a, 1] + MAT[a, 3])) * e1
        odd = float(0.5 * (MAT[a, 0] - MAT[a, 4])) * o0 + float(0.5 * (MAT[a, 1] - MAT[a, 3])) * o1
        out[a] = odd + even
        out[4 - a] = odd - even
    out[2] = float(MAT[2, 0]) * o0 + float(MAT[2, 1]) * o1
    return out


def sub_iota():
    return lax.broadcasted_iota(jnp.int32, (SUBS, LANES), 0)


def half_of():
    return sub_iota() >> 2


def live_tile(counts_ref):
    lane = lax.broadcasted_iota(jnp.int32, (SUBS, LANES), 1)
    return half_of() * LANES + lane < counts_ref[0]


def swap_halves(x):
    return pltpu.roll(x, SUBS // 2, axis=0)


def lane_pick(x, idx):
    return jnp.take_along_axis(x, idx, axis=1, mode="promise_in_bounds")


def code_tile(codes_ref, face, slots):
    base = face * slots
    rows = []
    for h in range(2):
        at = base + h * LANES
        at = at if isinstance(at, int) else pl.multiple_of(at, LANES)
        rows.append(jnp.broadcast_to(codes_ref[0:1, pl.ds(at, LANES)], (SUBS, LANES)))
    first, second = rows
    return jnp.where(half_of() == 0, first, second)


def side_offset(axis, up):
    return up * FACE_OFF[2 * axis + 1]


def pack_side(state, list_ref, out, axis, up, slots):
    half = half_of()
    low = half == 0
    lane_group = lax.broadcasted_iota(jnp.int32, (SUBS, LANES), 1) >> 5
    masks = [lane_group == q for q in range(1, 4)]
    side = 2 * axis
    row = jnp.where(up > 0, list_ref[0, side + 1 : side + 2, :], list_ref[0, side : side + 1, :])
    listed = jnp.broadcast_to(jnp.concatenate([row] * 4, axis=1), (SUBS, LANES))
    idx = listed & (LANES - 1)
    here = (listed < slots) & ((listed >> 7) == half)
    start = side_offset(axis, up)

    def combine(parts):
        picked = [lane_pick(part, idx) for part in parts]
        groups = []
        for x in range(2):
            four = picked[4 * x : 4 * x + 4]
            tile = four[0]
            for q in range(1, len(four)):
                tile = jnp.where(masks[q - 1], four[q], tile)
            tile = jnp.where(here, tile, 0.0)
            groups.append(tile + swap_halves(tile))
        return jnp.where(low, groups[0], groups[1])

    for p in range(FACE):
        node = start + FACE_U[side] * (p // ORDER) + FACE_V[side] * (p % ORDER)
        out[p] = combine([state[k * NODES + node] for k in range(8)])
    for g in range(4):
        parts = []
        for w in range(8):
            p = min(8 * g + w, FACE - 1)
            node = start + FACE_U[side] * (p // ORDER) + FACE_V[side] * (p % ORDER)
            parts.append(state[8 * NODES + node])
        out[FACE + g] = combine(parts)


def add_rows(acc, node, jumps, coef, direction, sign):
    lam, mu, buoy, speed = coef
    a, b, c = direction, (direction + 1) % 3, (direction + 2) % 3
    s_aa, s_bb, s_cc = 3 + a, 3 + b, 3 + c
    s_ab, s_ac, s_bc = 6 + c, 6 + b, 6 + a
    across = lam * jumps[a]
    flux = {
        a: buoy * jumps[s_aa],
        b: buoy * jumps[s_ab],
        c: buoy * jumps[s_ac],
        s_aa: across + (mu + mu) * jumps[a],
        s_bb: across,
        s_cc: across,
        s_ab: mu * jumps[b],
        s_ac: mu * jumps[c],
    }
    for k in range(FIELDS):
        row = k * NODES + node
        total = speed * jumps[k]
        if k in flux:
            total = total + flux[k] if sign > 0 else total - flux[k]
        acc[row] = acc[row] + total


def coefs(med, node):
    return [med[m * NODES + node] for m in range(4)]


def volume_pass(state, acc, med, products, average, scaled):
    def x_lines(j, carry):
        for k in range(5):
            for field, row in ((0, 3), (1, 8), (2, 7), (3, 0), (8, 1), (7, 2)):
                out = derivative([state[field * NODES + 25 * i + 5 * j + k] for i in range(5)])
                for i in range(5):
                    acc[row * NODES + 25 * i + 5 * j + k] = out[i]
        return carry

    lax.fori_loop(0, ORDER, x_lines, 0)

    def y_lines(i, carry):
        for k in range(5):
            for field, row, more in ((0, 8, 1), (1, 4, 0), (2, 6, 0), (8, 0, 1), (4, 1, 1), (6, 2, 1)):
                out = derivative([state[field * NODES + 25 * i + 5 * j + k] for j in range(5)])
                for j in range(5):
                    at = row * NODES + 25 * i + 5 * j + k
                    acc[at] = acc[at] + out[j] if more else out[j]
        return carry

    lax.fori_loop(0, ORDER, y_lines, 0)

    def z_line(first):
        parts = {}
        for field in (0, 1, 2, 7, 6, 5):
            parts[field] = derivative([state[field * NODES + first + k] for k in range(5)])
        for k in range(5):
            node = first + k
            lam, mu, buoy = (scaled(value) for value in coefs(med, node)[:3])
            old = [acc[row * NODES + node] for row in range(FIELDS) if row != 5]
            sdiv = [old[0] + parts[7][k], old[1] + parts[6][k], old[2] + parts[5][k]]
            g11, g22, g33 = old[3], old[4], parts[2][k]
            r23 = old[5] + parts[1][k]
            r13 = old[6] + parts[0][k]
            r12 = old[7]
            div = g11 + g22 + g33
            spread = lam * div
            mu2 = mu + mu
            volume = [buoy * s for s in sdiv]
            volume += [spread + mu2 * g for g in (g11, g22, g33)]
            volume += [mu * r for r in (r23, r13, r12)]
            own = [state[row * NODES + node] for row in range(FIELDS)]
            for row in range(FIELDS):
                acc[row * NODES + node] = average(own[row], row * NODES + node) + volume[row]
            dual = [pltpu.roll(x, SUBS - 2, axis=0) for x in own]
            pressure = div * (dual[3] + dual[4] + dual[5])
            normal = g11 * dual[3] + g22 * dual[4] + g33 * dual[5]
            shear = normal + normal + (r23 * dual[6] + r13 * dual[7] + r12 * dual[8])
            light = sdiv[0] * dual[0] + sdiv[1] * dual[1] + sdiv[2] * dual[2]
            for m, value in enumerate((pressure, shear, light)):
                products[pl.ds((m * LANES + node) * SUBS, SUBS), :] = value

    def z_lines(i, carry):
        for j in range(5):
            z_line(25 * i + 5 * j)
        return carry

    lax.fori_loop(0, ORDER, z_lines, 0)


def shot_sums(products, emit):
    for m in range(3):
        for g in range((NODES + 7) // 8):
            rows = min(8, NODES - 8 * g)
            base = (m * LANES + 8 * g) * SUBS
            for h in range(2):
                first = products[pl.ds(base + 4 * h, 8, stride=SUBS), :]
                second = products[pl.ds(base + 4 * h + 1, 8, stride=SUBS), :]
                emit(m, 8 * g, rows, h, (first + second)[:rows])


def local_pass(state, acc, med, codes_ref, slots, weight):
    half = half_of()
    low = half == 0
    free_code = 6 * slots + 4 * 32
    for face in range(6):
        codes = code_tile(codes_ref, face, slots)
        idx = codes & (LANES - 1)
        match = (codes >> 8) == (face ^ 1)
        same = match & (((codes >> 7) & 1) == half)
        cross = match & (((codes >> 7) & 1) != half)
        free = codes == free_code
        factor_v = jnp.where(free, 0.0, weight)
        factor_s = jnp.where(free, 2.0 * weight, weight)
        other = face ^ 1

        def body(u, carry, face=face, other=other, idx=idx, same=same, cross=cross,
                 factor_v=factor_v, factor_s=factor_s):
            for v in range(ORDER):
                shift = FACE_U[face] * u + FACE_V[face] * v
                node = FACE_OFF[face] + shift
                source = FACE_OFF[other] + shift
                jumps = []
                for k in range(FIELDS):
                    there = state[k * NODES + source]
                    outer = jnp.where(same, lane_pick(there, idx), 0.0)
                    outer = jnp.where(cross, lane_pick(swap_halves(there), idx), outer)
                    jump = outer - state[k * NODES + node]
                    jumps.append(jump * (factor_v if k < 3 else factor_s))
                add_rows(acc, node, jumps, coefs(med, node), face // 2, 2 * (face % 2) - 1)
            return carry

        lax.fori_loop(0, ORDER, body, 0, unroll=True)


def ghost_tiles(ghost, p, low):
    tile = ghost[p]
    turned = swap_halves(tile)
    tile9 = ghost[FACE + (p >> 3)]
    turned9 = swap_halves(tile9)
    chosen = half_of() == ((p >> 2) & 1)
    return jnp.where(low, tile, turned), jnp.where(low, turned, tile), jnp.where(chosen, tile9, turned9)


def ghost_pass(acc, med, codes_ref, ghost, axis, up, slots, scale):
    low = half_of() == 0
    face = 2 * axis + up
    sign = (2 * up - 1).astype(jnp.float32)
    codes = code_tile(codes_ref, face, slots) - (6 * slots + 32 * face)
    inside = (codes >= 0) & (codes < 32)
    weight = jnp.where(inside, scale, 0.0)
    idx = codes & 31
    shifted = [idx + 32 * q for q in range(4)]
    start = side_offset(axis, up)

    def body(u, carry):
        for v in range(ORDER):
            p = ORDER * u + v
            node = start + FACE_U[2 * axis] * u + FACE_V[2 * axis] * v
            first, second, nine = ghost_tiles(ghost, p, low)
            jumps = []
            for k in range(8):
                jumps.append(lane_pick(first if k < 4 else second, shifted[k % 4]) * weight)
            jumps.append(lane_pick(nine, idx + 32 * (p & 3)) * weight)
            lam, mu, buoy, speed = coefs(med, node)
            add_rows(acc, node, jumps, (sign * lam, sign * mu, sign * buoy, speed), axis, 1)
        return carry

    lax.fori_loop(0, ORDER, body, 0, unroll=True)


def other_sources(state, acc, med, codes_ref, ghosts, ups, axes, outer, slots, scale):
    half = half_of()
    low = half == 0
    first_ghost = 6 * slots

    def codes_of(face):
        return code_tile(codes_ref, face, slots)

    left = jnp.zeros((SUBS, LANES), jnp.int32)
    for face in range(6):
        codes = codes_of(face)
        source = jnp.where(codes < first_ghost, codes >> 8, 6 + ((codes - first_ghost) >> 5))
        usual = (source == (face ^ 1)) | (source >= 10)
        if face < 4:
            usual = usual | (source == 6 + face)
        left = left | jnp.where(usual, 0, 1)
    remaining = jnp.max(left)

    @pl.when(remaining > 0)
    def _():
        def pair(t, carry):
            face, origin = t // 10, t % 10
            codes = code_tile(codes_ref, face, slots)
            source = jnp.where(codes < first_ghost, codes >> 8, 6 + ((codes - first_ghost) >> 5))
            mine = source == origin
            done = (origin == (face ^ 1)) | ((face < 4) & (origin == 6 + face))
            count = jnp.max(jnp.where(mine, 1, 0))

            @pl.when((count > 0) & jnp.logical_not(done))
            def _():
                weight = jnp.where(mine, scale, 0.0)
                axis, sign = face >> 1, (2 * (face & 1) - 1).astype(jnp.float32)

                def strides(which):
                    line = which >> 1
                    off = (which & 1) * jnp.where(line == 0, 100, jnp.where(line == 1, 20, 4))
                    return off, jnp.where(line == 0, 5, 25), jnp.where(line == 2, 5, 1)

                off, du, dv = strides(face)
                off2, du2, dv2 = strides(jnp.minimum(origin, 5))

                def at_node(p, carry):
                    u, v = p // ORDER, p % ORDER
                    node = off + du * u + dv * v

                    @pl.when(origin < 6)
                    def _():
                        there_node = off2 + du2 * u + dv2 * v
                        idx = codes & (LANES - 1)
                        same = ((codes >> 7) & 1) == half
                        for k in range(FIELDS):
                            there = state[k * NODES + there_node]
                            turned = swap_halves(there)
                            outer[k] = jnp.where(same, lane_pick(there, idx), lane_pick(turned, idx)) * weight

                    @pl.when(origin >= 6)
                    def _():
                        for k in range(FIELDS):
                            outer[k] = jnp.zeros((SUBS, LANES), jnp.float32)

                    for ghost, up, line in zip(ghosts, ups, axes):

                        @pl.when(origin == 6 + 2 * line + up)
                        def _(ghost=ghost):
                            idx = (codes - first_ghost) & 31
                            first, second, nine = ghost_tiles(ghost, p, low)
                            for k in range(8):
                                tile = first if k < 4 else second
                                outer[k] = lane_pick(tile, idx + 32 * (k % 4)) * weight
                            outer[8] = lane_pick(nine, idx + 32 * (p & 3)) * weight

                    lam, mu, buoy, speed = coefs(med, node)
                    a = axis
                    b, c = lax.rem(axis + 1, 3), lax.rem(axis + 2, 3)
                    across = lam * outer[a]
                    flux = (
                        (a, buoy * outer[3 + a]),
                        (b, buoy * outer[6 + c]),
                        (c, buoy * outer[6 + b]),
                        (3 + a, across + (mu + mu) * outer[a]),
                        (3 + b, across),
                        (3 + c, across),
                        (6 + c, mu * outer[b]),
                        (6 + b, mu * outer[c]),
                        (6 + a, None),
                    )
                    for k, value in flux:
                        row = k * NODES + node
                        total = speed * outer[k]
                        if value is not None:
                            total = total + sign * value
                        acc[row] = acc[row] + total
                    return carry

                lax.fori_loop(0, FACE, at_node, 0)

            return carry

        lax.fori_loop(0, 60, pair, 0)


def link_ups(place_ref, links):
    return [1 - ((lax.div(place_ref[0], stride) + parity) & 1) for _, stride, parity in links]


def load_kernel(slots, links, mat_hbm, fwd_hbm, adj_hbm, state_ref, med_ref, mat_ref, sems, mat_sem):
    mat_copy = pltpu.make_async_copy(mat_hbm, mat_ref, mat_sem)
    mat_copy.start()
    copies = []
    for k in range(FIELDS):
        span = pl.ds(k * NODES, NODES)
        for n, far in enumerate((fwd_hbm, adj_hbm)):
            copies.append(pltpu.make_async_copy(far.at[span], state_ref.at[span, :, n], sems.at[n, k]))
            copies[-1].start()
    mat_copy.wait()
    spread_material(mat_ref, med_ref)
    for copy in copies:
        copy.wait()


def pack_kernel(slots, links, place_ref, state_ref, list_ref, *sends):
    ups = link_ups(place_ref, links)
    for n, link in enumerate(links):
        pack_side(state_ref, list_ref, sends[n], link[0], ups[n], slots)


def spread_material(mat_ref, med_ref):
    low = half_of() == 0
    for node in range(NODES):
        rows = []
        for m in range(3):
            first = jnp.broadcast_to(mat_ref[m, node : node + 1, 0:LANES], (SUBS, LANES))
            second = jnp.broadcast_to(mat_ref[m, node : node + 1, LANES : 2 * LANES], (SUBS, LANES))
            rows.append(jnp.where(low, first, second))
        lam, mu, buoy = rows
        speed = jnp.sqrt((lam + 2.0 * mu) * buoy)
        for m, value in enumerate((lam, mu, buoy, speed)):
            med_ref[m * NODES + node] = step_size * value


def first_kernel(slots, links, counts_ref, state_ref, med_ref, codes_ref, acc_ref, grad_ref, products):
    volume_pass(state_ref, acc_ref, med_ref, products, lambda own, row: own, lambda value: value)
    shot_sums(products, store_gradient(counts_ref, grad_ref, None))
    local_pass(state_ref, acc_ref, med_ref, codes_ref, slots, 0.5 * lift_weight)


def store_gradient(counts_ref, grad_ref, earlier_ref):
    lane = lax.broadcasted_iota(jnp.int32, (SUBS, LANES), 1)

    def emit(m, start, rows, h, value):
        at = (m, slice(start, start + rows), slice(h * LANES, (h + 1) * LANES))
        if earlier_ref is not None:
            value = (0.5 * step_size) * (earlier_ref[at] + value)
        grad_ref[at] = jnp.where((h * LANES + lane < counts_ref[0])[:rows], value, 0.0)

    return emit


def ghost_stage(slots, links, ups, state_ref, acc_ref, med_ref, codes_ref, ghosts, outer, scale):
    axes = [link[0] for link in links]
    for axis, up, ghost in zip(axes, ups, ghosts):
        ghost_pass(acc_ref, med_ref, codes_ref, ghost, axis, up, slots, scale)
    other_sources(state_ref, acc_ref, med_ref, codes_ref, ghosts, ups, axes, outer, slots, scale)


def middle_kernel(slots, links, place_ref, acc_in, state_ref, med_ref, codes_ref, list_ref, *rest):
    count = len(links)
    ghosts, mid_ref, sends, outer = rest[:count], rest[count], rest[count + 1 : 2 * count + 1], rest[-1]
    ups = link_ups(place_ref, links)
    ghost_stage(slots, links, ups, state_ref, mid_ref, med_ref, codes_ref, ghosts, outer, 0.5 * lift_weight)
    for n, link in enumerate(links):
        pack_side(mid_ref, list_ref, sends[n], link[0], ups[n], slots)


def second_volume_kernel(slots, links, counts_ref, mid_ref, state_ref, med_ref, first_ref, acc_ref, grad_ref, products):
    share = jnp.where(live_tile(counts_ref), 0.5, 0.0)
    volume_pass(
        mid_ref, acc_ref, med_ref, products,
        lambda own, row: share * (own + state_ref[row]), lambda value: share * value,
    )
    shot_sums(products, store_gradient(counts_ref, grad_ref, first_ref))


def second_faces_kernel(slots, links, counts_ref, acc_in, mid_ref, med_ref, codes_ref, acc_ref):
    weight = jnp.where(live_tile(counts_ref), 0.25 * lift_weight, 0.0)
    local_pass(mid_ref, acc_ref, med_ref, codes_ref, slots, weight)


def second_ghosts_kernel(chosen, slots, links, place_ref, acc_in, med_ref, codes_ref, *rest):
    ghosts, acc_ref = rest[: len(chosen)], rest[-1]
    ups = link_ups(place_ref, links)
    for n, ghost in zip(chosen, ghosts):
        ghost_pass(acc_ref, med_ref, codes_ref, ghost, links[n][0], ups[n], slots, 0.25 * lift_weight)


def other_sources_kernel(slots, links, place_ref, acc_in, mid_ref, med_ref, codes_ref, *rest):
    ghosts, (acc_ref, outer) = rest[: len(links)], rest[len(links) :]
    ups = link_ups(place_ref, links)
    axes = [link[0] for link in links]
    other_sources(mid_ref, acc_ref, med_ref, codes_ref, ghosts, ups, axes, outer, slots, 0.25 * lift_weight)


def split_kernel(slots, links, grad_ref, *rest):
    first_ref, second_ref = rest[len(links) :]
    cut = first_ref.shape[1]
    first_ref[...] = grad_ref[:, :cut]
    second_ref[...] = grad_ref[:, cut:]


def partial_kernel(slots, links, acc_in, a_ref, b_ref, near_ref, far_ref, acc_ref, first_ref, second_ref):
    first_ref[...] = a_ref[...] + near_ref[...]
    second_ref[...] = b_ref[...] + far_ref[...]


def total_kernel(slots, links, a_ref, b_ref, c_ref, d_ref, grad_ref):
    cut = a_ref.shape[1]
    grad_ref[:, :cut] = a_ref[...] + c_ref[...]
    grad_ref[:, cut:] = b_ref[...] + d_ref[...]


def store_kernel(slots, links, acc_ref, fwd_hbm, adj_hbm, sems):
    copies = []
    for k in range(FIELDS):
        span = pl.ds(k * NODES, NODES)
        for n, far in enumerate((fwd_hbm, adj_hbm)):
            copies.append(pltpu.make_async_copy(acc_ref.at[span, :, n], far.at[span], sems.at[n, k]))
            copies[-1].start()
    for copy in copies:
        copy.wait()


def tree_links(devices):
    links = []
    for axis, stride in ((0, DEV_Y), (1, 1)):
        for parity in range(2):
            pairs = [(d, d + stride) for d in range(devices - stride) if (d // stride) % 2 == parity]
            if pairs:
                links.append((axis, stride, parity, pairs + [(b, a) for a, b in pairs]))
    return links


def swapped(block, axis, distance):
    route = [(i, i ^ distance) for i in range(lax.axis_size(axis))]
    return lax.ppermute(block, axis, route)


def shards(forward, adjoint, material, counts, send_list, neighbours):
    shots, fields, nodes, slots = forward.shape
    halves = slots // LANES
    rows = fields * nodes
    assert 2 * shots * halves == SUBS and nodes == NODES and fields == FIELDS

    def dense(values):
        cut = values.reshape(shots, fields, nodes, halves, LANES)
        tiles = cut.transpose(1, 2, 3, 0, 4).reshape(rows, halves, shots, LANES)
        return pltpu.with_memory_space_constraint(tiles, pltpu.HBM)

    def restored(values):
        cut = values.reshape(fields, nodes, halves, shots, LANES)
        return cut.transpose(3, 0, 1, 2, 4).reshape(shots, fields, nodes, slots)

    links = tree_links(lax.axis_size("dom"))
    axes = tuple(link[:3] for link in links)
    place = lax.axis_index("dom").astype(jnp.int32).reshape(1)

    def exchange(sends):
        return [lax.ppermute(send, "dom", link[3]) for send, link in zip(sends, links)]

    vmem = pl.BlockSpec(memory_space=pltpu.VMEM)
    smem = pl.BlockSpec(memory_space=pltpu.SMEM)
    hbm = pl.BlockSpec(memory_space=pltpu.HBM)
    f32 = jnp.float32
    state_shape = pltpu.VMEM((rows, SUBS, LANES), f32)
    send_shape = pltpu.VMEM((FACE + 4, SUBS, LANES), f32)
    med_shape = pltpu.VMEM((4 * nodes, SUBS, LANES), f32)
    grad_shape = pltpu.VMEM(material.shape, f32)
    apart = (rows, halves, 2, shots, LANES)
    part_shape = jax.ShapeDtypeStruct((rows, halves, shots, LANES), f32)
    products = pltpu.VMEM((3 * LANES * SUBS, LANES), f32)
    outer = pltpu.VMEM((FIELDS, SUBS, LANES), f32)
    field_sems = pltpu.SemaphoreType.DMA((2, FIELDS))

    def call(kernel, out_shape, in_specs, name, micros, scratch=(), out_specs=None, aliases=None):
        return pl.pallas_call(
            functools.partial(kernel, slots, axes),
            out_shape=out_shape,
            in_specs=in_specs,
            out_specs=out_specs or [vmem] * len(out_shape),
            scratch_shapes=list(scratch),
            input_output_aliases=aliases or {},
            compiler_params=pltpu.CompilerParams(vmem_limit_bytes=VMEM_BYTES),
            cost_estimate=pl.CostEstimate(flops=0, bytes_accessed=micros * 3000000, transcendentals=0),
            name=name,
        )

    count = len(links)
    state, med = call(
        load_kernel, [pltpu.VMEM(apart, f32), med_shape], [hbm] * 3, "load", 4,
        [pltpu.VMEM(material.shape, f32), field_sems, pltpu.SemaphoreType.DMA],
    )(pltpu.with_memory_space_constraint(material, pltpu.HBM), dense(forward), dense(adjoint))
    state = state.reshape(rows, SUBS, LANES)
    sends = call(pack_kernel, [send_shape] * count, [smem, vmem, vmem], "pack", 2)(place, state, send_list)
    ghosts = exchange(sends)
    acc, grad_first = call(
        first_kernel, [state_shape, grad_shape], [smem] + [vmem] * 3, "first_section", 8, [products]
    )(counts, state, med, neighbours)
    mid, *sends = call(
        middle_kernel, [state_shape] + [send_shape] * count, [smem] + [vmem] * (5 + count), "first_ghosts", 4,
        [outer], aliases={1: 0},
    )(place, acc, state, med, neighbours, send_list, *ghosts)
    ghosts = exchange(sends)
    acc, grad = call(
        second_volume_kernel, [state_shape, grad_shape], [smem] + [vmem] * 4, "second_volume", 4, [products]
    )(counts, mid, state, med, grad_first)
    shot_devices = lax.axis_size("shot")
    doubling = shot_devices == 4
    if doubling:
        cut = (nodes // 2 + SUBS // 2) // SUBS * SUBS
        part_shapes = [pltpu.VMEM((3, size, slots), f32) for size in (cut, nodes - cut)]
        halved = call(split_kernel, part_shapes, [vmem] * (1 + count), "gradient_split", 0)(grad, *ghosts)
        pieces = [swapped(halved[0], "shot", 1), swapped(halved[1], "shot", 2)]
    (acc,) = call(
        second_faces_kernel, [state_shape], [smem] + [vmem] * 4, "second_faces", 4, aliases={1: 0}
    )(counts, acc, mid, med, neighbours)

    def add_ghosts(acc, chosen):
        (acc,) = call(
            functools.partial(second_ghosts_kernel, chosen), [state_shape], [smem] + [vmem] * (3 + len(chosen)),
            "second_ghosts", 2, aliases={1: 0},
        )(place, acc, med, neighbours, *[ghosts[n] for n in chosen])
        return acc

    acc = add_ghosts(acc, range(1))
    if doubling:
        acc, *parts = call(
            partial_kernel, [state_shape] + part_shapes, [vmem] * 5, "gradient_partial", 0, aliases={0: 0}
        )(acc, *halved, *pieces)
        pieces = [swapped(parts[0], "shot", 2), swapped(parts[1], "shot", 1)]
    else:
        gradient = lax.psum(grad, "shot")
    acc = add_ghosts(acc, range(1, count))
    (acc,) = call(
        other_sources_kernel, [state_shape], [smem] + [vmem] * (4 + count), "other_sources", 0, [outer], aliases={1: 0}
    )(place, acc, mid, med, neighbours, *ghosts)
    fwd, adj = call(store_kernel, [part_shape, part_shape], [vmem], "store", 4, [field_sems], [hbm, hbm])(
        acc.reshape(apart)
    )
    if doubling:
        (gradient,) = call(
            total_kernel, [jax.ShapeDtypeStruct(material.shape, f32)], [vmem] * 4, "gradient_total", 0
        )(*parts, *pieces)
    return restored(fwd), restored(adj), gradient


def solution(mesh):
    placed = (
        P("shot", None, None, "dom"),
        P("shot", None, None, "dom"),
        P(None, None, "dom"),
        P("dom"),
        P("dom", None, None),
        P("dom", None),
    )
    return jax.shard_map(
        shards,
        mesh=mesh,
        in_specs=placed,
        out_specs=(
            P("shot", None, None, "dom"),
            P("shot", None, None, "dom"),
            P(None, None, "dom"),
        ),
        check_vma=False,
    )
```

```python
import functools

import jax
import jax.numpy as jnp
import numpy as np
from jax import lax
from jax.experimental import pallas as pl
from jax.experimental.pallas import tpu as pltpu
from jax.sharding import PartitionSpec as P

DEV_Y = 4
ORDER = 5
NODES = ORDER**3
FACE = ORDER * ORDER
FIELDS = 9
LANES = 128
SUBS = 8
step_size = 0.01
lift_weight = 10.0
VMEM_BYTES = 16 * 1024 * 1024

FACE_OFF = (0, 100, 0, 20, 0, 4)
FACE_U = (5, 5, 25, 25, 25, 25)
FACE_V = (1, 1, 1, 1, 5, 5)


def derivative_matrix():
    points = np.array([-1.0, -np.sqrt(3.0 / 7.0), 0.0, np.sqrt(3.0 / 7.0), 1.0])
    barycentric = np.array(
        [1.0 / np.prod([points[a] - points[b] for b in range(5) if b != a]) for a in range(5)]
    )
    matrix = np.zeros((5, 5))
    for a in range(5):
        for b in range(5):
            if a != b:
                matrix[a, b] = barycentric[b] / barycentric[a] / (points[a] - points[b])
        matrix[a, a] = -np.sum(matrix[a])
    return matrix


MAT = derivative_matrix()


def derivative(u):
    e0, e1 = u[0] + u[4], u[1] + u[3]
    o0, o1 = u[0] - u[4], u[1] - u[3]
    mid = u[2] + u[2]
    e0, e1 = e0 - mid, e1 - mid
    out = [None] * 5
    for a in range(2):
        even = float(0.5 * (MAT[a, 0] + MAT[a, 4])) * e0 + float(0.5 * (MAT[a, 1] + MAT[a, 3])) * e1
        odd = float(0.5 * (MAT[a, 0] - MAT[a, 4])) * o0 + float(0.5 * (MAT[a, 1] - MAT[a, 3])) * o1
        out[a] = odd + even
        out[4 - a] = odd - even
    out[2] = float(MAT[2, 0]) * o0 + float(MAT[2, 1]) * o1
    return out


def sub_iota():
    return lax.broadcasted_iota(jnp.int32, (SUBS, LANES), 0)


def half_of():
    return sub_iota() >> 2


def live_tile(counts_ref):
    lane = lax.broadcasted_iota(jnp.int32, (SUBS, LANES), 1)
    return half_of() * LANES + lane < jnp.broadcast_to(counts_ref[...], (SUBS, LANES))


def swap_halves(x):
    return pltpu.roll(x, SUBS // 2, axis=0)


def lane_pick(x, idx):
    return jnp.take_along_axis(x, idx, axis=1, mode="promise_in_bounds")


def code_tile(codes_ref, face, slots):
    base = face * slots
    rows = []
    for h in range(2):
        at = base + h * LANES
        at = at if isinstance(at, int) else pl.multiple_of(at, LANES)
        rows.append(jnp.broadcast_to(codes_ref[0:1, pl.ds(at, LANES)], (SUBS, LANES)))
    first, second = rows
    return jnp.where(half_of() == 0, first, second)


def side_offset(axis, up):
    return up * FACE_OFF[2 * axis + 1]


def pack_side(state, list_ref, out, axis, up, slots):
    half = half_of()
    low = half == 0
    lane_group = lax.broadcasted_iota(jnp.int32, (SUBS, LANES), 1) >> 5
    masks = [lane_group == q for q in range(1, 4)]
    side = 2 * axis
    row = jnp.where(up > 0, list_ref[0, side + 1 : side + 2, :], list_ref[0, side : side + 1, :])
    listed = jnp.broadcast_to(jnp.concatenate([row] * 4, axis=1), (SUBS, LANES))
    idx = listed & (LANES - 1)
    here = (listed < slots) & ((listed >> 7) == half)
    start = side_offset(axis, up)

    def combine(parts):
        picked = [lane_pick(part, idx) for part in parts]
        groups = []
        for x in range(2):
            four = picked[4 * x : 4 * x + 4]
            tile = four[0]
            for q in range(1, len(four)):
                tile = jnp.where(masks[q - 1], four[q], tile)
            tile = jnp.where(here, tile, 0.0)
            groups.append(tile + swap_halves(tile))
        return jnp.where(low, groups[0], groups[1])

    for p in range(FACE):
        node = start + FACE_U[side] * (p // ORDER) + FACE_V[side] * (p % ORDER)
        out[p] = combine([state[k * NODES + node] for k in range(8)])
    for g in range(4):
        parts = []
        for w in range(8):
            p = min(8 * g + w, FACE - 1)
            node = start + FACE_U[side] * (p // ORDER) + FACE_V[side] * (p % ORDER)
            parts.append(state[8 * NODES + node])
        out[FACE + g] = combine(parts)


def add_rows(acc, node, jumps, coef, direction, sign):
    lam, mu, buoy, speed = coef
    a, b, c = direction, (direction + 1) % 3, (direction + 2) % 3
    s_aa, s_bb, s_cc = 3 + a, 3 + b, 3 + c
    s_ab, s_ac, s_bc = 6 + c, 6 + b, 6 + a
    across = lam * jumps[a]
    flux = {
        a: buoy * jumps[s_aa],
        b: buoy * jumps[s_ab],
        c: buoy * jumps[s_ac],
        s_aa: across + (mu + mu) * jumps[a],
        s_bb: across,
        s_cc: across,
        s_ab: mu * jumps[b],
        s_ac: mu * jumps[c],
    }
    for k in range(FIELDS):
        row = k * NODES + node
        total = speed * jumps[k]
        if k in flux:
            total = total + flux[k] if sign > 0 else total - flux[k]
        acc[row] = acc[row] + total


def coefs(med, node):
    return [med[m * NODES + node] for m in range(4)]


def volume_pass(state, acc, med, products, average, scaled):
    def x_lines(j, carry):
        for k in range(5):
            for field, row in ((0, 3), (1, 8), (2, 7), (3, 0), (8, 1), (7, 2)):
                out = derivative([state[field * NODES + 25 * i + 5 * j + k] for i in range(5)])
                for i in range(5):
                    acc[row * NODES + 25 * i + 5 * j + k] = out[i]
        return carry

    lax.fori_loop(0, ORDER, x_lines, 0)

    def y_lines(i, carry):
        for k in range(5):
            for field, row, more in ((0, 8, 1), (1, 4, 0), (2, 6, 0), (8, 0, 1), (4, 1, 1), (6, 2, 1)):
                out = derivative([state[field * NODES + 25 * i + 5 * j + k] for j in range(5)])
                for j in range(5):
                    at = row * NODES + 25 * i + 5 * j + k
                    acc[at] = acc[at] + out[j] if more else out[j]
        return carry

    lax.fori_loop(0, ORDER, y_lines, 0)

    def z_line(first):
        parts = {}
        for field in (0, 1, 2, 7, 6, 5):
            parts[field] = derivative([state[field * NODES + first + k] for k in range(5)])
        for k in range(5):
            node = first + k
            lam, mu, buoy = (scaled(value) for value in coefs(med, node)[:3])
            old = [acc[row * NODES + node] for row in range(FIELDS) if row != 5]
            sdiv = [old[0] + parts[7][k], old[1] + parts[6][k], old[2] + parts[5][k]]
            g11, g22, g33 = old[3], old[4], parts[2][k]
            r23 = old[5] + parts[1][k]
            r13 = old[6] + parts[0][k]
            r12 = old[7]
            div = g11 + g22 + g33
            spread = lam * div
            mu2 = mu + mu
            volume = [buoy * s for s in sdiv]
            volume += [spread + mu2 * g for g in (g11, g22, g33)]
            volume += [mu * r for r in (r23, r13, r12)]
            own = [state[row * NODES + node] for row in range(FIELDS)]
            for row in range(FIELDS):
                acc[row * NODES + node] = average(own[row], row * NODES + node) + volume[row]
            dual = [pltpu.roll(x, SUBS - 2, axis=0) for x in own]
            pressure = div * (dual[3] + dual[4] + dual[5])
            normal = g11 * dual[3] + g22 * dual[4] + g33 * dual[5]
            shear = normal + normal + (r23 * dual[6] + r13 * dual[7] + r12 * dual[8])
            light = sdiv[0] * dual[0] + sdiv[1] * dual[1] + sdiv[2] * dual[2]
            for m, value in enumerate((pressure, shear, light)):
                products[pl.ds((m * LANES + node) * SUBS, SUBS), :] = value

    def z_lines(i, carry):
        for j in range(5):
            z_line(25 * i + 5 * j)
        return carry

    lax.fori_loop(0, ORDER, z_lines, 0)


def shot_sums(products, emit):
    for m in range(3):
        for g in range((NODES + 7) // 8):
            rows = min(8, NODES - 8 * g)
            base = (m * LANES + 8 * g) * SUBS
            for h in range(2):
                first = products[pl.ds(base + 4 * h, 8, stride=SUBS), :]
                second = products[pl.ds(base + 4 * h + 1, 8, stride=SUBS), :]
                emit(m, 8 * g, rows, h, (first + second)[:rows])


def local_pass(state, acc, med, codes_ref, slots, weight):
    half = half_of()
    low = half == 0
    free_code = 6 * slots + 4 * 32
    for face in range(6):
        codes = code_tile(codes_ref, face, slots)
        idx = codes & (LANES - 1)
        match = (codes >> 8) == (face ^ 1)
        same = match & (((codes >> 7) & 1) == half)
        cross = match & (((codes >> 7) & 1) != half)
        free = codes == free_code
        factor_v = jnp.where(free, 0.0, weight)
        factor_s = jnp.where(free, 2.0 * weight, weight)
        other = face ^ 1

        def body(u, carry, face=face, other=other, idx=idx, same=same, cross=cross,
                 factor_v=factor_v, factor_s=factor_s):
            for v in range(ORDER):
                shift = FACE_U[face] * u + FACE_V[face] * v
                node = FACE_OFF[face] + shift
                source = FACE_OFF[other] + shift
                jumps = []
                for k in range(FIELDS):
                    there = state[k * NODES + source]
                    outer = jnp.where(same, lane_pick(there, idx), 0.0)
                    outer = jnp.where(cross, lane_pick(swap_halves(there), idx), outer)
                    jump = outer - state[k * NODES + node]
                    jumps.append(jump * (factor_v if k < 3 else factor_s))
                add_rows(acc, node, jumps, coefs(med, node), face // 2, 2 * (face % 2) - 1)
            return carry

        lax.fori_loop(0, ORDER, body, 0, unroll=True)


def ghost_tiles(ghost, p, low):
    tile = ghost[p]
    turned = swap_halves(tile)
    tile9 = ghost[FACE + (p >> 3)]
    turned9 = swap_halves(tile9)
    chosen = half_of() == ((p >> 2) & 1)
    return jnp.where(low, tile, turned), jnp.where(low, turned, tile), jnp.where(chosen, tile9, turned9)


def ghost_pass(acc, med, codes_ref, ghost, axis, up, slots, scale):
    low = half_of() == 0
    face = 2 * axis + up
    sign = (2 * up - 1).astype(jnp.float32)
    codes = code_tile(codes_ref, face, slots) - (6 * slots + 32 * face)
    inside = (codes >= 0) & (codes < 32)
    weight = jnp.where(inside, scale, 0.0)
    idx = codes & 31
    shifted = [idx + 32 * q for q in range(4)]
    start = side_offset(axis, up)

    def body(u, carry):
        for v in range(ORDER):
            p = ORDER * u + v
            node = start + FACE_U[2 * axis] * u + FACE_V[2 * axis] * v
            first, second, nine = ghost_tiles(ghost, p, low)
            jumps = []
            for k in range(8):
                jumps.append(lane_pick(first if k < 4 else second, shifted[k % 4]) * weight)
            jumps.append(lane_pick(nine, idx + 32 * (p & 3)) * weight)
            lam, mu, buoy, speed = coefs(med, node)
            add_rows(acc, node, jumps, (sign * lam, sign * mu, sign * buoy, speed), axis, 1)
        return carry

    lax.fori_loop(0, ORDER, body, 0, unroll=True)


def other_sources(state, acc, med, codes_ref, ghosts, ups, axes, outer, slots, scale):
    half = half_of()
    low = half == 0
    first_ghost = 6 * slots

    def codes_of(face):
        return code_tile(codes_ref, face, slots)

    left = jnp.zeros((SUBS, LANES), jnp.int32)
    for face in range(6):
        codes = codes_of(face)
        source = jnp.where(codes < first_ghost, codes >> 8, 6 + ((codes - first_ghost) >> 5))
        usual = (source == (face ^ 1)) | (source >= 10)
        if face < 4:
            usual = usual | (source == 6 + face)
        left = left | jnp.where(usual, 0, 1)
    remaining = jnp.max(left)

    @pl.when(remaining > 0)
    def _():
        def pair(t, carry):
            face, origin = t // 10, t % 10
            codes = code_tile(codes_ref, face, slots)
            source = jnp.where(codes < first_ghost, codes >> 8, 6 + ((codes - first_ghost) >> 5))
            mine = source == origin
            done = (origin == (face ^ 1)) | ((face < 4) & (origin == 6 + face))
            count = jnp.max(jnp.where(mine, 1, 0))

            @pl.when((count > 0) & jnp.logical_not(done))
            def _():
                weight = jnp.where(mine, scale, 0.0)
                axis, sign = face >> 1, (2 * (face & 1) - 1).astype(jnp.float32)

                def strides(which):
                    line = which >> 1
                    off = (which & 1) * jnp.where(line == 0, 100, jnp.where(line == 1, 20, 4))
                    return off, jnp.where(line == 0, 5, 25), jnp.where(line == 2, 5, 1)

                off, du, dv = strides(face)
                off2, du2, dv2 = strides(jnp.minimum(origin, 5))

                def at_node(p, carry):
                    u, v = p // ORDER, p % ORDER
                    node = off + du * u + dv * v

                    @pl.when(origin < 6)
                    def _():
                        there_node = off2 + du2 * u + dv2 * v
                        idx = codes & (LANES - 1)
                        same = ((codes >> 7) & 1) == half
                        for k in range(FIELDS):
                            there = state[k * NODES + there_node]
                            turned = swap_halves(there)
                            outer[k] = jnp.where(same, lane_pick(there, idx), lane_pick(turned, idx)) * weight

                    @pl.when(origin >= 6)
                    def _():
                        for k in range(FIELDS):
                            outer[k] = jnp.zeros((SUBS, LANES), jnp.float32)

                    for ghost, up, line in zip(ghosts, ups, axes):

                        @pl.when(origin == 6 + 2 * line + up)
                        def _(ghost=ghost):
                            idx = (codes - first_ghost) & 31
                            first, second, nine = ghost_tiles(ghost, p, low)
                            for k in range(8):
                                tile = first if k < 4 else second
                                outer[k] = lane_pick(tile, idx + 32 * (k % 4)) * weight
                            outer[8] = lane_pick(nine, idx + 32 * (p & 3)) * weight

                    lam, mu, buoy, speed = coefs(med, node)
                    a = axis
                    b, c = lax.rem(axis + 1, 3), lax.rem(axis + 2, 3)
                    across = lam * outer[a]
                    flux = (
                        (a, buoy * outer[3 + a]),
                        (b, buoy * outer[6 + c]),
                        (c, buoy * outer[6 + b]),
                        (3 + a, across + (mu + mu) * outer[a]),
                        (3 + b, across),
                        (3 + c, across),
                        (6 + c, mu * outer[b]),
                        (6 + b, mu * outer[c]),
                        (6 + a, None),
                    )
                    for k, value in flux:
                        row = k * NODES + node
                        total = speed * outer[k]
                        if value is not None:
                            total = total + sign * value
                        acc[row] = acc[row] + total
                    return carry

                lax.fori_loop(0, FACE, at_node, 0)

            return carry

        lax.fori_loop(0, 60, pair, 0)


def link_ups(place_ref, links):
    return [1 - ((lax.div(place_ref[0], stride) + parity) & 1) for _, stride, parity in links]


def load_kernel(slots, links, mat_hbm, fwd_hbm, adj_hbm, state_ref, med_ref, mat_ref, sems, mat_sem):
    mat_copy = pltpu.make_async_copy(mat_hbm, mat_ref, mat_sem)
    mat_copy.start()
    copies = []
    for k in range(FIELDS * ORDER):
        span = pl.ds(k * FACE, FACE)
        for n, far in enumerate((fwd_hbm, adj_hbm)):
            copies.append(pltpu.make_async_copy(far.at[span], state_ref.at[span, :, n], sems.at[n, k]))
            copies[-1].start()
    mat_copy.wait()
    spread_material(mat_ref, med_ref)
    for copy in copies:
        copy.wait()


def pack_links(slots, links, place_ref, state_ref, list_ref, sends, line):
    ups = link_ups(place_ref, links)
    chosen = [n for n, link in enumerate(links) if link[0] == line]
    for n, send in zip(chosen, sends):
        pack_side(state_ref, list_ref, send, line, ups[n], slots)


def pack_kernel(line, slots, links, place_ref, state_ref, list_ref, *sends):
    pack_links(slots, links, place_ref, state_ref, list_ref, sends, line)


def late_pack_kernel(line, slots, links, place_ref, state_ref, list_ref, grad_ref, *sends):
    pack_links(slots, links, place_ref, state_ref, list_ref, sends, line)


def spread_material(mat_ref, med_ref):
    low = half_of() == 0
    for node in range(NODES):
        rows = []
        for m in range(3):
            first = jnp.broadcast_to(mat_ref[m, node : node + 1, 0:LANES], (SUBS, LANES))
            second = jnp.broadcast_to(mat_ref[m, node : node + 1, LANES : 2 * LANES], (SUBS, LANES))
            rows.append(jnp.where(low, first, second))
        lam, mu, buoy = rows
        speed = jnp.sqrt((lam + 2.0 * mu) * buoy)
        for m, value in enumerate((lam, mu, buoy, speed)):
            med_ref[m * NODES + node] = step_size * value


def first_kernel(slots, links, counts_ref, state_ref, med_ref, codes_ref, acc_ref, grad_ref, products):
    volume_pass(state_ref, acc_ref, med_ref, products, lambda own, row: own, lambda value: value)
    shot_sums(products, store_gradient(counts_ref, [grad_ref], None))
    local_pass(state_ref, acc_ref, med_ref, codes_ref, slots, 0.5 * lift_weight)


def store_gradient(counts_ref, grad_refs, earlier_ref):
    lane = lax.broadcasted_iota(jnp.int32, (SUBS, LANES), 1)
    count = jnp.broadcast_to(counts_ref[...], (SUBS, LANES))

    def emit(m, start, rows, h, value):
        at = (m, slice(start, start + rows), slice(h * LANES, (h + 1) * LANES))
        if earlier_ref is not None:
            value = (0.5 * step_size) * (earlier_ref[at] + value)
        value = jnp.where((h * LANES + lane < count)[:rows], value, 0.0)
        for grad_ref in grad_refs:
            size = grad_ref.shape[1]
            if 0 <= start < size:
                grad_ref[m, start : start + rows, h * LANES : (h + 1) * LANES] = value
            start -= size

    return emit


def ghost_stage(slots, links, ups, state_ref, acc_ref, med_ref, codes_ref, ghosts, outer, scale):
    axes = [link[0] for link in links]
    for axis, up, ghost in zip(axes, ups, ghosts):
        ghost_pass(acc_ref, med_ref, codes_ref, ghost, axis, up, slots, scale)
    other_sources(state_ref, acc_ref, med_ref, codes_ref, ghosts, ups, axes, outer, slots, scale)


def middle_kernel(slots, links, place_ref, acc_in, state_ref, med_ref, codes_ref, list_ref, *rest):
    count = len(links)
    ghosts, mid_ref, sends, outer = rest[:count], rest[count], rest[count + 1 : -1], rest[-1]
    ups = link_ups(place_ref, links)
    ghost_stage(slots, links, ups, state_ref, mid_ref, med_ref, codes_ref, ghosts, outer, 0.5 * lift_weight)
    pack_links(slots, links, place_ref, mid_ref, list_ref, sends, 0)


def second_volume_kernel(slots, links, counts_ref, mid_ref, state_ref, med_ref, first_ref, acc_ref, near_ref, far_ref, products):
    share = jnp.where(live_tile(counts_ref), 0.5, 0.0)
    volume_pass(
        mid_ref, acc_ref, med_ref, products,
        lambda own, row: share * (own + state_ref[row]), lambda value: share * value,
    )
    shot_sums(products, store_gradient(counts_ref, [near_ref, far_ref], first_ref))


def second_faces_kernel(slots, links, counts_ref, acc_in, mid_ref, med_ref, codes_ref, acc_ref):
    weight = jnp.where(live_tile(counts_ref), 0.25 * lift_weight, 0.0)
    local_pass(mid_ref, acc_ref, med_ref, codes_ref, slots, weight)


def second_ghosts_kernel(chosen, slots, links, place_ref, acc_in, med_ref, codes_ref, *rest):
    ghosts, acc_ref = rest[: len(chosen)], rest[-1]
    ups = link_ups(place_ref, links)
    for n, ghost in zip(chosen, ghosts):
        ghost_pass(acc_ref, med_ref, codes_ref, ghost, links[n][0], ups[n], slots, 0.25 * lift_weight)


def other_sources_kernel(slots, links, place_ref, acc_in, mid_ref, med_ref, codes_ref, *rest):
    ghosts, (acc_ref, outer) = rest[: len(links)], rest[len(links) :]
    ups = link_ups(place_ref, links)
    axes = [link[0] for link in links]
    other_sources(mid_ref, acc_ref, med_ref, codes_ref, ghosts, ups, axes, outer, slots, 0.25 * lift_weight)


def partial_kernel(slots, links, acc_in, a_ref, b_ref, near_ref, far_ref, acc_ref, first_ref, second_ref):
    first_ref[...] = a_ref[...] + near_ref[...]
    second_ref[...] = b_ref[...] + far_ref[...]


def total_kernel(slots, links, a_ref, b_ref, c_ref, d_ref, grad_ref):
    cut = a_ref.shape[1]
    grad_ref[:, :cut] = a_ref[...] + c_ref[...]
    grad_ref[:, cut:] = b_ref[...] + d_ref[...]


def store_kernel(slots, links, acc_ref, fwd_hbm, adj_hbm, sems):
    copies = []
    for k in range(FIELDS):
        span = pl.ds(k * NODES, NODES)
        for n, far in enumerate((fwd_hbm, adj_hbm)):
            copies.append(pltpu.make_async_copy(acc_ref.at[span, :, n], far.at[span], sems.at[n, k]))
            copies[-1].start()
    for copy in copies:
        copy.wait()


def tree_links(devices):
    links = []
    for axis, stride in ((0, DEV_Y), (1, 1)):
        for parity in range(2):
            pairs = [(d, d + stride) for d in range(devices - stride) if (d // stride) % 2 == parity]
            if pairs:
                links.append((axis, stride, parity, pairs + [(b, a) for a, b in pairs]))
    return links


def swapped(block, axis, distance):
    route = [(i, i ^ distance) for i in range(lax.axis_size(axis))]
    return lax.ppermute(block, axis, route)


def shards(forward, adjoint, material, counts, send_list, neighbours):
    shots, fields, nodes, slots = forward.shape
    halves = slots // LANES
    rows = fields * nodes
    assert 2 * shots * halves == SUBS and nodes == NODES and fields == FIELDS

    def dense(values):
        cut = values.reshape(shots, fields, nodes, halves, LANES)
        tiles = cut.transpose(1, 2, 3, 0, 4).reshape(rows, halves, shots, LANES)
        return pltpu.with_memory_space_constraint(tiles, pltpu.HBM)

    def restored(values):
        cut = values.reshape(fields, nodes, halves, shots, LANES)
        return cut.transpose(3, 0, 1, 2, 4).reshape(shots, fields, nodes, slots)

    links = tree_links(lax.axis_size("dom"))
    axes = tuple(link[:3] for link in links)
    place = lax.axis_index("dom").astype(jnp.int32).reshape(1)
    counts = counts.reshape(1, 1)

    def exchange(sends, line):
        routes = [link[3] for link in links if link[0] == line]
        return [lax.ppermute(send, "dom", route) for send, route in zip(sends, routes)]

    vmem = pl.BlockSpec(memory_space=pltpu.VMEM)
    smem = pl.BlockSpec(memory_space=pltpu.SMEM)
    hbm = pl.BlockSpec(memory_space=pltpu.HBM)
    f32 = jnp.float32
    state_shape = pltpu.VMEM((rows, SUBS, LANES), f32)
    send_shape = pltpu.VMEM((FACE + 4, SUBS, LANES), f32)
    med_shape = pltpu.VMEM((4 * nodes, SUBS, LANES), f32)
    grad_shape = pltpu.VMEM(material.shape, f32)
    apart = (rows, halves, 2, shots, LANES)
    part_shape = jax.ShapeDtypeStruct((rows, halves, shots, LANES), f32)
    products = pltpu.VMEM((3 * LANES * SUBS, LANES), f32)
    outer = pltpu.VMEM((FIELDS, SUBS, LANES), f32)
    field_sems = pltpu.SemaphoreType.DMA((2, FIELDS))

    def call(kernel, out_shape, in_specs, name, micros, scratch=(), out_specs=None, aliases=None):
        return pl.pallas_call(
            functools.partial(kernel, slots, axes),
            out_shape=out_shape,
            in_specs=in_specs,
            out_specs=out_specs or [vmem] * len(out_shape),
            scratch_shapes=list(scratch),
            input_output_aliases=aliases or {},
            compiler_params=pltpu.CompilerParams(vmem_limit_bytes=VMEM_BYTES),
            cost_estimate=pl.CostEstimate(flops=int(micros * 10**9), bytes_accessed=0, transcendentals=0),
            name=name,
        )

    count = len(links)
    state, med = call(
        load_kernel, [pltpu.VMEM(apart, f32), med_shape], [hbm] * 3, "load", 4,
        [pltpu.VMEM(material.shape, f32), pltpu.SemaphoreType.DMA((2, FIELDS * ORDER)), pltpu.SemaphoreType.DMA],
    )(pltpu.with_memory_space_constraint(material, pltpu.HBM), dense(forward), dense(adjoint))
    state = state.reshape(rows, SUBS, LANES)
    by_line = [[send_shape for link in links if link[0] == line] for line in range(2)]
    across = len(by_line[0])
    ghosts = []
    for line in range(2):
        sends = call(functools.partial(pack_kernel, line), by_line[line], [smem, vmem, vmem], "pack", 0)(
            place, state, send_list
        )
        ghosts += exchange(sends, line)
    acc, grad_first = call(
        first_kernel, [state_shape, grad_shape], [vmem] + [vmem] * 3, "first_section", 8, [products]
    )(counts, state, med, neighbours)
    mid, *sends = call(
        middle_kernel, [state_shape] + by_line[0], [smem] + [vmem] * (5 + count), "first_ghosts", 4,
        [outer], aliases={1: 0},
    )(place, acc, state, med, neighbours, send_list, *ghosts)
    ghosts = exchange(sends, 0)
    cut = (nodes // 2 + SUBS // 2) // SUBS * SUBS
    part_shapes = [pltpu.VMEM((3, size, slots), f32) for size in (cut, nodes - cut)]
    acc, *halved = call(
        second_volume_kernel, [state_shape] + part_shapes, [vmem] + [vmem] * 4, "second_volume", 0, [products]
    )(counts, mid, state, med, grad_first)
    sends = call(
        functools.partial(late_pack_kernel, 1), by_line[1], [smem] + [vmem] * 3, "pack", 0.5
    )(place, mid, send_list, halved[0])
    ghosts += exchange(sends, 1)
    doubling = lax.axis_size("shot") == 4
    if doubling:
        pieces = [swapped(halved[0], "shot", 1), swapped(halved[1], "shot", 2)]
    (acc,) = call(
        second_faces_kernel, [state_shape], [vmem] + [vmem] * 4, "second_faces", 0.5, aliases={1: 0}
    )(counts, acc, mid, med, neighbours)

    def add_ghosts(acc, chosen, micros):
        (acc,) = call(
            functools.partial(second_ghosts_kernel, chosen), [state_shape], [smem] + [vmem] * (3 + len(chosen)),
            "second_ghosts", micros, aliases={1: 0},
        )(place, acc, med, neighbours, *[ghosts[n] for n in chosen])
        return acc

    acc = add_ghosts(acc, range(across), 1)
    if doubling:
        acc, *parts = call(
            partial_kernel, [state_shape] + part_shapes, [vmem] * 5, "gradient_partial", 0, aliases={0: 0}
        )(acc, *halved, *pieces)
        pieces = [swapped(parts[0], "shot", 2), swapped(parts[1], "shot", 1)]
    else:
        gradient = lax.psum(jnp.concatenate(halved, axis=1), "shot")
    acc = add_ghosts(acc, range(across, count), 1)
    (acc,) = call(
        other_sources_kernel, [state_shape], [smem] + [vmem] * (4 + count), "other_sources", 0, [outer], aliases={1: 0}
    )(place, acc, mid, med, neighbours, *ghosts)
    fwd, adj = call(store_kernel, [part_shape, part_shape], [vmem], "store", 4, [field_sems], [hbm, hbm])(
        acc.reshape(apart)
    )
    if doubling:
        (gradient,) = call(
            total_kernel, [jax.ShapeDtypeStruct(material.shape, f32)], [vmem] * 4, "gradient_total", 0
        )(*parts, *pieces)
    return restored(fwd), restored(adj), gradient


def solution(mesh):
    placed = (
        P("shot", None, None, "dom"),
        P("shot", None, None, "dom"),
        P(None, None, "dom"),
        P("dom"),
        P("dom", None, None),
        P("dom", None),
    )
    return jax.shard_map(
        shards,
        mesh=mesh,
        in_specs=placed,
        out_specs=(
            P("shot", None, None, "dom"),
            P("shot", None, None, "dom"),
            P(None, None, "dom"),
        ),
        check_vma=False,
    )
```

```python
import functools

import jax
import jax.numpy as jnp
import numpy as np
from jax import lax
from jax.experimental import pallas as pl
from jax.experimental.pallas import tpu as pltpu
from jax.sharding import PartitionSpec as P

DEV_Y = 4
ORDER = 5
NODES = ORDER**3
FACE = ORDER * ORDER
FIELDS = 9
LANES = 128
SUBS = 8
step_size = 0.01
lift_weight = 10.0
VMEM_BYTES = 16 * 1024 * 1024

FACE_OFF = (0, 100, 0, 20, 0, 4)
FACE_U = (5, 5, 25, 25, 25, 25)
FACE_V = (1, 1, 1, 1, 5, 5)


def derivative_matrix():
    points = np.array([-1.0, -np.sqrt(3.0 / 7.0), 0.0, np.sqrt(3.0 / 7.0), 1.0])
    barycentric = np.array(
        [1.0 / np.prod([points[a] - points[b] for b in range(5) if b != a]) for a in range(5)]
    )
    matrix = np.zeros((5, 5))
    for a in range(5):
        for b in range(5):
            if a != b:
                matrix[a, b] = barycentric[b] / barycentric[a] / (points[a] - points[b])
        matrix[a, a] = -np.sum(matrix[a])
    return matrix


MAT = derivative_matrix()


def derivative(u):
    e0, e1 = u[0] + u[4], u[1] + u[3]
    o0, o1 = u[0] - u[4], u[1] - u[3]
    mid = u[2] + u[2]
    e0, e1 = e0 - mid, e1 - mid
    out = [None] * 5
    for a in range(2):
        even = float(0.5 * (MAT[a, 0] + MAT[a, 4])) * e0 + float(0.5 * (MAT[a, 1] + MAT[a, 3])) * e1
        odd = float(0.5 * (MAT[a, 0] - MAT[a, 4])) * o0 + float(0.5 * (MAT[a, 1] - MAT[a, 3])) * o1
        out[a] = odd + even
        out[4 - a] = odd - even
    out[2] = float(MAT[2, 0]) * o0 + float(MAT[2, 1]) * o1
    return out


def sub_iota():
    return lax.broadcasted_iota(jnp.int32, (SUBS, LANES), 0)


def half_of():
    return sub_iota() >> 2


def swap_halves(x):
    return pltpu.roll(x, SUBS // 2, axis=0)


def lane_pick(x, idx):
    return jnp.take_along_axis(x, idx, axis=1, mode="promise_in_bounds")


def code_tile(codes_ref, face, slots):
    base = face * slots
    rows = []
    for h in range(2):
        at = base + h * LANES
        at = at if isinstance(at, int) else pl.multiple_of(at, LANES)
        rows.append(jnp.broadcast_to(codes_ref[0:1, pl.ds(at, LANES)], (SUBS, LANES)))
    first, second = rows
    return jnp.where(half_of() == 0, first, second)


def side_offset(axis, up):
    return up * FACE_OFF[2 * axis + 1]


def pack_side(state, list_ref, out, axis, up, slots):
    half = half_of()
    low = half == 0
    lane_group = lax.broadcasted_iota(jnp.int32, (SUBS, LANES), 1) >> 5
    masks = [lane_group == q for q in range(1, 4)]
    side = 2 * axis
    row = jnp.where(up > 0, list_ref[0, side + 1 : side + 2, :], list_ref[0, side : side + 1, :])
    listed = jnp.broadcast_to(jnp.concatenate([row] * 4, axis=1), (SUBS, LANES))
    idx = listed & (LANES - 1)
    here = (listed < slots) & ((listed >> 7) == half)
    start = side_offset(axis, up)

    def combine(parts):
        picked = [lane_pick(part, idx) for part in parts]
        groups = []
        for x in range(2):
            four = picked[4 * x : 4 * x + 4]
            tile = four[0]
            for q in range(1, len(four)):
                tile = jnp.where(masks[q - 1], four[q], tile)
            tile = jnp.where(here, tile, 0.0)
            groups.append(tile + swap_halves(tile))
        return jnp.where(low, groups[0], groups[1])

    for p in range(FACE):
        node = start + FACE_U[side] * (p // ORDER) + FACE_V[side] * (p % ORDER)
        out[p] = combine([state[k * NODES + node] for k in range(8)])
    for g in range(4):
        parts = []
        for w in range(8):
            p = min(8 * g + w, FACE - 1)
            node = start + FACE_U[side] * (p // ORDER) + FACE_V[side] * (p % ORDER)
            parts.append(state[8 * NODES + node])
        out[FACE + g] = combine(parts)


def add_rows(acc, node, jumps, coef, direction, sign):
    lam, mu, buoy, speed = coef
    a, b, c = direction, (direction + 1) % 3, (direction + 2) % 3
    s_aa, s_bb, s_cc = 3 + a, 3 + b, 3 + c
    s_ab, s_ac, s_bc = 6 + c, 6 + b, 6 + a
    across = lam * jumps[a]
    flux = {
        a: buoy * jumps[s_aa],
        b: buoy * jumps[s_ab],
        c: buoy * jumps[s_ac],
        s_aa: across + (mu + mu) * jumps[a],
        s_bb: across,
        s_cc: across,
        s_ab: mu * jumps[b],
        s_ac: mu * jumps[c],
    }
    for k in range(FIELDS):
        row = k * NODES + node
        total = speed * jumps[k]
        if k in flux:
            total = total + flux[k] if sign > 0 else total - flux[k]
        acc[row] = acc[row] + total


def coefs(med, node):
    return [med[m * NODES + node] for m in range(4)]


def volume_pass(state, turned, acc, med, products, average, scaled):
    def x_lines(j, carry):
        for k in range(5):
            for field, row in ((0, 3), (1, 8), (2, 7), (3, 0), (8, 1), (7, 2)):
                out = derivative([state[field * NODES + 25 * i + 5 * j + k] for i in range(5)])
                for i in range(5):
                    acc[row * NODES + 25 * i + 5 * j + k] = out[i]
        return carry

    lax.fori_loop(0, ORDER, x_lines, 0)

    def y_lines(i, carry):
        for k in range(5):
            for field, row, more in ((0, 8, 1), (1, 4, 0), (2, 6, 0), (8, 0, 1), (4, 1, 1), (6, 2, 1)):
                out = derivative([state[field * NODES + 25 * i + 5 * j + k] for j in range(5)])
                for j in range(5):
                    at = row * NODES + 25 * i + 5 * j + k
                    acc[at] = acc[at] + out[j] if more else out[j]
        return carry

    lax.fori_loop(0, ORDER, y_lines, 0)

    def z_line(first):
        parts = {}
        for field in (0, 1, 2, 7, 6, 5):
            parts[field] = derivative([state[field * NODES + first + k] for k in range(5)])
        for k in range(5):
            node = first + k
            lam, mu, buoy = (scaled(value) for value in coefs(med, node)[:3])
            old = [acc[row * NODES + node] for row in range(FIELDS) if row != 5]
            sdiv = [old[0] + parts[7][k], old[1] + parts[6][k], old[2] + parts[5][k]]
            g11, g22, g33 = old[3], old[4], parts[2][k]
            r23 = old[5] + parts[1][k]
            r13 = old[6] + parts[0][k]
            r12 = old[7]
            div = g11 + g22 + g33
            spread = lam * div
            mu2 = mu + mu
            volume = [buoy * s for s in sdiv]
            volume += [spread + mu2 * g for g in (g11, g22, g33)]
            volume += [mu * r for r in (r23, r13, r12)]
            own = [state[row * NODES + node] for row in range(FIELDS)]
            for row in range(FIELDS):
                turned[row * NODES + node] = swap_halves(own[row])
                acc[row * NODES + node] = average(own[row], row * NODES + node) + volume[row]
            dual = [pltpu.roll(x, SUBS - 2, axis=0) for x in own]
            pressure = div * (dual[3] + dual[4] + dual[5])
            normal = g11 * dual[3] + g22 * dual[4] + g33 * dual[5]
            shear = normal + normal + (r23 * dual[6] + r13 * dual[7] + r12 * dual[8])
            light = sdiv[0] * dual[0] + sdiv[1] * dual[1] + sdiv[2] * dual[2]
            for m, value in enumerate((pressure, shear, light)):
                products[pl.ds((m * LANES + node) * SUBS, SUBS), :] = value

    def z_lines(i, carry):
        for j in range(5):
            z_line(25 * i + 5 * j)
        return carry

    lax.fori_loop(0, ORDER, z_lines, 0)


def shot_sums(products, emit):
    for m in range(3):
        for g in range((NODES + 7) // 8):
            rows = min(8, NODES - 8 * g)
            base = (m * LANES + 8 * g) * SUBS
            for h in range(2):
                first = products[pl.ds(base + 4 * h, 8, stride=SUBS), :]
                second = products[pl.ds(base + 4 * h + 1, 8, stride=SUBS), :]
                emit(m, 8 * g, rows, h, (first + second)[:rows])


def local_pass(state, turned, acc, med, codes_ref, slots, weight):
    half = half_of()
    low = half == 0
    free_code = 6 * slots + 4 * 32
    for face in range(6):
        codes = code_tile(codes_ref, face, slots)
        idx = codes & (LANES - 1)
        match = (codes >> 8) == (face ^ 1)
        same = match & (((codes >> 7) & 1) == half)
        cross = match & (((codes >> 7) & 1) != half)
        free = codes == free_code
        factor_v = jnp.where(free, 0.0, weight)
        factor_s = jnp.where(free, 2.0 * weight, weight)
        other = face ^ 1

        def body(u, carry, face=face, other=other, idx=idx, same=same, cross=cross,
                 factor_v=factor_v, factor_s=factor_s):
            for v in range(ORDER):
                shift = FACE_U[face] * u + FACE_V[face] * v
                node = FACE_OFF[face] + shift
                source = FACE_OFF[other] + shift
                jumps = []
                for k in range(FIELDS):
                    there = state[k * NODES + source]
                    outer = jnp.where(same, lane_pick(there, idx), 0.0)
                    outer = jnp.where(cross, lane_pick(turned[k * NODES + source], idx), outer)
                    jump = outer - state[k * NODES + node]
                    jumps.append(jump * (factor_v if k < 3 else factor_s))
                add_rows(acc, node, jumps, coefs(med, node), face // 2, 2 * (face % 2) - 1)
            return carry

        lax.fori_loop(0, ORDER, body, 0, unroll=True)


def ghost_tiles(ghost, p, low):
    tile = ghost[p]
    turned = swap_halves(tile)
    tile9 = ghost[FACE + (p >> 3)]
    turned9 = swap_halves(tile9)
    chosen = half_of() == ((p >> 2) & 1)
    return jnp.where(low, tile, turned), jnp.where(low, turned, tile), jnp.where(chosen, tile9, turned9)


def ghost_pass(acc, med, codes_ref, ghost, axis, up, slots, scale):
    low = half_of() == 0
    face = 2 * axis + up
    sign = (2 * up - 1).astype(jnp.float32)
    codes = code_tile(codes_ref, face, slots) - (6 * slots + 32 * face)
    inside = (codes >= 0) & (codes < 32)
    weight = jnp.where(inside, scale, 0.0)
    idx = codes & 31
    shifted = [idx + 32 * q for q in range(4)]
    start = side_offset(axis, up)

    def body(u, carry):
        for v in range(ORDER):
            p = ORDER * u + v
            node = start + FACE_U[2 * axis] * u + FACE_V[2 * axis] * v
            first, second, nine = ghost_tiles(ghost, p, low)
            jumps = []
            for k in range(8):
                jumps.append(lane_pick(first if k < 4 else second, shifted[k % 4]) * weight)
            jumps.append(lane_pick(nine, idx + 32 * (p & 3)) * weight)
            lam, mu, buoy, speed = coefs(med, node)
            add_rows(acc, node, jumps, (sign * lam, sign * mu, sign * buoy, speed), axis, 1)
        return carry

    lax.fori_loop(0, ORDER, body, 0, unroll=True)


def other_sources(state, acc, med, codes_ref, ghosts, ups, axes, outer, slots, scale):
    half = half_of()
    low = half == 0
    first_ghost = 6 * slots

    def codes_of(face):
        return code_tile(codes_ref, face, slots)

    left = jnp.zeros((SUBS, LANES), jnp.int32)
    for face in range(6):
        codes = codes_of(face)
        source = jnp.where(codes < first_ghost, codes >> 8, 6 + ((codes - first_ghost) >> 5))
        usual = (source == (face ^ 1)) | (source >= 10)
        if face < 4:
            usual = usual | (source == 6 + face)
        left = left | jnp.where(usual, 0, 1)
    remaining = jnp.max(left)

    @pl.when(remaining > 0)
    def _():
        def pair(t, carry):
            face, origin = t // 10, t % 10
            codes = code_tile(codes_ref, face, slots)
            source = jnp.where(codes < first_ghost, codes >> 8, 6 + ((codes - first_ghost) >> 5))
            mine = source == origin
            done = (origin == (face ^ 1)) | ((face < 4) & (origin == 6 + face))
            count = jnp.max(jnp.where(mine, 1, 0))

            @pl.when((count > 0) & jnp.logical_not(done))
            def _():
                weight = jnp.where(mine, scale, 0.0)
                axis, sign = face >> 1, (2 * (face & 1) - 1).astype(jnp.float32)

                def strides(which):
                    line = which >> 1
                    off = (which & 1) * jnp.where(line == 0, 100, jnp.where(line == 1, 20, 4))
                    return off, jnp.where(line == 0, 5, 25), jnp.where(line == 2, 5, 1)

                off, du, dv = strides(face)
                off2, du2, dv2 = strides(jnp.minimum(origin, 5))

                def at_node(p, carry):
                    u, v = p // ORDER, p % ORDER
                    node = off + du * u + dv * v

                    @pl.when(origin < 6)
                    def _():
                        there_node = off2 + du2 * u + dv2 * v
                        idx = codes & (LANES - 1)
                        same = ((codes >> 7) & 1) == half
                        for k in range(FIELDS):
                            there = state[k * NODES + there_node]
                            turned = swap_halves(there)
                            outer[k] = jnp.where(same, lane_pick(there, idx), lane_pick(turned, idx)) * weight

                    @pl.when(origin >= 6)
                    def _():
                        for k in range(FIELDS):
                            outer[k] = jnp.zeros((SUBS, LANES), jnp.float32)

                    for ghost, up, line in zip(ghosts, ups, axes):

                        @pl.when(origin == 6 + 2 * line + up)
                        def _(ghost=ghost):
                            idx = (codes - first_ghost) & 31
                            first, second, nine = ghost_tiles(ghost, p, low)
                            for k in range(8):
                                tile = first if k < 4 else second
                                outer[k] = lane_pick(tile, idx + 32 * (k % 4)) * weight
                            outer[8] = lane_pick(nine, idx + 32 * (p & 3)) * weight

                    lam, mu, buoy, speed = coefs(med, node)
                    a = axis
                    b, c = lax.rem(axis + 1, 3), lax.rem(axis + 2, 3)
                    across = lam * outer[a]
                    flux = (
                        (a, buoy * outer[3 + a]),
                        (b, buoy * outer[6 + c]),
                        (c, buoy * outer[6 + b]),
                        (3 + a, across + (mu + mu) * outer[a]),
                        (3 + b, across),
                        (3 + c, across),
                        (6 + c, mu * outer[b]),
                        (6 + b, mu * outer[c]),
                        (6 + a, None),
                    )
                    for k, value in flux:
                        row = k * NODES + node
                        total = speed * outer[k]
                        if value is not None:
                            total = total + sign * value
                        acc[row] = acc[row] + total
                    return carry

                lax.fori_loop(0, FACE, at_node, 0)

            return carry

        lax.fori_loop(0, 60, pair, 0)


def link_ups(place_ref, links):
    return [1 - ((lax.div(place_ref[0], stride) + parity) & 1) for _, stride, parity in links]


def load_kernel(slots, links, mat_hbm, fwd_hbm, adj_hbm, state_ref, med_ref, mat_ref, sems, mat_sem):
    mat_copy = pltpu.make_async_copy(mat_hbm, mat_ref, mat_sem)
    mat_copy.start()
    copies = []
    for k in range(FIELDS):
        span = pl.ds(k * NODES, NODES)
        for n, far in enumerate((fwd_hbm, adj_hbm)):
            copies.append(pltpu.make_async_copy(far.at[span], state_ref.at[span, :, n], sems.at[n, k]))
            copies[-1].start()
    mat_copy.wait()
    spread_material(mat_ref, med_ref)
    for copy in copies:
        copy.wait()


def pack_links(slots, links, place_ref, state_ref, list_ref, sends, line):
    ups = link_ups(place_ref, links)
    chosen = [n for n, link in enumerate(links) if link[0] == line]
    for n, send in zip(chosen, sends):
        pack_side(state_ref, list_ref, send, line, ups[n], slots)


def pack_kernel(line, slots, links, place_ref, state_ref, list_ref, *sends):
    pack_links(slots, links, place_ref, state_ref, list_ref, sends, line)


def late_pack_kernel(slots, links, place_ref, state_ref, list_ref, grad_ref, *sends):
    across = sum(link[0] == 0 for link in links)
    pack_links(slots, links, place_ref, state_ref, list_ref, sends[:across], 0)
    pack_links(slots, links, place_ref, state_ref, list_ref, sends[across:], 1)


def spread_material(mat_ref, med_ref):
    low = half_of() == 0
    for node in range(NODES):
        rows = []
        for m in range(3):
            first = jnp.broadcast_to(mat_ref[m, node : node + 1, 0:LANES], (SUBS, LANES))
            second = jnp.broadcast_to(mat_ref[m, node : node + 1, LANES : 2 * LANES], (SUBS, LANES))
            rows.append(jnp.where(low, first, second))
        lam, mu, buoy = rows
        speed = jnp.sqrt((lam + 2.0 * mu) * buoy)
        for m, value in enumerate((lam, mu, buoy, speed)):
            med_ref[m * NODES + node] = step_size * value


def first_kernel(slots, links, counts_ref, state_ref, med_ref, codes_ref, acc_ref, grad_ref, live_ref, products, turned):
    lane = lax.broadcasted_iota(jnp.int32, (SUBS, LANES), 1)
    count = jnp.broadcast_to(counts_ref[...].reshape(1, 1), (SUBS, LANES))
    live_ref[...] = jnp.where(half_of() * LANES + lane < count, 1.0, 0.0)
    volume_pass(state_ref, turned, acc_ref, med_ref, products, lambda own, row: own, lambda value: value)
    shot_sums(products, store_gradient(live_ref, [grad_ref], None))
    local_pass(state_ref, turned, acc_ref, med_ref, codes_ref, slots, 0.5 * lift_weight)


def store_gradient(live_ref, grad_refs, earlier_ref):
    alive = [jnp.broadcast_to(live_ref[4 * h : 4 * h + 1, :], (SUBS, LANES)) > 0.0 for h in range(2)]

    def emit(m, start, rows, h, value):
        at = (m, slice(start, start + rows), slice(h * LANES, (h + 1) * LANES))
        if earlier_ref is not None:
            value = (0.5 * step_size) * (earlier_ref[at] + value)
        value = jnp.where(alive[h][:rows], value, 0.0)
        for grad_ref in grad_refs:
            size = grad_ref.shape[1]
            if 0 <= start < size:
                grad_ref[m, start : start + rows, h * LANES : (h + 1) * LANES] = value
            start -= size

    return emit


def ghost_stage(slots, links, ups, state_ref, acc_ref, med_ref, codes_ref, ghosts, outer, scale):
    axes = [link[0] for link in links]
    for axis, up, ghost in zip(axes, ups, ghosts):
        ghost_pass(acc_ref, med_ref, codes_ref, ghost, axis, up, slots, scale)
    other_sources(state_ref, acc_ref, med_ref, codes_ref, ghosts, ups, axes, outer, slots, scale)


def middle_kernel(slots, links, place_ref, acc_in, state_ref, med_ref, codes_ref, *rest):
    ghosts, (mid_ref, outer) = rest[: len(links)], rest[len(links) :]
    ups = link_ups(place_ref, links)
    ghost_stage(slots, links, ups, state_ref, mid_ref, med_ref, codes_ref, ghosts, outer, 0.5 * lift_weight)


def second_volume_kernel(
    slots, links, live_ref, mid_ref, state_ref, med_ref, first_ref, acc_ref, turned, near_ref, far_ref, products
):
    share = 0.5 * live_ref[...]
    volume_pass(
        mid_ref, turned, acc_ref, med_ref, products,
        lambda own, row: share * (own + state_ref[row]), lambda value: share * value,
    )
    shot_sums(products, store_gradient(live_ref, [near_ref, far_ref], first_ref))


def second_faces_kernel(slots, links, live_ref, acc_in, mid_ref, turned, med_ref, codes_ref, acc_ref):
    weight = (0.25 * lift_weight) * live_ref[...]
    local_pass(mid_ref, turned, acc_ref, med_ref, codes_ref, slots, weight)


def second_ghosts_kernel(chosen, slots, links, place_ref, acc_in, med_ref, codes_ref, *rest):
    ghosts, acc_ref = rest[: len(chosen)], rest[-1]
    ups = link_ups(place_ref, links)
    for n, ghost in zip(chosen, ghosts):
        ghost_pass(acc_ref, med_ref, codes_ref, ghost, links[n][0], ups[n], slots, 0.25 * lift_weight)


def other_sources_kernel(slots, links, place_ref, acc_in, mid_ref, med_ref, codes_ref, *rest):
    ghosts, (acc_ref, outer) = rest[: len(links)], rest[len(links) :]
    ups = link_ups(place_ref, links)
    axes = [link[0] for link in links]
    other_sources(mid_ref, acc_ref, med_ref, codes_ref, ghosts, ups, axes, outer, slots, 0.25 * lift_weight)


def partial_kernel(slots, links, acc_in, a_ref, b_ref, near_ref, far_ref, acc_ref, first_ref, second_ref):
    first_ref[...] = a_ref[...] + near_ref[...]
    second_ref[...] = b_ref[...] + far_ref[...]


def total_kernel(slots, links, a_ref, b_ref, c_ref, d_ref, grad_ref):
    cut = a_ref.shape[1]
    grad_ref[:, :cut] = a_ref[...] + c_ref[...]
    grad_ref[:, cut:] = b_ref[...] + d_ref[...]


def store_kernel(slots, links, acc_ref, fwd_hbm, adj_hbm, sems):
    copies = []
    for k in range(FIELDS):
        span = pl.ds(k * NODES, NODES)
        for n, far in enumerate((fwd_hbm, adj_hbm)):
            copies.append(pltpu.make_async_copy(acc_ref.at[span, :, n], far.at[span], sems.at[n, k]))
            copies[-1].start()
    for copy in copies:
        copy.wait()


def tree_links(devices):
    links = []
    for axis, stride in ((0, DEV_Y), (1, 1)):
        for parity in range(2):
            pairs = [(d, d + stride) for d in range(devices - stride) if (d // stride) % 2 == parity]
            if pairs:
                links.append((axis, stride, parity, pairs + [(b, a) for a, b in pairs]))
    return links


def swapped(block, axis, distance):
    route = [(i, i ^ distance) for i in range(lax.axis_size(axis))]
    return lax.ppermute(block, axis, route)


def shards(forward, adjoint, material, counts, send_list, neighbours):
    shots, fields, nodes, slots = forward.shape
    halves = slots // LANES
    rows = fields * nodes
    assert 2 * shots * halves == SUBS and nodes == NODES and fields == FIELDS

    def dense(values):
        cut = values.reshape(shots, fields, nodes, halves, LANES)
        tiles = cut.transpose(1, 2, 3, 0, 4).reshape(rows, halves, shots, LANES)
        return pltpu.with_memory_space_constraint(tiles, pltpu.HBM)

    def restored(values):
        cut = values.reshape(fields, nodes, halves, shots, LANES)
        return cut.transpose(3, 0, 1, 2, 4).reshape(shots, fields, nodes, slots)

    links = tree_links(lax.axis_size("dom"))
    axes = tuple(link[:3] for link in links)
    place = lax.axis_index("dom").astype(jnp.int32).reshape(1)

    def exchange(sends, line):
        routes = [link[3] for link in links if link[0] == line]
        return [lax.ppermute(send, "dom", route) for send, route in zip(sends, routes)]

    vmem = pl.BlockSpec(memory_space=pltpu.VMEM)
    smem = pl.BlockSpec(memory_space=pltpu.SMEM)
    hbm = pl.BlockSpec(memory_space=pltpu.HBM)
    f32 = jnp.float32
    state_shape = pltpu.VMEM((rows, SUBS, LANES), f32)
    send_shape = pltpu.VMEM((FACE + 4, SUBS, LANES), f32)
    med_shape = pltpu.VMEM((4 * nodes, SUBS, LANES), f32)
    grad_shape = pltpu.VMEM(material.shape, f32)
    apart = (rows, halves, 2, shots, LANES)
    part_shape = jax.ShapeDtypeStruct((rows, halves, shots, LANES), f32)
    products = pltpu.VMEM((3 * LANES * SUBS, LANES), f32)
    outer = pltpu.VMEM((FIELDS, SUBS, LANES), f32)
    field_sems = pltpu.SemaphoreType.DMA((2, FIELDS))

    def call(kernel, out_shape, in_specs, name, micros, scratch=(), out_specs=None, aliases=None):
        return pl.pallas_call(
            functools.partial(kernel, slots, axes),
            out_shape=out_shape,
            in_specs=in_specs,
            out_specs=out_specs or [vmem] * len(out_shape),
            scratch_shapes=list(scratch),
            input_output_aliases=aliases or {},
            compiler_params=pltpu.CompilerParams(vmem_limit_bytes=VMEM_BYTES),
            cost_estimate=pl.CostEstimate(flops=int(micros * 10**9), bytes_accessed=0, transcendentals=0),
            name=name,
        )

    count = len(links)
    state, med = call(
        load_kernel, [pltpu.VMEM(apart, f32), med_shape], [hbm] * 3, "load", 4,
        [pltpu.VMEM(material.shape, f32), field_sems, pltpu.SemaphoreType.DMA],
    )(
        pltpu.with_memory_space_constraint(material, pltpu.HBM), dense(forward), dense(adjoint),
    )
    state = state.reshape(rows, SUBS, LANES)
    by_line = [[send_shape for link in links if link[0] == line] for line in range(2)]
    across = len(by_line[0])
    ghosts = []
    for line in range(2):
        sends = call(functools.partial(pack_kernel, line), by_line[line], [smem, vmem, vmem], "pack", 0)(
            place, state, send_list
        )
        ghosts += exchange(sends, line)
    acc, grad_first, live = call(
        first_kernel, [state_shape, grad_shape, pltpu.VMEM((SUBS, LANES), f32)], [vmem] + [vmem] * 3, "first_section", 8, [products, pltpu.VMEM((rows, SUBS, LANES), f32)]
    )(counts, state, med, neighbours)
    (mid,) = call(
        middle_kernel, [state_shape], [smem] + [vmem] * (4 + count), "first_ghosts", 4, [outer], aliases={1: 0}
    )(place, acc, state, med, neighbours, *ghosts)
    cut = (nodes // 2 + SUBS // 2) // SUBS * SUBS
    part_shapes = [pltpu.VMEM((3, size, slots), f32) for size in (cut, nodes - cut)]
    acc, turned, *halved = call(
        second_volume_kernel, [state_shape] * 2 + part_shapes, [vmem] + [vmem] * 4, "second_volume", 0, [products]
    )(live, mid, state, med, grad_first)
    sends = call(late_pack_kernel, [send_shape] * count, [smem] + [vmem] * 3, "pack", 0.5)(
        place, mid, send_list, halved[0]
    )
    ghosts = exchange(sends[:across], 0) + exchange(sends[across:], 1)
    doubling = lax.axis_size("shot") == 4
    if doubling:
        pieces = [swapped(halved[0], "shot", 1), swapped(halved[1], "shot", 2)]
    (acc,) = call(
        second_faces_kernel, [state_shape], [vmem] * 6, "second_faces", 0.5, aliases={1: 0}
    )(live, acc, mid, turned, med, neighbours)

    def add_ghosts(acc, chosen, micros):
        (acc,) = call(
            functools.partial(second_ghosts_kernel, chosen), [state_shape], [smem] + [vmem] * (3 + len(chosen)),
            "second_ghosts", micros, aliases={1: 0},
        )(place, acc, med, neighbours, *[ghosts[n] for n in chosen])
        return acc

    if doubling:
        acc, *parts = call(
            partial_kernel, [state_shape] + part_shapes, [vmem] * 5, "gradient_partial", 0, aliases={0: 0}
        )(acc, *halved, *pieces)
        pieces = [swapped(parts[0], "shot", 2), swapped(parts[1], "shot", 1)]
    else:
        gradient = lax.psum(jnp.concatenate(halved, axis=1), "shot")
    acc = add_ghosts(acc, range(count), 1)
    (acc,) = call(
        other_sources_kernel, [state_shape], [smem] + [vmem] * (4 + count), "other_sources", 0, [outer], aliases={1: 0}
    )(place, acc, mid, med, neighbours, *ghosts)
    fwd, adj = call(store_kernel, [part_shape, part_shape], [vmem], "store", 4, [field_sems], [hbm, hbm])(
        acc.reshape(apart)
    )
    if doubling:
        (gradient,) = call(
            total_kernel, [jax.ShapeDtypeStruct(material.shape, f32)], [vmem] * 4, "gradient_total", 0
        )(*parts, *pieces)
    return restored(fwd), restored(adj), gradient


def solution(mesh):
    placed = (
        P("shot", None, None, "dom"),
        P("shot", None, None, "dom"),
        P(None, None, "dom"),
        P("dom"),
        P("dom", None, None),
        P("dom", None),
    )
    return jax.shard_map(
        shards,
        mesh=mesh,
        in_specs=placed,
        out_specs=(
            P("shot", None, None, "dom"),
            P("shot", None, None, "dom"),
            P(None, None, "dom"),
        ),
        check_vma=False,
    )
```

```python
import functools

import jax
import jax.numpy as jnp
import numpy as np
from jax import lax
from jax.experimental import pallas as pl
from jax.experimental.pallas import tpu as pltpu
from jax.sharding import PartitionSpec as P

DEV_Y = 4
ORDER = 5
NODES = ORDER**3
FACE = ORDER * ORDER
FIELDS = 9
LANES = 128
SUBS = 8
step_size = 0.01
lift_weight = 10.0
VMEM_BYTES = 16 * 1024 * 1024

FACE_OFF = (0, 100, 0, 20, 0, 4)
FACE_U = (5, 5, 25, 25, 25, 25)
FACE_V = (1, 1, 1, 1, 5, 5)


def derivative_matrix():
    points = np.array([-1.0, -np.sqrt(3.0 / 7.0), 0.0, np.sqrt(3.0 / 7.0), 1.0])
    barycentric = np.array(
        [1.0 / np.prod([points[a] - points[b] for b in range(5) if b != a]) for a in range(5)]
    )
    matrix = np.zeros((5, 5))
    for a in range(5):
        for b in range(5):
            if a != b:
                matrix[a, b] = barycentric[b] / barycentric[a] / (points[a] - points[b])
        matrix[a, a] = -np.sum(matrix[a])
    return matrix


MAT = derivative_matrix()


def derivative(u):
    e0, e1 = u[0] + u[4], u[1] + u[3]
    o0, o1 = u[0] - u[4], u[1] - u[3]
    mid = u[2] + u[2]
    e0, e1 = e0 - mid, e1 - mid
    out = [None] * 5
    for a in range(2):
        even = float(0.5 * (MAT[a, 0] + MAT[a, 4])) * e0 + float(0.5 * (MAT[a, 1] + MAT[a, 3])) * e1
        odd = float(0.5 * (MAT[a, 0] - MAT[a, 4])) * o0 + float(0.5 * (MAT[a, 1] - MAT[a, 3])) * o1
        out[a] = odd + even
        out[4 - a] = odd - even
    out[2] = float(MAT[2, 0]) * o0 + float(MAT[2, 1]) * o1
    return out


def sub_iota():
    return lax.broadcasted_iota(jnp.int32, (SUBS, LANES), 0)


def half_of():
    return sub_iota() >> 2


def swap_halves(x):
    return pltpu.roll(x, SUBS // 2, axis=0)


def lane_pick(x, idx):
    return jnp.take_along_axis(x, idx, axis=1, mode="promise_in_bounds")


def code_tile(codes_ref, face, slots):
    base = face * slots
    rows = []
    for h in range(2):
        at = base + h * LANES
        at = at if isinstance(at, int) else pl.multiple_of(at, LANES)
        rows.append(jnp.broadcast_to(codes_ref[0:1, pl.ds(at, LANES)], (SUBS, LANES)))
    first, second = rows
    return jnp.where(half_of() == 0, first, second)


def side_offset(axis, up):
    return up * FACE_OFF[2 * axis + 1]


def pack_side(state, list_ref, out, axis, up, slots):
    half = half_of()
    low = half == 0
    lane_group = lax.broadcasted_iota(jnp.int32, (SUBS, LANES), 1) >> 5
    masks = [lane_group == q for q in range(1, 4)]
    side = 2 * axis
    row = jnp.where(up > 0, list_ref[0, side + 1 : side + 2, :], list_ref[0, side : side + 1, :])
    listed = jnp.broadcast_to(jnp.concatenate([row] * 4, axis=1), (SUBS, LANES))
    idx = listed & (LANES - 1)
    here = (listed < slots) & ((listed >> 7) == half)
    start = side_offset(axis, up)

    def combine(parts):
        picked = [lane_pick(part, idx) for part in parts]
        groups = []
        for x in range(2):
            four = picked[4 * x : 4 * x + 4]
            tile = four[0]
            for q in range(1, len(four)):
                tile = jnp.where(masks[q - 1], four[q], tile)
            tile = jnp.where(here, tile, 0.0)
            groups.append(tile + swap_halves(tile))
        return jnp.where(low, groups[0], groups[1])

    for p in range(FACE):
        node = start + FACE_U[side] * (p // ORDER) + FACE_V[side] * (p % ORDER)
        out[p] = combine([state[k * NODES + node] for k in range(8)])
    for g in range(4):
        parts = []
        for w in range(8):
            p = min(8 * g + w, FACE - 1)
            node = start + FACE_U[side] * (p // ORDER) + FACE_V[side] * (p % ORDER)
            parts.append(state[8 * NODES + node])
        out[FACE + g] = combine(parts)


def correction(jumps, coef, direction, sign):
    lam, mu, buoy, speed = coef
    a, b, c = direction, (direction + 1) % 3, (direction + 2) % 3
    s_aa, s_bb, s_cc = 3 + a, 3 + b, 3 + c
    s_ab, s_ac, s_bc = 6 + c, 6 + b, 6 + a
    across = lam * jumps[a]
    flux = {
        a: buoy * jumps[s_aa],
        b: buoy * jumps[s_ab],
        c: buoy * jumps[s_ac],
        s_aa: across + (mu + mu) * jumps[a],
        s_bb: across,
        s_cc: across,
        s_ab: mu * jumps[b],
        s_ac: mu * jumps[c],
    }
    rows = []
    for k in range(FIELDS):
        total = speed * jumps[k]
        if k in flux:
            total = total + flux[k] if sign > 0 else total - flux[k]
        rows.append(total)
    return rows


def add_rows(acc, node, rows):
    for k in range(FIELDS):
        row = k * NODES + node
        acc[row] = acc[row] + rows[k]


def coefs(med, node):
    return [med[m * NODES + node] for m in range(4)]


def volume_pass(state, of_face, acc, med, products, average, scaled):
    lines = [of_face(face) for face in (0, 1)]

    def x_lines(j, carry, lines=lines):
        for line in lines:
            line(j)
        for k in range(5):
            for field, row in ((0, 3), (1, 8), (2, 7), (3, 0), (8, 1), (7, 2)):
                out = derivative([state[field * NODES + 25 * i + 5 * j + k] for i in range(5)])
                for i in range(5):
                    acc[row * NODES + 25 * i + 5 * j + k] = out[i]
        return carry

    lax.fori_loop(0, ORDER, x_lines, 0)

    lines = [of_face(face) for face in (2, 3)]

    def y_lines(i, carry, lines=lines):
        for line in lines:
            line(i)
        for k in range(5):
            for field, row, more in ((0, 8, 1), (1, 4, 0), (2, 6, 0), (8, 0, 1), (4, 1, 1), (6, 2, 1)):
                out = derivative([state[field * NODES + 25 * i + 5 * j + k] for j in range(5)])
                for j in range(5):
                    at = row * NODES + 25 * i + 5 * j + k
                    acc[at] = acc[at] + out[j] if more else out[j]
        return carry

    lax.fori_loop(0, ORDER, y_lines, 0)

    def z_line(first):
        parts = {}
        for field in (0, 1, 2, 7, 6, 5):
            parts[field] = derivative([state[field * NODES + first + k] for k in range(5)])
        for k in range(5):
            node = first + k
            lam, mu, buoy = (scaled(value) for value in coefs(med, node)[:3])
            old = [acc[row * NODES + node] for row in range(FIELDS) if row != 5]
            sdiv = [old[0] + parts[7][k], old[1] + parts[6][k], old[2] + parts[5][k]]
            g11, g22, g33 = old[3], old[4], parts[2][k]
            r23 = old[5] + parts[1][k]
            r13 = old[6] + parts[0][k]
            r12 = old[7]
            div = g11 + g22 + g33
            spread = lam * div
            mu2 = mu + mu
            volume = [buoy * s for s in sdiv]
            volume += [spread + mu2 * g for g in (g11, g22, g33)]
            volume += [mu * r for r in (r23, r13, r12)]
            own = [state[row * NODES + node] for row in range(FIELDS)]
            for row in range(FIELDS):
                acc[row * NODES + node] = average(own[row], row * NODES + node) + volume[row]
            dual = [pltpu.roll(x, SUBS - 2, axis=0) for x in own]
            pressure = div * (dual[3] + dual[4] + dual[5])
            normal = g11 * dual[3] + g22 * dual[4] + g33 * dual[5]
            shear = normal + normal + (r23 * dual[6] + r13 * dual[7] + r12 * dual[8])
            light = sdiv[0] * dual[0] + sdiv[1] * dual[1] + sdiv[2] * dual[2]
            for m, value in enumerate((pressure, shear, light)):
                products[pl.ds((m * LANES + node) * SUBS, SUBS), :] = value

    lines = [of_face(face) for face in (4, 5)]

    def z_lines(i, carry, lines=lines):
        for line in lines:
            line(i)
        for j in range(5):
            z_line(25 * i + 5 * j)
        return carry

    lax.fori_loop(0, ORDER, z_lines, 0)


def shot_sums(products, emit):
    for m in range(3):
        for g in range((NODES + 7) // 8):
            rows = min(8, NODES - 8 * g)
            base = (m * LANES + 8 * g) * SUBS
            for h in range(2):
                first = products[pl.ds(base + 4 * h, 8, stride=SUBS), :]
                second = products[pl.ds(base + 4 * h + 1, 8, stride=SUBS), :]
                emit(m, 8 * g, rows, h, (first + second)[:rows])


def face_jumps(state, jumps, codes_ref, slots, weight):
    half = half_of()
    free_code = 6 * slots + 4 * 32

    def of_face(face):
        codes = code_tile(codes_ref, face, slots)
        idx = codes & (LANES - 1)
        match = (codes >> 8) == (face ^ 1)
        same = match & (((codes >> 7) & 1) == half)
        cross = match & (((codes >> 7) & 1) != half)
        free = codes == free_code
        factor_v = jnp.where(free, 0.0, weight)
        factor_s = jnp.where(free, 2.0 * weight, weight)
        other = face ^ 1

        def line(u):
            for v in range(ORDER):
                shift = FACE_U[face] * u + FACE_V[face] * v
                for k in range(FIELDS):
                    there = state[k * NODES + FACE_OFF[other] + shift]
                    outer = jnp.where(same, lane_pick(there, idx), 0.0)
                    outer = jnp.where(cross, lane_pick(swap_halves(there), idx), outer)
                    jump = outer - state[k * NODES + FACE_OFF[face] + shift]
                    at = (face * FIELDS + k) * FACE + ORDER * u + v
                    jumps[at] = jump * (factor_v if k < 3 else factor_s)

        return line

    return of_face


def local_pass(jumps, acc, med):
    for node in range(NODES):
        place = (node // 25, node // 5 % 5, node % 5)
        total = None
        for axis in range(3):
            if place[axis] in (0, 4):
                face = 2 * axis + place[axis] // 4
                u, v = [place[n] for n in range(3) if n != axis]
                found = [jumps[(face * FIELDS + k) * FACE + ORDER * u + v] for k in range(FIELDS)]
                rows = correction(found, coefs(med, node), axis, 2 * (face % 2) - 1)
                total = rows if total is None else [x + y for x, y in zip(total, rows)]
        if total is not None:
            add_rows(acc, node, total)


def ghost_tiles(ghost, p, low):
    tile = ghost[p]
    turned = swap_halves(tile)
    tile9 = ghost[FACE + (p >> 3)]
    turned9 = swap_halves(tile9)
    chosen = half_of() == ((p >> 2) & 1)
    return jnp.where(low, tile, turned), jnp.where(low, turned, tile), jnp.where(chosen, tile9, turned9)


def ghost_pass(acc, med, codes_ref, ghost, axis, up, slots, scale):
    low = half_of() == 0
    face = 2 * axis + up
    sign = (2 * up - 1).astype(jnp.float32)
    codes = code_tile(codes_ref, face, slots) - (6 * slots + 32 * face)
    inside = (codes >= 0) & (codes < 32)
    weight = jnp.where(inside, scale, 0.0)
    idx = codes & 31
    shifted = [idx + 32 * q for q in range(4)]
    start = side_offset(axis, up)

    def body(u, carry):
        for v in range(ORDER):
            p = ORDER * u + v
            node = start + FACE_U[2 * axis] * u + FACE_V[2 * axis] * v
            first, second, nine = ghost_tiles(ghost, p, low)
            jumps = []
            for k in range(8):
                jumps.append(lane_pick(first if k < 4 else second, shifted[k % 4]) * weight)
            jumps.append(lane_pick(nine, idx + 32 * (p & 3)) * weight)
            lam, mu, buoy, speed = coefs(med, node)
            add_rows(acc, node, correction(jumps, (sign * lam, sign * mu, sign * buoy, speed), axis, 1))
        return carry

    lax.fori_loop(0, ORDER, body, 0, unroll=True)


def other_sources(state, acc, med, codes_ref, ghosts, ups, axes, outer, slots, scale):
    half = half_of()
    low = half == 0
    first_ghost = 6 * slots

    def codes_of(face):
        return code_tile(codes_ref, face, slots)

    left = jnp.zeros((SUBS, LANES), jnp.int32)
    for face in range(6):
        codes = codes_of(face)
        source = jnp.where(codes < first_ghost, codes >> 8, 6 + ((codes - first_ghost) >> 5))
        usual = (source == (face ^ 1)) | (source >= 10)
        if face < 4:
            usual = usual | (source == 6 + face)
        left = left | jnp.where(usual, 0, 1)
    remaining = jnp.max(left)

    @pl.when(remaining > 0)
    def _():
        def pair(t, carry):
            face, origin = t // 10, t % 10
            codes = code_tile(codes_ref, face, slots)
            source = jnp.where(codes < first_ghost, codes >> 8, 6 + ((codes - first_ghost) >> 5))
            mine = source == origin
            done = (origin == (face ^ 1)) | ((face < 4) & (origin == 6 + face))
            count = jnp.max(jnp.where(mine, 1, 0))

            @pl.when((count > 0) & jnp.logical_not(done))
            def _():
                weight = jnp.where(mine, scale, 0.0)
                axis, sign = face >> 1, (2 * (face & 1) - 1).astype(jnp.float32)

                def strides(which):
                    line = which >> 1
                    off = (which & 1) * jnp.where(line == 0, 100, jnp.where(line == 1, 20, 4))
                    return off, jnp.where(line == 0, 5, 25), jnp.where(line == 2, 5, 1)

                off, du, dv = strides(face)
                off2, du2, dv2 = strides(jnp.minimum(origin, 5))

                def at_node(p, carry):
                    u, v = p // ORDER, p % ORDER
                    node = off + du * u + dv * v

                    @pl.when(origin < 6)
                    def _():
                        there_node = off2 + du2 * u + dv2 * v
                        idx = codes & (LANES - 1)
                        same = ((codes >> 7) & 1) == half
                        for k in range(FIELDS):
                            there = state[k * NODES + there_node]
                            turned = swap_halves(there)
                            outer[k] = jnp.where(same, lane_pick(there, idx), lane_pick(turned, idx)) * weight

                    @pl.when(origin >= 6)
                    def _():
                        for k in range(FIELDS):
                            outer[k] = jnp.zeros((SUBS, LANES), jnp.float32)

                    for ghost, up, line in zip(ghosts, ups, axes):

                        @pl.when(origin == 6 + 2 * line + up)
                        def _(ghost=ghost):
                            idx = (codes - first_ghost) & 31
                            first, second, nine = ghost_tiles(ghost, p, low)
                            for k in range(8):
                                tile = first if k < 4 else second
                                outer[k] = lane_pick(tile, idx + 32 * (k % 4)) * weight
                            outer[8] = lane_pick(nine, idx + 32 * (p & 3)) * weight

                    lam, mu, buoy, speed = coefs(med, node)
                    a = axis
                    b, c = lax.rem(axis + 1, 3), lax.rem(axis + 2, 3)
                    across = lam * outer[a]
                    flux = (
                        (a, buoy * outer[3 + a]),
                        (b, buoy * outer[6 + c]),
                        (c, buoy * outer[6 + b]),
                        (3 + a, across + (mu + mu) * outer[a]),
                        (3 + b, across),
                        (3 + c, across),
                        (6 + c, mu * outer[b]),
                        (6 + b, mu * outer[c]),
                        (6 + a, None),
                    )
                    for k, value in flux:
                        row = k * NODES + node
                        total = speed * outer[k]
                        if value is not None:
                            total = total + sign * value
                        acc[row] = acc[row] + total
                    return carry

                lax.fori_loop(0, FACE, at_node, 0)

            return carry

        lax.fori_loop(0, 60, pair, 0)


def link_ups(place_ref, links):
    return [1 - ((lax.div(place_ref[0], stride) + parity) & 1) for _, stride, parity in links]


def load_kernel(slots, links, mat_hbm, fwd_hbm, adj_hbm, state_ref, med_ref, mat_ref, sems, mat_sem):
    mat_copy = pltpu.make_async_copy(mat_hbm, mat_ref, mat_sem)
    mat_copy.start()
    copies = []
    for k in range(FIELDS):
        span = pl.ds(k * NODES, NODES)
        for n, far in enumerate((fwd_hbm, adj_hbm)):
            copies.append(pltpu.make_async_copy(far.at[span], state_ref.at[span, :, n], sems.at[n, k]))
            copies[-1].start()
    mat_copy.wait()
    spread_material(mat_ref, med_ref)
    for copy in copies:
        copy.wait()


def pack_links(slots, links, place_ref, state_ref, list_ref, sends, line):
    ups = link_ups(place_ref, links)
    chosen = [n for n, link in enumerate(links) if link[0] == line]
    for n, send in zip(chosen, sends):
        pack_side(state_ref, list_ref, send, line, ups[n], slots)


def pack_kernel(line, slots, links, place_ref, state_ref, list_ref, *sends):
    pack_links(slots, links, place_ref, state_ref, list_ref, sends, line)


def late_pack_kernel(slots, links, place_ref, state_ref, list_ref, grad_ref, *sends):
    across = sum(link[0] == 0 for link in links)
    pack_links(slots, links, place_ref, state_ref, list_ref, sends[:across], 0)
    pack_links(slots, links, place_ref, state_ref, list_ref, sends[across:], 1)


def spread_material(mat_ref, med_ref):
    low = half_of() == 0
    for node in range(NODES):
        rows = []
        for m in range(3):
            first = jnp.broadcast_to(mat_ref[m, node : node + 1, 0:LANES], (SUBS, LANES))
            second = jnp.broadcast_to(mat_ref[m, node : node + 1, LANES : 2 * LANES], (SUBS, LANES))
            rows.append(jnp.where(low, first, second))
        lam, mu, buoy = rows
        speed = jnp.sqrt((lam + 2.0 * mu) * buoy)
        for m, value in enumerate((lam, mu, buoy, speed)):
            med_ref[m * NODES + node] = step_size * value


def first_kernel(slots, links, counts_ref, state_ref, med_ref, codes_ref, acc_ref, grad_ref, live_ref, products, jumps):
    lane = lax.broadcasted_iota(jnp.int32, (SUBS, LANES), 1)
    count = jnp.broadcast_to(counts_ref[...].reshape(1, 1), (SUBS, LANES))
    live_ref[...] = jnp.where(half_of() * LANES + lane < count, 1.0, 0.0)
    of_face = face_jumps(state_ref, jumps, codes_ref, slots, 0.5 * lift_weight)
    volume_pass(state_ref, of_face, acc_ref, med_ref, products, lambda own, row: own, lambda value: value)
    shot_sums(products, store_gradient(live_ref, [grad_ref], None))
    local_pass(jumps, acc_ref, med_ref)


def store_gradient(live_ref, grad_refs, earlier_ref):
    alive = [jnp.broadcast_to(live_ref[4 * h : 4 * h + 1, :], (SUBS, LANES)) > 0.0 for h in range(2)]

    def emit(m, start, rows, h, value):
        at = (m, slice(start, start + rows), slice(h * LANES, (h + 1) * LANES))
        if earlier_ref is not None:
            value = (0.5 * step_size) * (earlier_ref[at] + value)
        value = jnp.where(alive[h][:rows], value, 0.0)
        for grad_ref in grad_refs:
            size = grad_ref.shape[1]
            if 0 <= start < size:
                grad_ref[m, start : start + rows, h * LANES : (h + 1) * LANES] = value
            start -= size

    return emit


def ghost_stage(slots, links, ups, state_ref, acc_ref, med_ref, codes_ref, ghosts, outer, scale):
    axes = [link[0] for link in links]
    for axis, up, ghost in zip(axes, ups, ghosts):
        ghost_pass(acc_ref, med_ref, codes_ref, ghost, axis, up, slots, scale)
    other_sources(state_ref, acc_ref, med_ref, codes_ref, ghosts, ups, axes, outer, slots, scale)


def middle_kernel(slots, links, place_ref, acc_in, state_ref, med_ref, codes_ref, *rest):
    ghosts, (mid_ref, outer) = rest[: len(links)], rest[len(links) :]
    ups = link_ups(place_ref, links)
    ghost_stage(slots, links, ups, state_ref, mid_ref, med_ref, codes_ref, ghosts, outer, 0.5 * lift_weight)


def second_volume_kernel(
    slots, links, live_ref, mid_ref, state_ref, med_ref, codes_ref, first_ref, acc_ref, jumps, near_ref, far_ref, products
):
    share = 0.5 * live_ref[...]
    of_face = face_jumps(mid_ref, jumps, codes_ref, slots, (0.25 * lift_weight) * live_ref[...])
    volume_pass(
        mid_ref, of_face, acc_ref, med_ref, products,
        lambda own, row: share * (own + state_ref[row]), lambda value: share * value,
    )
    shot_sums(products, store_gradient(live_ref, [near_ref, far_ref], first_ref))


def second_faces_kernel(slots, links, acc_in, jumps, med_ref, acc_ref):
    local_pass(jumps, acc_ref, med_ref)


def second_ghosts_kernel(chosen, slots, links, place_ref, acc_in, med_ref, codes_ref, *rest):
    ghosts, acc_ref = rest[: len(chosen)], rest[-1]
    ups = link_ups(place_ref, links)
    for n, ghost in zip(chosen, ghosts):
        ghost_pass(acc_ref, med_ref, codes_ref, ghost, links[n][0], ups[n], slots, 0.25 * lift_weight)


def other_sources_kernel(slots, links, place_ref, acc_in, mid_ref, med_ref, codes_ref, *rest):
    ghosts, (acc_ref, outer) = rest[: len(links)], rest[len(links) :]
    ups = link_ups(place_ref, links)
    axes = [link[0] for link in links]
    other_sources(mid_ref, acc_ref, med_ref, codes_ref, ghosts, ups, axes, outer, slots, 0.25 * lift_weight)


def partial_kernel(slots, links, acc_in, a_ref, b_ref, near_ref, far_ref, acc_ref, first_ref, second_ref):
    first_ref[...] = a_ref[...] + near_ref[...]
    second_ref[...] = b_ref[...] + far_ref[...]


def total_kernel(slots, links, a_ref, b_ref, c_ref, d_ref, grad_ref):
    cut = a_ref.shape[1]
    grad_ref[:, :cut] = a_ref[...] + c_ref[...]
    grad_ref[:, cut:] = b_ref[...] + d_ref[...]


def store_kernel(slots, links, acc_ref, fwd_hbm, adj_hbm, sems):
    copies = []
    for k in range(FIELDS):
        span = pl.ds(k * NODES, NODES)
        for n, far in enumerate((fwd_hbm, adj_hbm)):
            copies.append(pltpu.make_async_copy(acc_ref.at[span, :, n], far.at[span], sems.at[n, k]))
            copies[-1].start()
    for copy in copies:
        copy.wait()


def tree_links(devices):
    links = []
    for axis, stride in ((0, DEV_Y), (1, 1)):
        for parity in range(2):
            pairs = [(d, d + stride) for d in range(devices - stride) if (d // stride) % 2 == parity]
            if pairs:
                links.append((axis, stride, parity, pairs + [(b, a) for a, b in pairs]))
    return links


def swapped(block, axis, distance):
    route = [(i, i ^ distance) for i in range(lax.axis_size(axis))]
    return lax.ppermute(block, axis, route)


def shards(forward, adjoint, material, counts, send_list, neighbours):
    shots, fields, nodes, slots = forward.shape
    halves = slots // LANES
    rows = fields * nodes
    assert 2 * shots * halves == SUBS and nodes == NODES and fields == FIELDS

    def dense(values):
        cut = values.reshape(shots, fields, nodes, halves, LANES)
        tiles = cut.transpose(1, 2, 3, 0, 4).reshape(rows, halves, shots, LANES)
        return pltpu.with_memory_space_constraint(tiles, pltpu.HBM)

    def restored(values):
        cut = values.reshape(fields, nodes, halves, shots, LANES)
        return cut.transpose(3, 0, 1, 2, 4).reshape(shots, fields, nodes, slots)

    links = tree_links(lax.axis_size("dom"))
    axes = tuple(link[:3] for link in links)
    place = lax.axis_index("dom").astype(jnp.int32).reshape(1)

    def exchange(sends, line):
        routes = [link[3] for link in links if link[0] == line]
        return [lax.ppermute(send, "dom", route) for send, route in zip(sends, routes)]

    vmem = pl.BlockSpec(memory_space=pltpu.VMEM)
    smem = pl.BlockSpec(memory_space=pltpu.SMEM)
    hbm = pl.BlockSpec(memory_space=pltpu.HBM)
    f32 = jnp.float32
    state_shape = pltpu.VMEM((rows, SUBS, LANES), f32)
    send_shape = pltpu.VMEM((FACE + 4, SUBS, LANES), f32)
    med_shape = pltpu.VMEM((4 * nodes, SUBS, LANES), f32)
    grad_shape = pltpu.VMEM(material.shape, f32)
    apart = (rows, halves, 2, shots, LANES)
    part_shape = jax.ShapeDtypeStruct((rows, halves, shots, LANES), f32)
    products = pltpu.VMEM((3 * LANES * SUBS, LANES), f32)
    outer = pltpu.VMEM((FIELDS, SUBS, LANES), f32)
    jumps_shape = pltpu.VMEM((6 * fields * FACE, SUBS, LANES), f32)
    field_sems = pltpu.SemaphoreType.DMA((2, FIELDS))

    def call(kernel, out_shape, in_specs, name, micros, scratch=(), out_specs=None, aliases=None):
        return pl.pallas_call(
            functools.partial(kernel, slots, axes),
            out_shape=out_shape,
            in_specs=in_specs,
            out_specs=out_specs or [vmem] * len(out_shape),
            scratch_shapes=list(scratch),
            input_output_aliases=aliases or {},
            compiler_params=pltpu.CompilerParams(vmem_limit_bytes=VMEM_BYTES),
            cost_estimate=pl.CostEstimate(flops=int(micros * 10**9), bytes_accessed=0, transcendentals=0),
            name=name,
        )

    count = len(links)
    state, med = call(
        load_kernel, [pltpu.VMEM(apart, f32), med_shape], [hbm] * 3, "load", 4,
        [pltpu.VMEM(material.shape, f32), field_sems, pltpu.SemaphoreType.DMA],
    )(
        pltpu.with_memory_space_constraint(material, pltpu.HBM), dense(forward), dense(adjoint),
    )
    state = state.reshape(rows, SUBS, LANES)
    by_line = [[send_shape for link in links if link[0] == line] for line in range(2)]
    across = len(by_line[0])
    ghosts = []
    for line in range(2):
        sends = call(functools.partial(pack_kernel, line), by_line[line], [smem, vmem, vmem], "pack", 0)(
            place, state, send_list
        )
        ghosts += exchange(sends, line)
    acc, grad_first, live = call(
        first_kernel, [state_shape, grad_shape, pltpu.VMEM((SUBS, LANES), f32)], [vmem] + [vmem] * 3, "first_section", 8, [products, jumps_shape]
    )(counts, state, med, neighbours)
    (mid,) = call(
        middle_kernel, [state_shape], [smem] + [vmem] * (4 + count), "first_ghosts", 4, [outer], aliases={1: 0}
    )(place, acc, state, med, neighbours, *ghosts)
    cut = (nodes // 2 + SUBS // 2) // SUBS * SUBS
    part_shapes = [pltpu.VMEM((3, size, slots), f32) for size in (cut, nodes - cut)]
    acc, jumps, *halved = call(
        second_volume_kernel, [state_shape, jumps_shape] + part_shapes, [vmem] * 6, "second_volume", 0, [products]
    )(live, mid, state, med, neighbours, grad_first)
    sends = call(late_pack_kernel, [send_shape] * count, [smem] + [vmem] * 3, "pack", 0.5)(
        place, mid, send_list, halved[0]
    )
    ghosts = exchange(sends[:across], 0) + exchange(sends[across:], 1)
    doubling = lax.axis_size("shot") == 4
    if doubling:
        pieces = [swapped(halved[0], "shot", 1), swapped(halved[1], "shot", 2)]
    (acc,) = call(
        second_faces_kernel, [state_shape], [vmem] * 3, "second_faces", 0.5, aliases={0: 0}
    )(acc, jumps, med)

    def add_ghosts(acc, chosen, micros):
        (acc,) = call(
            functools.partial(second_ghosts_kernel, chosen), [state_shape], [smem] + [vmem] * (3 + len(chosen)),
            "second_ghosts", micros, aliases={1: 0},
        )(place, acc, med, neighbours, *[ghosts[n] for n in chosen])
        return acc

    if doubling:
        acc, *parts = call(
            partial_kernel, [state_shape] + part_shapes, [vmem] * 5, "gradient_partial", 0, aliases={0: 0}
        )(acc, *halved, *pieces)
        pieces = [swapped(parts[0], "shot", 2), swapped(parts[1], "shot", 1)]
    else:
        gradient = lax.psum(jnp.concatenate(halved, axis=1), "shot")
    acc = add_ghosts(acc, range(count), 1)
    (acc,) = call(
        other_sources_kernel, [state_shape], [smem] + [vmem] * (4 + count), "other_sources", 0, [outer], aliases={1: 0}
    )(place, acc, mid, med, neighbours, *ghosts)
    fwd, adj = call(store_kernel, [part_shape, part_shape], [vmem], "store", 4, [field_sems], [hbm, hbm])(
        acc.reshape(apart)
    )
    if doubling:
        (gradient,) = call(
            total_kernel, [jax.ShapeDtypeStruct(material.shape, f32)], [vmem] * 4, "gradient_total", 0
        )(*parts, *pieces)
    return restored(fwd), restored(adj), gradient


def solution(mesh):
    placed = (
        P("shot", None, None, "dom"),
        P("shot", None, None, "dom"),
        P(None, None, "dom"),
        P("dom"),
        P("dom", None, None),
        P("dom", None),
    )
    return jax.shard_map(
        shards,
        mesh=mesh,
        in_specs=placed,
        out_specs=(
            P("shot", None, None, "dom"),
            P("shot", None, None, "dom"),
            P(None, None, "dom"),
        ),
        check_vma=False,
    )
```

```python
import functools

import jax
import jax.numpy as jnp
import numpy as np
from jax import lax
from jax.experimental import pallas as pl
from jax.experimental.pallas import tpu as pltpu
from jax.sharding import PartitionSpec as P

DEV_Y = 4
ORDER = 5
NODES = ORDER**3
FACE = ORDER * ORDER
FIELDS = 9
LANES = 128
SUBS = 8
step_size = 0.01
lift_weight = 10.0
VMEM_BYTES = 16 * 1024 * 1024

FACE_OFF = (0, 100, 0, 20, 0, 4)
FACE_U = (5, 5, 25, 25, 25, 25)
FACE_V = (1, 1, 1, 1, 5, 5)


def derivative_matrix():
    points = np.array([-1.0, -np.sqrt(3.0 / 7.0), 0.0, np.sqrt(3.0 / 7.0), 1.0])
    barycentric = np.array(
        [1.0 / np.prod([points[a] - points[b] for b in range(5) if b != a]) for a in range(5)]
    )
    matrix = np.zeros((5, 5))
    for a in range(5):
        for b in range(5):
            if a != b:
                matrix[a, b] = barycentric[b] / barycentric[a] / (points[a] - points[b])
        matrix[a, a] = -np.sum(matrix[a])
    return matrix


MAT = derivative_matrix()


def derivative(u):
    e0, e1 = u[0] + u[4], u[1] + u[3]
    o0, o1 = u[0] - u[4], u[1] - u[3]
    mid = u[2] + u[2]
    e0, e1 = e0 - mid, e1 - mid
    out = [None] * 5
    for a in range(2):
        even = float(0.5 * (MAT[a, 0] + MAT[a, 4])) * e0 + float(0.5 * (MAT[a, 1] + MAT[a, 3])) * e1
        odd = float(0.5 * (MAT[a, 0] - MAT[a, 4])) * o0 + float(0.5 * (MAT[a, 1] - MAT[a, 3])) * o1
        out[a] = odd + even
        out[4 - a] = odd - even
    out[2] = float(MAT[2, 0]) * o0 + float(MAT[2, 1]) * o1
    return out


def sub_iota():
    return lax.broadcasted_iota(jnp.int32, (SUBS, LANES), 0)


def half_of():
    return sub_iota() >> 2


def swap_halves(x):
    return pltpu.roll(x, SUBS // 2, axis=0)


def lane_pick(x, idx):
    return jnp.take_along_axis(x, idx, axis=1, mode="promise_in_bounds")


def code_tile(codes_ref, face, slots):
    base = face * slots
    rows = []
    for h in range(2):
        at = base + h * LANES
        at = at if isinstance(at, int) else pl.multiple_of(at, LANES)
        rows.append(jnp.broadcast_to(codes_ref[0:1, pl.ds(at, LANES)], (SUBS, LANES)))
    first, second = rows
    return jnp.where(half_of() == 0, first, second)


def side_offset(axis, up):
    return up * FACE_OFF[2 * axis + 1]


def pack_side(state, list_ref, out, axis, up, slots):
    half = half_of()
    low = half == 0
    lane_group = lax.broadcasted_iota(jnp.int32, (SUBS, LANES), 1) >> 5
    masks = [lane_group == q for q in range(1, 4)]
    side = 2 * axis
    row = jnp.where(up > 0, list_ref[0, side + 1 : side + 2, :], list_ref[0, side : side + 1, :])
    listed = jnp.broadcast_to(jnp.concatenate([row] * 4, axis=1), (SUBS, LANES))
    idx = listed & (LANES - 1)
    here = (listed < slots) & ((listed >> 7) == half)
    start = side_offset(axis, up)

    def combine(parts):
        picked = [lane_pick(part, idx) for part in parts]
        groups = []
        for x in range(2):
            four = picked[4 * x : 4 * x + 4]
            tile = four[0]
            for q in range(1, len(four)):
                tile = jnp.where(masks[q - 1], four[q], tile)
            tile = jnp.where(here, tile, 0.0)
            groups.append(tile + swap_halves(tile))
        return jnp.where(low, groups[0], groups[1])

    for p in range(FACE):
        node = start + FACE_U[side] * (p // ORDER) + FACE_V[side] * (p % ORDER)
        out[p] = combine([state[k * NODES + node] for k in range(8)])
    for g in range(4):
        parts = []
        for w in range(8):
            p = min(8 * g + w, FACE - 1)
            node = start + FACE_U[side] * (p // ORDER) + FACE_V[side] * (p % ORDER)
            parts.append(state[8 * NODES + node])
        out[FACE + g] = combine(parts)


def add_rows(acc, node, jumps, coef, direction, sign):
    lam, mu, buoy, speed = coef
    a, b, c = direction, (direction + 1) % 3, (direction + 2) % 3
    s_aa, s_bb, s_cc = 3 + a, 3 + b, 3 + c
    s_ab, s_ac, s_bc = 6 + c, 6 + b, 6 + a
    across = lam * jumps[a]
    flux = {
        a: buoy * jumps[s_aa],
        b: buoy * jumps[s_ab],
        c: buoy * jumps[s_ac],
        s_aa: across + (mu + mu) * jumps[a],
        s_bb: across,
        s_cc: across,
        s_ab: mu * jumps[b],
        s_ac: mu * jumps[c],
    }
    for k in range(FIELDS):
        row = k * NODES + node
        total = speed * jumps[k]
        if k in flux:
            total = total + flux[k] if sign > 0 else total - flux[k]
        acc[row] = acc[row] + total


def coefs(med, node):
    return [med[m * NODES + node] for m in range(4)]


def volume_pass(state, acc, med, products, average, scaled):
    def x_lines(j, carry):
        for k in range(5):
            for field, row in ((0, 3), (1, 8), (2, 7), (3, 0), (8, 1), (7, 2)):
                out = derivative([state[field * NODES + 25 * i + 5 * j + k] for i in range(5)])
                for i in range(5):
                    acc[row * NODES + 25 * i + 5 * j + k] = out[i]
        return carry

    lax.fori_loop(0, ORDER, x_lines, 0)

    def y_lines(i, carry):
        for k in range(5):
            for field, row, more in ((0, 8, 1), (1, 4, 0), (2, 6, 0), (8, 0, 1), (4, 1, 1), (6, 2, 1)):
                out = derivative([state[field * NODES + 25 * i + 5 * j + k] for j in range(5)])
                for j in range(5):
                    at = row * NODES + 25 * i + 5 * j + k
                    acc[at] = acc[at] + out[j] if more else out[j]
        return carry

    lax.fori_loop(0, ORDER, y_lines, 0)

    def z_line(first):
        parts = {}
        for field in (0, 1, 2, 7, 6, 5):
            parts[field] = derivative([state[field * NODES + first + k] for k in range(5)])
        for k in range(5):
            node = first + k
            lam, mu, buoy = (scaled(value) for value in coefs(med, node)[:3])
            old = [acc[row * NODES + node] for row in range(FIELDS) if row != 5]
            sdiv = [old[0] + parts[7][k], old[1] + parts[6][k], old[2] + parts[5][k]]
            g11, g22, g33 = old[3], old[4], parts[2][k]
            r23 = old[5] + parts[1][k]
            r13 = old[6] + parts[0][k]
            r12 = old[7]
            div = g11 + g22 + g33
            spread = lam * div
            mu2 = mu + mu
            volume = [buoy * s for s in sdiv]
            volume += [spread + mu2 * g for g in (g11, g22, g33)]
            volume += [mu * r for r in (r23, r13, r12)]
            own = [state[row * NODES + node] for row in range(FIELDS)]
            for row in range(FIELDS):
                acc[row * NODES + node] = average(own[row], row * NODES + node) + volume[row]
            dual = [pltpu.roll(x, SUBS - 2, axis=0) for x in own]
            pressure = div * (dual[3] + dual[4] + dual[5])
            normal = g11 * dual[3] + g22 * dual[4] + g33 * dual[5]
            shear = normal + normal + (r23 * dual[6] + r13 * dual[7] + r12 * dual[8])
            light = sdiv[0] * dual[0] + sdiv[1] * dual[1] + sdiv[2] * dual[2]
            for m, value in enumerate((pressure, shear, light)):
                products[pl.ds((m * LANES + node) * SUBS, SUBS), :] = value

    def z_lines(i, carry):
        for j in range(5):
            z_line(25 * i + 5 * j)
        return carry

    lax.fori_loop(0, ORDER, z_lines, 0)


def shot_sums(products, emit):
    for m in range(3):
        for g in range((NODES + 7) // 8):
            rows = min(8, NODES - 8 * g)
            base = (m * LANES + 8 * g) * SUBS
            for h in range(2):
                first = products[pl.ds(base + 4 * h, 8, stride=SUBS), :]
                second = products[pl.ds(base + 4 * h + 1, 8, stride=SUBS), :]
                emit(m, 8 * g, rows, h, (first + second)[:rows])


def local_pass(state, acc, med, codes_ref, slots, weight):
    half = half_of()
    low = half == 0
    free_code = 6 * slots + 4 * 32
    for face in range(6):
        codes = code_tile(codes_ref, face, slots)
        idx = codes & (LANES - 1)
        match = (codes >> 8) == (face ^ 1)
        same = match & (((codes >> 7) & 1) == half)
        cross = match & (((codes >> 7) & 1) != half)
        free = codes == free_code
        factor_v = jnp.where(free, 0.0, weight)
        factor_s = jnp.where(free, 2.0 * weight, weight)
        other = face ^ 1

        def body(u, carry, face=face, other=other, idx=idx, same=same, cross=cross,
                 factor_v=factor_v, factor_s=factor_s):
            for v in range(ORDER):
                shift = FACE_U[face] * u + FACE_V[face] * v
                node = FACE_OFF[face] + shift
                source = FACE_OFF[other] + shift
                jumps = []
                for k in range(FIELDS):
                    there = state[k * NODES + source]
                    outer = jnp.where(same, lane_pick(there, idx), 0.0)
                    outer = jnp.where(cross, lane_pick(swap_halves(there), idx), outer)
                    jump = outer - state[k * NODES + node]
                    jumps.append(jump * (factor_v if k < 3 else factor_s))
                add_rows(acc, node, jumps, coefs(med, node), face // 2, 2 * (face % 2) - 1)
            return carry

        lax.fori_loop(0, ORDER, body, 0, unroll=True)


def ghost_tiles(ghost, p, low):
    tile = ghost[p]
    turned = swap_halves(tile)
    tile9 = ghost[FACE + (p >> 3)]
    turned9 = swap_halves(tile9)
    chosen = half_of() == ((p >> 2) & 1)
    return jnp.where(low, tile, turned), jnp.where(low, turned, tile), jnp.where(chosen, tile9, turned9)


def ghost_pass(acc, med, codes_ref, ghost, axis, up, paired, slots, scale):
    low = half_of() == 0
    face = 2 * axis + up
    sign = (2 * up - 1).astype(jnp.float32)
    codes = code_tile(codes_ref, face, slots) - (6 * slots + 32 * face)
    inside = (codes >= 0) & (codes < 32)
    weight = jnp.where(inside, jnp.where(paired, scale, 0.0), 0.0)
    idx = codes & 31
    shifted = [idx + 32 * q for q in range(4)]
    start = side_offset(axis, up)

    def body(u, carry):
        for v in range(ORDER):
            p = ORDER * u + v
            node = start + FACE_U[2 * axis] * u + FACE_V[2 * axis] * v
            first, second, nine = ghost_tiles(ghost, p, low)
            jumps = []
            for k in range(8):
                jumps.append(lane_pick(first if k < 4 else second, shifted[k % 4]) * weight)
            jumps.append(lane_pick(nine, idx + 32 * (p & 3)) * weight)
            lam, mu, buoy, speed = coefs(med, node)
            add_rows(acc, node, jumps, (sign * lam, sign * mu, sign * buoy, speed), axis, 1)
        return carry

    lax.fori_loop(0, ORDER, body, 0, unroll=True)


def other_sources(state, acc, med, codes_ref, ghosts, ups, paired, axes, outer, slots, scale):
    half = half_of()
    low = half == 0
    first_ghost = 6 * slots

    def codes_of(face):
        return code_tile(codes_ref, face, slots)

    left = jnp.zeros((SUBS, LANES), jnp.int32)
    for face in range(6):
        codes = codes_of(face)
        source = jnp.where(codes < first_ghost, codes >> 8, 6 + ((codes - first_ghost) >> 5))
        usual = (source == (face ^ 1)) | (source >= 10)
        if face < 4:
            usual = usual | (source == 6 + face)
        left = left | jnp.where(usual, 0, 1)
    remaining = jnp.max(left)

    @pl.when(remaining > 0)
    def _():
        def pair(t, carry):
            face, origin = t // 10, t % 10
            codes = code_tile(codes_ref, face, slots)
            source = jnp.where(codes < first_ghost, codes >> 8, 6 + ((codes - first_ghost) >> 5))
            mine = source == origin
            done = (origin == (face ^ 1)) | ((face < 4) & (origin == 6 + face))
            count = jnp.max(jnp.where(mine, 1, 0))

            @pl.when((count > 0) & jnp.logical_not(done))
            def _():
                weight = jnp.where(mine, scale, 0.0)
                axis, sign = face >> 1, (2 * (face & 1) - 1).astype(jnp.float32)

                def strides(which):
                    line = which >> 1
                    off = (which & 1) * jnp.where(line == 0, 100, jnp.where(line == 1, 20, 4))
                    return off, jnp.where(line == 0, 5, 25), jnp.where(line == 2, 5, 1)

                off, du, dv = strides(face)
                off2, du2, dv2 = strides(jnp.minimum(origin, 5))

                def at_node(p, carry):
                    u, v = p // ORDER, p % ORDER
                    node = off + du * u + dv * v

                    @pl.when(origin < 6)
                    def _():
                        there_node = off2 + du2 * u + dv2 * v
                        idx = codes & (LANES - 1)
                        same = ((codes >> 7) & 1) == half
                        for k in range(FIELDS):
                            there = state[k * NODES + there_node]
                            turned = swap_halves(there)
                            outer[k] = jnp.where(same, lane_pick(there, idx), lane_pick(turned, idx)) * weight

                    @pl.when(origin >= 6)
                    def _():
                        for k in range(FIELDS):
                            outer[k] = jnp.zeros((SUBS, LANES), jnp.float32)

                    for ghost, up, pair_here, line in zip(ghosts, ups, paired, axes):

                        @pl.when((origin == 6 + 2 * line + up) & pair_here)
                        def _(ghost=ghost):
                            idx = (codes - first_ghost) & 31
                            first, second, nine = ghost_tiles(ghost, p, low)
                            for k in range(8):
                                tile = first if k < 4 else second
                                outer[k] = lane_pick(tile, idx + 32 * (k % 4)) * weight
                            outer[8] = lane_pick(nine, idx + 32 * (p & 3)) * weight

                    lam, mu, buoy, speed = coefs(med, node)
                    a = axis
                    b, c = lax.rem(axis + 1, 3), lax.rem(axis + 2, 3)
                    across = lam * outer[a]
                    flux = (
                        (a, buoy * outer[3 + a]),
                        (b, buoy * outer[6 + c]),
                        (c, buoy * outer[6 + b]),
                        (3 + a, across + (mu + mu) * outer[a]),
                        (3 + b, across),
                        (3 + c, across),
                        (6 + c, mu * outer[b]),
                        (6 + b, mu * outer[c]),
                        (6 + a, None),
                    )
                    for k, value in flux:
                        row = k * NODES + node
                        total = speed * outer[k]
                        if value is not None:
                            total = total + sign * value
                        acc[row] = acc[row] + total
                    return carry

                lax.fori_loop(0, FACE, at_node, 0)

            return carry

        lax.fori_loop(0, 60, pair, 0)


def link_ups(place_ref, links):
    return [1 - ((lax.div(place_ref[0], stride) + parity) & 1) for _, stride, parity, _ in links]


def link_paired(place_ref, links, ups):
    others = [place_ref[0] + (2 * up - 1) * link[1] for up, link in zip(ups, links)]
    return [(other >= 0) & (other < link[3]) for other, link in zip(others, links)]


def load_kernel(slots, links, mat_hbm, fwd_hbm, adj_hbm, state_ref, med_ref, mat_ref, sems, mat_sem):
    mat_copy = pltpu.make_async_copy(mat_hbm, mat_ref, mat_sem)
    mat_copy.start()
    copies = []
    for k in range(FIELDS):
        span = pl.ds(k * NODES, NODES)
        for n, far in enumerate((fwd_hbm, adj_hbm)):
            copies.append(pltpu.make_async_copy(far.at[span], state_ref.at[span, :, n], sems.at[n, k]))
            copies[-1].start()
    mat_copy.wait()
    spread_material(mat_ref, med_ref)
    for copy in copies:
        copy.wait()


def pack_links(slots, links, place_ref, state_ref, list_ref, sends, line):
    ups = link_ups(place_ref, links)
    chosen = [n for n, link in enumerate(links) if link[0] == line]
    for n, send in zip(chosen, sends):
        pack_side(state_ref, list_ref, send, line, ups[n], slots)


def pack_kernel(line, slots, links, place_ref, state_ref, list_ref, *sends):
    pack_links(slots, links, place_ref, state_ref, list_ref, sends, line)


def late_pack_kernel(slots, links, place_ref, state_ref, list_ref, grad_ref, *sends):
    across = sum(link[0] == 0 for link in links)
    pack_links(slots, links, place_ref, state_ref, list_ref, sends[:across], 0)
    pack_links(slots, links, place_ref, state_ref, list_ref, sends[across:], 1)


def spread_material(mat_ref, med_ref):
    low = half_of() == 0
    for node in range(NODES):
        rows = []
        for m in range(3):
            first = jnp.broadcast_to(mat_ref[m, node : node + 1, 0:LANES], (SUBS, LANES))
            second = jnp.broadcast_to(mat_ref[m, node : node + 1, LANES : 2 * LANES], (SUBS, LANES))
            rows.append(jnp.where(low, first, second))
        lam, mu, buoy = rows
        speed = jnp.sqrt((lam + 2.0 * mu) * buoy)
        for m, value in enumerate((lam, mu, buoy, speed)):
            med_ref[m * NODES + node] = step_size * value


def first_kernel(slots, links, counts_ref, state_ref, med_ref, codes_ref, acc_ref, grad_ref, live_ref, products):
    lane = lax.broadcasted_iota(jnp.int32, (SUBS, LANES), 1)
    count = jnp.broadcast_to(counts_ref[...].reshape(1, 1), (SUBS, LANES))
    live_ref[...] = jnp.where(half_of() * LANES + lane < count, 1.0, 0.0)
    volume_pass(state_ref, acc_ref, med_ref, products, lambda own, row: own, lambda value: value)
    shot_sums(products, store_gradient(live_ref, [grad_ref], None))
    local_pass(state_ref, acc_ref, med_ref, codes_ref, slots, 0.5 * lift_weight)


def store_gradient(live_ref, grad_refs, earlier_ref):
    alive = [jnp.broadcast_to(live_ref[4 * h : 4 * h + 1, :], (SUBS, LANES)) > 0.0 for h in range(2)]

    def emit(m, start, rows, h, value):
        at = (m, slice(start, start + rows), slice(h * LANES, (h + 1) * LANES))
        if earlier_ref is not None:
            value = (0.5 * step_size) * (earlier_ref[at] + value)
        value = jnp.where(alive[h][:rows], value, 0.0)
        for grad_ref in grad_refs:
            size = grad_ref.shape[1]
            if 0 <= start < size:
                grad_ref[m, start : start + rows, h * LANES : (h + 1) * LANES] = value
            start -= size

    return emit


def add_ghosts(links, place_ref, acc_ref, med_ref, codes_ref, ghosts, slots, scale):
    ups = link_ups(place_ref, links)
    paired = link_paired(place_ref, links, ups)
    for link, up, pair_here, ghost in zip(links, ups, paired, ghosts):
        ghost_pass(acc_ref, med_ref, codes_ref, ghost, link[0], up, pair_here, slots, scale)


def add_others(links, place_ref, state_ref, acc_ref, med_ref, codes_ref, ghosts, outer, slots, scale):
    ups = link_ups(place_ref, links)
    paired = link_paired(place_ref, links, ups)
    axes = [link[0] for link in links]
    other_sources(state_ref, acc_ref, med_ref, codes_ref, ghosts, ups, paired, axes, outer, slots, scale)


def middle_kernel(slots, links, place_ref, acc_in, state_ref, med_ref, codes_ref, *rest):
    ghosts, (mid_ref, outer) = rest[: len(links)], rest[len(links) :]
    add_ghosts(links, place_ref, mid_ref, med_ref, codes_ref, ghosts, slots, 0.5 * lift_weight)
    add_others(links, place_ref, state_ref, mid_ref, med_ref, codes_ref, ghosts, outer, slots, 0.5 * lift_weight)


def second_volume_kernel(
    slots, links, live_ref, mid_ref, state_ref, med_ref, first_ref, acc_ref, near_ref, far_ref, products
):
    share = 0.5 * live_ref[...]
    volume_pass(
        mid_ref, acc_ref, med_ref, products,
        lambda own, row: share * (own + state_ref[row]), lambda value: share * value,
    )
    shot_sums(products, store_gradient(live_ref, [near_ref, far_ref], first_ref))


def second_faces_kernel(slots, links, live_ref, acc_in, mid_ref, med_ref, codes_ref, acc_ref):
    weight = (0.25 * lift_weight) * live_ref[...]
    local_pass(mid_ref, acc_ref, med_ref, codes_ref, slots, weight)


def second_ghosts_kernel(slots, links, place_ref, acc_in, mid_ref, med_ref, codes_ref, *rest):
    ghosts, (acc_ref, outer) = rest[: len(links)], rest[len(links) :]
    add_ghosts(links, place_ref, acc_ref, med_ref, codes_ref, ghosts, slots, 0.25 * lift_weight)
    add_others(links, place_ref, mid_ref, acc_ref, med_ref, codes_ref, ghosts, outer, slots, 0.25 * lift_weight)


def partial_kernel(slots, links, acc_in, a_ref, b_ref, near_ref, far_ref, acc_ref, first_ref, second_ref):
    first_ref[...] = a_ref[...] + near_ref[...]
    second_ref[...] = b_ref[...] + far_ref[...]


def total_kernel(slots, links, a_ref, b_ref, c_ref, d_ref, grad_ref):
    cut = a_ref.shape[1]
    grad_ref[:, :cut] = a_ref[...] + c_ref[...]
    grad_ref[:, cut:] = b_ref[...] + d_ref[...]


def store_kernel(slots, links, acc_ref, fwd_hbm, adj_hbm, sems):
    copies = []
    for k in range(FIELDS):
        span = pl.ds(k * NODES, NODES)
        for n, far in enumerate((fwd_hbm, adj_hbm)):
            copies.append(pltpu.make_async_copy(acc_ref.at[span, :, n], far.at[span], sems.at[n, k]))
            copies[-1].start()
    for copy in copies:
        copy.wait()


def tree_links(devices):
    links = []
    for axis, stride in ((0, DEV_Y), (1, 1)):
        for parity in range(2):
            pairs = [(d, d + stride) for d in range(devices - stride) if (d // stride) % 2 == parity]
            if pairs:
                alone = set(range(devices)) - {d for pair in pairs for d in pair}
                route = pairs + [(b, a) for a, b in pairs] + [(d, d) for d in sorted(alone)]
                links.append((axis, stride, parity, devices, route))
    return links


def swapped(block, axis, distance):
    route = [(i, i ^ distance) for i in range(lax.axis_size(axis))]
    return lax.ppermute(block, axis, route)


def shards(forward, adjoint, material, counts, send_list, neighbours):
    shots, fields, nodes, slots = forward.shape
    halves = slots // LANES
    rows = fields * nodes
    assert 2 * shots * halves == SUBS and nodes == NODES and fields == FIELDS

    def dense(values):
        cut = values.reshape(shots, fields, nodes, halves, LANES)
        tiles = cut.transpose(1, 2, 3, 0, 4).reshape(rows, halves, shots, LANES)
        return pltpu.with_memory_space_constraint(tiles, pltpu.HBM)

    def restored(values):
        cut = values.reshape(fields, nodes, halves, shots, LANES)
        return cut.transpose(3, 0, 1, 2, 4).reshape(shots, fields, nodes, slots)

    links = tree_links(lax.axis_size("dom"))
    axes = tuple(link[:4] for link in links)
    place = lax.axis_index("dom").astype(jnp.int32).reshape(1)

    def exchange(sends, line):
        routes = [link[4] for link in links if link[0] == line]
        return [lax.ppermute(send, "dom", route) for send, route in zip(sends, routes)]

    vmem = pl.BlockSpec(memory_space=pltpu.VMEM)
    smem = pl.BlockSpec(memory_space=pltpu.SMEM)
    hbm = pl.BlockSpec(memory_space=pltpu.HBM)
    f32 = jnp.float32
    state_shape = pltpu.VMEM((rows, SUBS, LANES), f32)
    send_shape = pltpu.VMEM((FACE + 4, SUBS, LANES), f32)
    med_shape = pltpu.VMEM((4 * nodes, SUBS, LANES), f32)
    grad_shape = pltpu.VMEM(material.shape, f32)
    apart = (rows, halves, 2, shots, LANES)
    part_shape = jax.ShapeDtypeStruct((rows, halves, shots, LANES), f32)
    products = pltpu.VMEM((3 * LANES * SUBS, LANES), f32)
    outer = pltpu.VMEM((FIELDS, SUBS, LANES), f32)
    field_sems = pltpu.SemaphoreType.DMA((2, FIELDS))

    def call(kernel, out_shape, in_specs, name, micros, scratch=(), out_specs=None, aliases=None):
        return pl.pallas_call(
            functools.partial(kernel, slots, axes),
            out_shape=out_shape,
            in_specs=in_specs,
            out_specs=out_specs or [vmem] * len(out_shape),
            scratch_shapes=list(scratch),
            input_output_aliases=aliases or {},
            compiler_params=pltpu.CompilerParams(vmem_limit_bytes=VMEM_BYTES),
            cost_estimate=pl.CostEstimate(flops=int(micros * 10**9), bytes_accessed=0, transcendentals=0),
            name=name,
        )

    count = len(links)
    state, med = call(
        load_kernel, [pltpu.VMEM(apart, f32), med_shape], [hbm] * 3, "load", 4,
        [pltpu.VMEM(material.shape, f32), field_sems, pltpu.SemaphoreType.DMA],
    )(
        pltpu.with_memory_space_constraint(material, pltpu.HBM), dense(forward), dense(adjoint),
    )
    state = state.reshape(rows, SUBS, LANES)
    by_line = [[send_shape for link in links if link[0] == line] for line in range(2)]
    across = len(by_line[0])
    ghosts = []
    for line in range(2):
        sends = call(functools.partial(pack_kernel, line), by_line[line], [smem, vmem, vmem], "pack", 0)(
            place, state, send_list
        )
        ghosts += exchange(sends, line)
    acc, grad_first, live = call(
        first_kernel, [state_shape, grad_shape, pltpu.VMEM((SUBS, LANES), f32)], [vmem] + [vmem] * 3, "first_section", 8, [products]
    )(counts, state, med, neighbours)
    (mid,) = call(
        middle_kernel, [state_shape], [smem] + [vmem] * (4 + count), "first_ghosts", 4, [outer], aliases={1: 0}
    )(place, acc, state, med, neighbours, *ghosts)
    cut = (nodes // 2 + SUBS // 2) // SUBS * SUBS
    part_shapes = [pltpu.VMEM((3, size, slots), f32) for size in (cut, nodes - cut)]
    acc, *halved = call(
        second_volume_kernel, [state_shape] + part_shapes, [vmem] + [vmem] * 4, "second_volume", 0, [products]
    )(live, mid, state, med, grad_first)
    sends = call(late_pack_kernel, [send_shape] * count, [smem] + [vmem] * 3, "pack", 0.5)(
        place, mid, send_list, halved[0]
    )
    ghosts = exchange(sends[:across], 0) + exchange(sends[across:], 1)
    doubling = lax.axis_size("shot") == 4
    if doubling:
        pieces = [swapped(halved[0], "shot", 1), swapped(halved[1], "shot", 2)]
    (acc,) = call(
        second_faces_kernel, [state_shape], [vmem] * 5, "second_faces", 0.5, aliases={1: 0}
    )(live, acc, mid, med, neighbours)

    if doubling:
        acc, *parts = call(
            partial_kernel, [state_shape] + part_shapes, [vmem] * 5, "gradient_partial", 0, aliases={0: 0}
        )(acc, *halved, *pieces)
        pieces = [swapped(parts[0], "shot", 2), swapped(parts[1], "shot", 1)]
    else:
        gradient = lax.psum(jnp.concatenate(halved, axis=1), "shot")
    (acc,) = call(
        second_ghosts_kernel, [state_shape], [smem] + [vmem] * (4 + count), "second_ghosts", 1, [outer], aliases={1: 0}
    )(place, acc, mid, med, neighbours, *ghosts)
    fwd, adj = call(store_kernel, [part_shape, part_shape], [vmem], "store", 4, [field_sems], [hbm, hbm])(
        acc.reshape(apart)
    )
    if doubling:
        (gradient,) = call(
            total_kernel, [jax.ShapeDtypeStruct(material.shape, f32)], [vmem] * 4, "gradient_total", 0
        )(*parts, *pieces)
    return restored(fwd), restored(adj), gradient


def solution(mesh):
    placed = (
        P("shot", None, None, "dom"),
        P("shot", None, None, "dom"),
        P(None, None, "dom"),
        P("dom"),
        P("dom", None, None),
        P("dom", None),
    )
    return jax.shard_map(
        shards,
        mesh=mesh,
        in_specs=placed,
        out_specs=(
            P("shot", None, None, "dom"),
            P("shot", None, None, "dom"),
            P(None, None, "dom"),
        ),
        check_vma=False,
    )
```

```python
import functools

import jax
import jax.numpy as jnp
import numpy as np
from jax import lax
from jax.experimental import pallas as pl
from jax.experimental.pallas import tpu as pltpu
from jax.sharding import PartitionSpec as P

DEV_Y = 4
ORDER = 5
NODES = ORDER**3
FACE = ORDER * ORDER
FIELDS = 9
LANES = 128
SUBS = 8
step_size = 0.01
lift_weight = 10.0
VMEM_BYTES = 16 * 1024 * 1024

FACE_OFF = (0, 100, 0, 20, 0, 4)
FACE_U = (5, 5, 25, 25, 25, 25)
FACE_V = (1, 1, 1, 1, 5, 5)


def derivative_matrix():
    points = np.array([-1.0, -np.sqrt(3.0 / 7.0), 0.0, np.sqrt(3.0 / 7.0), 1.0])
    barycentric = np.array(
        [1.0 / np.prod([points[a] - points[b] for b in range(5) if b != a]) for a in range(5)]
    )
    matrix = np.zeros((5, 5))
    for a in range(5):
        for b in range(5):
            if a != b:
                matrix[a, b] = barycentric[b] / barycentric[a] / (points[a] - points[b])
        matrix[a, a] = -np.sum(matrix[a])
    return matrix


MAT = derivative_matrix()


def derivative(u):
    e0, e1 = u[0] + u[4], u[1] + u[3]
    o0, o1 = u[0] - u[4], u[1] - u[3]
    mid = u[2] + u[2]
    e0, e1 = e0 - mid, e1 - mid
    out = [None] * 5
    for a in range(2):
        even = float(0.5 * (MAT[a, 0] + MAT[a, 4])) * e0 + float(0.5 * (MAT[a, 1] + MAT[a, 3])) * e1
        odd = float(0.5 * (MAT[a, 0] - MAT[a, 4])) * o0 + float(0.5 * (MAT[a, 1] - MAT[a, 3])) * o1
        out[a] = odd + even
        out[4 - a] = odd - even
    out[2] = float(MAT[2, 0]) * o0 + float(MAT[2, 1]) * o1
    return out


def sub_iota():
    return lax.broadcasted_iota(jnp.int32, (SUBS, LANES), 0)


def half_of():
    return sub_iota() >> 2


def swap_halves(x):
    return pltpu.roll(x, SUBS // 2, axis=0)


def lane_pick(x, idx):
    return jnp.take_along_axis(x, idx, axis=1, mode="promise_in_bounds")


def code_tile(codes_ref, face, slots):
    base = face * slots
    rows = []
    for h in range(2):
        at = base + h * LANES
        at = at if isinstance(at, int) else pl.multiple_of(at, LANES)
        rows.append(jnp.broadcast_to(codes_ref[0:1, pl.ds(at, LANES)], (SUBS, LANES)))
    first, second = rows
    return jnp.where(half_of() == 0, first, second)


def side_offset(axis, up):
    return up * FACE_OFF[2 * axis + 1]


def pack_side(state, list_ref, out, axis, up, slots):
    half = half_of()
    low = half == 0
    lane_group = lax.broadcasted_iota(jnp.int32, (SUBS, LANES), 1) >> 5
    masks = [lane_group == q for q in range(1, 4)]
    side = 2 * axis
    row = jnp.where(up > 0, list_ref[0, side + 1 : side + 2, :], list_ref[0, side : side + 1, :])
    listed = jnp.broadcast_to(jnp.concatenate([row] * 4, axis=1), (SUBS, LANES))
    idx = listed & (LANES - 1)
    here = (listed < slots) & ((listed >> 7) == half)
    start = side_offset(axis, up)

    def combine(parts):
        picked = [lane_pick(part, idx) for part in parts]
        groups = []
        for x in range(2):
            four = picked[4 * x : 4 * x + 4]
            tile = four[0]
            for q in range(1, len(four)):
                tile = jnp.where(masks[q - 1], four[q], tile)
            tile = jnp.where(here, tile, 0.0)
            groups.append(tile + swap_halves(tile))
        return jnp.where(low, groups[0], groups[1])

    for p in range(FACE):
        node = start + FACE_U[side] * (p // ORDER) + FACE_V[side] * (p % ORDER)
        out[p] = combine([state[k * NODES + node] for k in range(8)])
    for g in range(4):
        parts = []
        for w in range(8):
            p = min(8 * g + w, FACE - 1)
            node = start + FACE_U[side] * (p // ORDER) + FACE_V[side] * (p % ORDER)
            parts.append(state[8 * NODES + node])
        out[FACE + g] = combine(parts)


def add_rows(acc, node, jumps, coef, direction, sign):
    lam, mu, buoy, speed = coef
    a, b, c = direction, (direction + 1) % 3, (direction + 2) % 3
    s_aa, s_bb, s_cc = 3 + a, 3 + b, 3 + c
    s_ab, s_ac, s_bc = 6 + c, 6 + b, 6 + a
    across = lam * jumps[a]
    flux = {
        a: buoy * jumps[s_aa],
        b: buoy * jumps[s_ab],
        c: buoy * jumps[s_ac],
        s_aa: across + (mu + mu) * jumps[a],
        s_bb: across,
        s_cc: across,
        s_ab: mu * jumps[b],
        s_ac: mu * jumps[c],
    }
    for k in range(FIELDS):
        row = k * NODES + node
        total = speed * jumps[k]
        if k in flux:
            total = total + flux[k] if sign > 0 else total - flux[k]
        acc[row] = acc[row] + total


def coefs(med, node):
    return [med[m * NODES + node] for m in range(4)]


def volume_pass(state, acc, med, products, average, scaled):
    def x_lines(j, carry):
        for k in range(5):
            for field, row in ((0, 3), (1, 8), (2, 7), (3, 0), (8, 1), (7, 2)):
                out = derivative([state[field * NODES + 25 * i + 5 * j + k] for i in range(5)])
                for i in range(5):
                    acc[row * NODES + 25 * i + 5 * j + k] = out[i]
        return carry

    lax.fori_loop(0, ORDER, x_lines, 0)

    def y_lines(i, carry):
        for k in range(5):
            for field, row, more in ((0, 8, 1), (1, 4, 0), (2, 6, 0), (8, 0, 1), (4, 1, 1), (6, 2, 1)):
                out = derivative([state[field * NODES + 25 * i + 5 * j + k] for j in range(5)])
                for j in range(5):
                    at = row * NODES + 25 * i + 5 * j + k
                    acc[at] = acc[at] + out[j] if more else out[j]
        return carry

    lax.fori_loop(0, ORDER, y_lines, 0)

    def z_line(first):
        parts = {}
        for field in (0, 1, 2, 7, 6, 5):
            parts[field] = derivative([state[field * NODES + first + k] for k in range(5)])
        for k in range(5):
            node = first + k
            lam, mu, buoy = (scaled(value) for value in coefs(med, node)[:3])
            old = [acc[row * NODES + node] for row in range(FIELDS) if row != 5]
            sdiv = [old[0] + parts[7][k], old[1] + parts[6][k], old[2] + parts[5][k]]
            g11, g22, g33 = old[3], old[4], parts[2][k]
            r23 = old[5] + parts[1][k]
            r13 = old[6] + parts[0][k]
            r12 = old[7]
            div = g11 + g22 + g33
            spread = lam * div
            mu2 = mu + mu
            volume = [buoy * s for s in sdiv]
            volume += [spread + mu2 * g for g in (g11, g22, g33)]
            volume += [mu * r for r in (r23, r13, r12)]
            own = [state[row * NODES + node] for row in range(FIELDS)]
            for row in range(FIELDS):
                acc[row * NODES + node] = average(own[row], row * NODES + node) + volume[row]
            dual = [pltpu.roll(x, SUBS - 2, axis=0) for x in own]
            pressure = div * (dual[3] + dual[4] + dual[5])
            normal = g11 * dual[3] + g22 * dual[4] + g33 * dual[5]
            shear = normal + normal + (r23 * dual[6] + r13 * dual[7] + r12 * dual[8])
            light = sdiv[0] * dual[0] + sdiv[1] * dual[1] + sdiv[2] * dual[2]
            for m, value in enumerate((pressure, shear, light)):
                products[pl.ds((m * LANES + node) * SUBS, SUBS), :] = value

    def z_lines(i, carry):
        for j in range(5):
            z_line(25 * i + 5 * j)
        return carry

    lax.fori_loop(0, ORDER, z_lines, 0)


def shot_sums(products, emit):
    for m in range(3):
        for g in range((NODES + 7) // 8):
            rows = min(8, NODES - 8 * g)
            base = (m * LANES + 8 * g) * SUBS
            for h in range(2):
                first = products[pl.ds(base + 4 * h, 8, stride=SUBS), :]
                second = products[pl.ds(base + 4 * h + 1, 8, stride=SUBS), :]
                emit(m, 8 * g, rows, h, (first + second)[:rows])


def local_pass(state, acc, med, codes_ref, slots, weight):
    half = half_of()
    low = half == 0
    free_code = 6 * slots + 4 * 32
    for face in range(6):
        codes = code_tile(codes_ref, face, slots)
        idx = codes & (LANES - 1)
        match = (codes >> 8) == (face ^ 1)
        same = match & (((codes >> 7) & 1) == half)
        cross = match & (((codes >> 7) & 1) != half)
        free = codes == free_code
        factor_v = jnp.where(free, 0.0, weight)
        factor_s = jnp.where(free, 2.0 * weight, weight)
        other = face ^ 1

        def body(u, carry, face=face, other=other, idx=idx, same=same, cross=cross,
                 factor_v=factor_v, factor_s=factor_s):
            for v in range(ORDER):
                shift = FACE_U[face] * u + FACE_V[face] * v
                node = FACE_OFF[face] + shift
                source = FACE_OFF[other] + shift
                jumps = []
                for k in range(FIELDS):
                    there = state[k * NODES + source]
                    outer = jnp.where(same, lane_pick(there, idx), 0.0)
                    outer = jnp.where(cross, lane_pick(swap_halves(there), idx), outer)
                    jump = outer - state[k * NODES + node]
                    jumps.append(jump * (factor_v if k < 3 else factor_s))
                add_rows(acc, node, jumps, coefs(med, node), face // 2, 2 * (face % 2) - 1)
            return carry

        lax.fori_loop(0, ORDER, body, 0, unroll=True)


def ghost_tiles(ghost, p, low):
    tile = ghost[p]
    turned = swap_halves(tile)
    tile9 = ghost[FACE + (p >> 3)]
    turned9 = swap_halves(tile9)
    chosen = half_of() == ((p >> 2) & 1)
    return jnp.where(low, tile, turned), jnp.where(low, turned, tile), jnp.where(chosen, tile9, turned9)


def ghost_pass(acc, med, codes_ref, ghost, axis, up, paired, slots, scale):
    low = half_of() == 0
    face = 2 * axis + up
    sign = (2 * up - 1).astype(jnp.float32)
    codes = code_tile(codes_ref, face, slots) - (6 * slots + 32 * face)
    inside = (codes >= 0) & (codes < 32)
    weight = jnp.where(inside, jnp.where(paired, scale, 0.0), 0.0)
    idx = codes & 31
    shifted = [idx + 32 * q for q in range(4)]
    start = side_offset(axis, up)

    def body(u, carry):
        for v in range(ORDER):
            p = ORDER * u + v
            node = start + FACE_U[2 * axis] * u + FACE_V[2 * axis] * v
            first, second, nine = ghost_tiles(ghost, p, low)
            jumps = []
            for k in range(8):
                jumps.append(lane_pick(first if k < 4 else second, shifted[k % 4]) * weight)
            jumps.append(lane_pick(nine, idx + 32 * (p & 3)) * weight)
            lam, mu, buoy, speed = coefs(med, node)
            add_rows(acc, node, jumps, (sign * lam, sign * mu, sign * buoy, speed), axis, 1)
        return carry

    lax.fori_loop(0, ORDER, body, 0, unroll=True)


def other_sources(state, acc, med, codes_ref, ghosts, ups, paired, axes, outer, slots, scale):
    half = half_of()
    low = half == 0
    first_ghost = 6 * slots

    def codes_of(face):
        return code_tile(codes_ref, face, slots)

    left = jnp.zeros((SUBS, LANES), jnp.int32)
    for face in range(6):
        codes = codes_of(face)
        source = jnp.where(codes < first_ghost, codes >> 8, 6 + ((codes - first_ghost) >> 5))
        usual = (source == (face ^ 1)) | (source >= 10)
        if face < 4:
            usual = usual | (source == 6 + face)
        left = left | jnp.where(usual, 0, 1)
    remaining = jnp.max(left)

    @pl.when(remaining > 0)
    def _():
        def pair(t, carry):
            face, origin = t // 10, t % 10
            codes = code_tile(codes_ref, face, slots)
            source = jnp.where(codes < first_ghost, codes >> 8, 6 + ((codes - first_ghost) >> 5))
            mine = source == origin
            done = (origin == (face ^ 1)) | ((face < 4) & (origin == 6 + face))
            count = jnp.max(jnp.where(mine, 1, 0))

            @pl.when((count > 0) & jnp.logical_not(done))
            def _():
                weight = jnp.where(mine, scale, 0.0)
                axis, sign = face >> 1, (2 * (face & 1) - 1).astype(jnp.float32)

                def strides(which):
                    line = which >> 1
                    off = (which & 1) * jnp.where(line == 0, 100, jnp.where(line == 1, 20, 4))
                    return off, jnp.where(line == 0, 5, 25), jnp.where(line == 2, 5, 1)

                off, du, dv = strides(face)
                off2, du2, dv2 = strides(jnp.minimum(origin, 5))

                def at_node(p, carry):
                    u, v = p // ORDER, p % ORDER
                    node = off + du * u + dv * v

                    @pl.when(origin < 6)
                    def _():
                        there_node = off2 + du2 * u + dv2 * v
                        idx = codes & (LANES - 1)
                        same = ((codes >> 7) & 1) == half
                        for k in range(FIELDS):
                            there = state[k * NODES + there_node]
                            turned = swap_halves(there)
                            outer[k] = jnp.where(same, lane_pick(there, idx), lane_pick(turned, idx)) * weight

                    @pl.when(origin >= 6)
                    def _():
                        for k in range(FIELDS):
                            outer[k] = jnp.zeros((SUBS, LANES), jnp.float32)

                    for ghost, up, pair_here, line in zip(ghosts, ups, paired, axes):

                        @pl.when((origin == 6 + 2 * line + up) & pair_here)
                        def _(ghost=ghost):
                            idx = (codes - first_ghost) & 31
                            first, second, nine = ghost_tiles(ghost, p, low)
                            for k in range(8):
                                tile = first if k < 4 else second
                                outer[k] = lane_pick(tile, idx + 32 * (k % 4)) * weight
                            outer[8] = lane_pick(nine, idx + 32 * (p & 3)) * weight

                    lam, mu, buoy, speed = coefs(med, node)
                    a = axis
                    b, c = lax.rem(axis + 1, 3), lax.rem(axis + 2, 3)
                    across = lam * outer[a]
                    flux = (
                        (a, buoy * outer[3 + a]),
                        (b, buoy * outer[6 + c]),
                        (c, buoy * outer[6 + b]),
                        (3 + a, across + (mu + mu) * outer[a]),
                        (3 + b, across),
                        (3 + c, across),
                        (6 + c, mu * outer[b]),
                        (6 + b, mu * outer[c]),
                        (6 + a, None),
                    )
                    for k, value in flux:
                        row = k * NODES + node
                        total = speed * outer[k]
                        if value is not None:
                            total = total + sign * value
                        acc[row] = acc[row] + total
                    return carry

                lax.fori_loop(0, FACE, at_node, 0)

            return carry

        lax.fori_loop(0, 60, pair, 0)


def link_ups(place_ref, links):
    return [1 - ((lax.div(place_ref[0], stride) + parity) & 1) for _, stride, parity, _ in links]


def link_paired(place_ref, links, ups):
    others = [place_ref[0] + (2 * up - 1) * link[1] for up, link in zip(ups, links)]
    return [(other >= 0) & (other < link[3]) for other, link in zip(others, links)]


def load_kernel(slots, links, mat_hbm, fwd_hbm, adj_hbm, state_ref, med_ref, mat_ref, sems, mat_sem):
    mat_copy = pltpu.make_async_copy(mat_hbm, mat_ref, mat_sem)
    mat_copy.start()
    copies = []
    for k in range(FIELDS):
        span = pl.ds(k * NODES, NODES)
        for n, far in enumerate((fwd_hbm, adj_hbm)):
            copies.append(pltpu.make_async_copy(far.at[span], state_ref.at[span, :, n], sems.at[n, k]))
            copies[-1].start()
    mat_copy.wait()
    spread_material(mat_ref, med_ref)
    for copy in copies:
        copy.wait()


def pack_links(slots, links, place_ref, state_ref, list_ref, sends, line):
    ups = link_ups(place_ref, links)
    chosen = [n for n, link in enumerate(links) if link[0] == line]
    for n, send in zip(chosen, sends):
        pack_side(state_ref, list_ref, send, line, ups[n], slots)


def pack_kernel(line, slots, links, place_ref, state_ref, list_ref, *sends):
    pack_links(slots, links, place_ref, state_ref, list_ref, sends, line)


def late_pack_kernel(slots, links, place_ref, state_ref, list_ref, grad_ref, *sends):
    across = sum(link[0] == 0 for link in links)
    pack_links(slots, links, place_ref, state_ref, list_ref, sends[:across], 0)
    pack_links(slots, links, place_ref, state_ref, list_ref, sends[across:], 1)


def spread_material(mat_ref, med_ref):
    low = half_of() == 0
    for node in range(NODES):
        rows = []
        for m in range(3):
            first = jnp.broadcast_to(mat_ref[m, node : node + 1, 0:LANES], (SUBS, LANES))
            second = jnp.broadcast_to(mat_ref[m, node : node + 1, LANES : 2 * LANES], (SUBS, LANES))
            rows.append(jnp.where(low, first, second))
        lam, mu, buoy = rows
        speed = jnp.sqrt((lam + 2.0 * mu) * buoy)
        for m, value in enumerate((lam, mu, buoy, speed)):
            med_ref[m * NODES + node] = step_size * value


def first_kernel(slots, links, counts_ref, state_ref, med_ref, codes_ref, acc_ref, grad_ref, live_ref, products):
    lane = lax.broadcasted_iota(jnp.int32, (SUBS, LANES), 1)
    count = jnp.broadcast_to(counts_ref[...].reshape(1, 1), (SUBS, LANES))
    live_ref[...] = jnp.where(half_of() * LANES + lane < count, 1.0, 0.0)
    volume_pass(state_ref, acc_ref, med_ref, products, lambda own, row: own, lambda value: value)
    shot_sums(products, store_gradient(live_ref, [grad_ref], None))
    local_pass(state_ref, acc_ref, med_ref, codes_ref, slots, 0.5 * lift_weight)


def store_gradient(live_ref, grad_refs, earlier_ref):
    alive = [jnp.broadcast_to(live_ref[4 * h : 4 * h + 1, :], (SUBS, LANES)) > 0.0 for h in range(2)]

    def emit(m, start, rows, h, value):
        at = (m, slice(start, start + rows), slice(h * LANES, (h + 1) * LANES))
        if earlier_ref is not None:
            value = (0.5 * step_size) * (earlier_ref[at] + value)
        value = jnp.where(alive[h][:rows], value, 0.0)
        for grad_ref in grad_refs:
            size = grad_ref.shape[1]
            if 0 <= start < size:
                grad_ref[m, start : start + rows, h * LANES : (h + 1) * LANES] = value
            start -= size

    return emit


def add_ghosts(links, place_ref, acc_ref, med_ref, codes_ref, ghosts, slots, scale):
    ups = link_ups(place_ref, links)
    paired = link_paired(place_ref, links, ups)
    for link, up, pair_here, ghost in zip(links, ups, paired, ghosts):
        ghost_pass(acc_ref, med_ref, codes_ref, ghost, link[0], up, pair_here, slots, scale)


def add_others(links, place_ref, state_ref, acc_ref, med_ref, codes_ref, ghosts, outer, slots, scale):
    ups = link_ups(place_ref, links)
    paired = link_paired(place_ref, links, ups)
    axes = [link[0] for link in links]
    other_sources(state_ref, acc_ref, med_ref, codes_ref, ghosts, ups, paired, axes, outer, slots, scale)


def middle_kernel(slots, links, place_ref, acc_in, state_ref, med_ref, codes_ref, *rest):
    ghosts, (mid_ref, outer) = rest[: len(links)], rest[len(links) :]
    add_ghosts(links, place_ref, mid_ref, med_ref, codes_ref, ghosts, slots, 0.5 * lift_weight)
    add_others(links, place_ref, state_ref, mid_ref, med_ref, codes_ref, ghosts, outer, slots, 0.5 * lift_weight)


def second_volume_kernel(
    slots, links, live_ref, mid_ref, state_ref, med_ref, first_ref, acc_ref, near_ref, far_ref, products
):
    share = 0.5 * live_ref[...]
    volume_pass(
        mid_ref, acc_ref, med_ref, products,
        lambda own, row: share * (own + state_ref[row]), lambda value: share * value,
    )
    shot_sums(products, store_gradient(live_ref, [near_ref, far_ref], first_ref))


def second_faces_kernel(slots, links, live_ref, acc_in, mid_ref, med_ref, codes_ref, acc_ref):
    weight = (0.25 * lift_weight) * live_ref[...]
    local_pass(mid_ref, acc_ref, med_ref, codes_ref, slots, weight)


def second_ghosts_kernel(slots, links, place_ref, acc_in, mid_ref, med_ref, codes_ref, *rest):
    ghosts, (acc_ref, outer) = rest[: len(links)], rest[len(links) :]
    add_ghosts(links, place_ref, acc_ref, med_ref, codes_ref, ghosts, slots, 0.25 * lift_weight)
    add_others(links, place_ref, mid_ref, acc_ref, med_ref, codes_ref, ghosts, outer, slots, 0.25 * lift_weight)


def partial_kernel(slots, links, acc_in, a_ref, b_ref, near_ref, far_ref, acc_ref, first_ref, second_ref):
    first_ref[...] = a_ref[...] + near_ref[...]
    second_ref[...] = b_ref[...] + far_ref[...]


def total_kernel(slots, links, a_ref, b_ref, c_ref, d_ref, grad_ref):
    cut = a_ref.shape[1]
    grad_ref[:, :cut] = a_ref[...] + c_ref[...]
    grad_ref[:, cut:] = b_ref[...] + d_ref[...]


def store_kernel(slots, links, acc_ref, fwd_hbm, adj_hbm, sems):
    copies = []
    for k in range(FIELDS):
        span = pl.ds(k * NODES, NODES)
        for n, far in enumerate((fwd_hbm, adj_hbm)):
            copies.append(pltpu.make_async_copy(acc_ref.at[span, :, n], far.at[span], sems.at[n, k]))
            copies[-1].start()
    for copy in copies:
        copy.wait()


def tree_links(devices):
    links = []
    for axis, stride in ((0, DEV_Y), (1, 1)):
        for parity in range(2):
            pairs = [(d, d + stride) for d in range(devices - stride) if (d // stride) % 2 == parity]
            if pairs:
                alone = set(range(devices)) - {d for pair in pairs for d in pair}
                route = pairs + [(b, a) for a, b in pairs] + [(d, d) for d in sorted(alone)]
                links.append((axis, stride, parity, devices, route))
    return links


def swapped(block, axis, distance):
    route = [(i, i ^ distance) for i in range(lax.axis_size(axis))]
    return lax.ppermute(block, axis, route)


def shards(forward, adjoint, material, counts, send_list, neighbours):
    shots, fields, nodes, slots = forward.shape
    halves = slots // LANES
    rows = fields * nodes
    assert 2 * shots * halves == SUBS and nodes == NODES and fields == FIELDS

    def dense(values):
        cut = values.reshape(shots, fields, nodes, halves, LANES)
        tiles = cut.transpose(1, 2, 3, 0, 4).reshape(rows, halves, shots, LANES)
        return pltpu.with_memory_space_constraint(tiles, pltpu.HBM)

    def restored(values):
        cut = values.reshape(fields, nodes, halves, shots, LANES)
        return cut.transpose(3, 0, 1, 2, 4).reshape(shots, fields, nodes, slots)

    links = tree_links(lax.axis_size("dom"))
    axes = tuple(link[:4] for link in links)
    place = lax.axis_index("dom").astype(jnp.int32).reshape(1)

    def exchange(sends, line):
        routes = [link[4] for link in links if link[0] == line]
        return [lax.ppermute(send, "dom", route) for send, route in zip(sends, routes)]

    vmem = pl.BlockSpec(memory_space=pltpu.VMEM)
    smem = pl.BlockSpec(memory_space=pltpu.SMEM)
    hbm = pl.BlockSpec(memory_space=pltpu.HBM)
    f32 = jnp.float32
    state_shape = pltpu.VMEM((rows, SUBS, LANES), f32)
    send_shape = pltpu.VMEM((FACE + 4, SUBS, LANES), f32)
    med_shape = pltpu.VMEM((4 * nodes, SUBS, LANES), f32)
    grad_shape = pltpu.VMEM(material.shape, f32)
    apart = (rows, halves, 2, shots, LANES)
    part_shape = jax.ShapeDtypeStruct((rows, halves, shots, LANES), f32)
    products = pltpu.VMEM((3 * LANES * SUBS, LANES), f32)
    outer = pltpu.VMEM((FIELDS, SUBS, LANES), f32)
    field_sems = pltpu.SemaphoreType.DMA((2, FIELDS))

    def call(kernel, out_shape, in_specs, name, micros, scratch=(), out_specs=None, aliases=None):
        return pl.pallas_call(
            functools.partial(kernel, slots, axes),
            out_shape=out_shape,
            in_specs=in_specs,
            out_specs=out_specs or [vmem] * len(out_shape),
            scratch_shapes=list(scratch),
            input_output_aliases=aliases or {},
            compiler_params=pltpu.CompilerParams(vmem_limit_bytes=VMEM_BYTES),
            cost_estimate=pl.CostEstimate(flops=int(micros * 10**9), bytes_accessed=0, transcendentals=0),
            name=name,
        )

    count = len(links)
    state, med = call(
        load_kernel, [pltpu.VMEM(apart, f32), med_shape], [hbm] * 3, "load", 4,
        [pltpu.VMEM(material.shape, f32), field_sems, pltpu.SemaphoreType.DMA],
    )(
        pltpu.with_memory_space_constraint(material, pltpu.HBM), dense(forward), dense(adjoint),
    )
    state = state.reshape(rows, SUBS, LANES)
    by_line = [[send_shape for link in links if link[0] == line] for line in range(2)]
    across = len(by_line[0])
    ghosts = []
    for line in range(2):
        sends = call(functools.partial(pack_kernel, line), by_line[line], [smem, vmem, vmem], "pack", 0)(
            place, state, send_list
        )
        ghosts += exchange(sends, line)
    acc, grad_first, live = call(
        first_kernel, [state_shape, grad_shape, pltpu.VMEM((SUBS, LANES), f32)], [vmem] + [vmem] * 3, "first_section", 8, [products]
    )(counts, state, med, neighbours)
    (mid,) = call(
        middle_kernel, [state_shape], [smem] + [vmem] * (4 + count), "first_ghosts", 4, [outer], aliases={1: 0}
    )(place, acc, state, med, neighbours, *ghosts)
    cut = (nodes // 2 + SUBS // 2) // SUBS * SUBS
    part_shapes = [pltpu.VMEM((3, size, slots), f32) for size in (cut, nodes - cut)]
    acc, *halved = call(
        second_volume_kernel, [state_shape] + part_shapes, [vmem] + [vmem] * 4, "second_volume", 0, [products]
    )(live, mid, state, med, grad_first)
    sends = call(late_pack_kernel, [send_shape] * count, [smem] + [vmem] * 3, "pack", 0.5)(
        place, mid, send_list, halved[0]
    )
    ghosts = exchange(sends[:across], 0) + exchange(sends[across:], 1)
    doubling = lax.axis_size("shot") == 4
    if doubling:
        pieces = [swapped(halved[0], "shot", 1), swapped(halved[1], "shot", 2)]
    if doubling:
        acc, *parts = call(
            partial_kernel, [state_shape] + part_shapes, [vmem] * 5, "gradient_partial", 0, aliases={0: 0}
        )(acc, *halved, *pieces)
        pieces = [swapped(parts[0], "shot", 2), swapped(parts[1], "shot", 1)]
    else:
        gradient = lax.psum(jnp.concatenate(halved, axis=1), "shot")
    (acc,) = call(
        second_faces_kernel, [state_shape], [vmem] * 5, "second_faces", 0.5, aliases={1: 0}
    )(live, acc, mid, med, neighbours)

    (acc,) = call(
        second_ghosts_kernel, [state_shape], [smem] + [vmem] * (4 + count), "second_ghosts", 1, [outer], aliases={1: 0}
    )(place, acc, mid, med, neighbours, *ghosts)
    fwd, adj = call(store_kernel, [part_shape, part_shape], [vmem], "store", 4, [field_sems], [hbm, hbm])(
        acc.reshape(apart)
    )
    if doubling:
        (gradient,) = call(
            total_kernel, [jax.ShapeDtypeStruct(material.shape, f32)], [vmem] * 4, "gradient_total", 0
        )(*parts, *pieces)
    return restored(fwd), restored(adj), gradient


def solution(mesh):
    placed = (
        P("shot", None, None, "dom"),
        P("shot", None, None, "dom"),
        P(None, None, "dom"),
        P("dom"),
        P("dom", None, None),
        P("dom", None),
    )
    return jax.shard_map(
        shards,
        mesh=mesh,
        in_specs=placed,
        out_specs=(
            P("shot", None, None, "dom"),
            P("shot", None, None, "dom"),
            P(None, None, "dom"),
        ),
        check_vma=False,
    )
```

```python
import functools

import jax
import jax.numpy as jnp
import numpy as np
from jax import lax
from jax.experimental import pallas as pl
from jax.experimental.pallas import tpu as pltpu
from jax.sharding import PartitionSpec as P

DEV_Y = 4
ORDER = 5
NODES = ORDER**3
FACE = ORDER * ORDER
FIELDS = 9
LANES = 128
SUBS = 8
step_size = 0.01
lift_weight = 10.0
VMEM_BYTES = 16 * 1024 * 1024

FACE_OFF = (0, 100, 0, 20, 0, 4)
FACE_U = (5, 5, 25, 25, 25, 25)
FACE_V = (1, 1, 1, 1, 5, 5)


def derivative_matrix():
    points = np.array([-1.0, -np.sqrt(3.0 / 7.0), 0.0, np.sqrt(3.0 / 7.0), 1.0])
    barycentric = np.array(
        [1.0 / np.prod([points[a] - points[b] for b in range(5) if b != a]) for a in range(5)]
    )
    matrix = np.zeros((5, 5))
    for a in range(5):
        for b in range(5):
            if a != b:
                matrix[a, b] = barycentric[b] / barycentric[a] / (points[a] - points[b])
        matrix[a, a] = -np.sum(matrix[a])
    return matrix


MAT = derivative_matrix()


def derivative(u):
    e0, e1 = u[0] + u[4], u[1] + u[3]
    o0, o1 = u[0] - u[4], u[1] - u[3]
    mid = u[2] + u[2]
    e0, e1 = e0 - mid, e1 - mid
    out = [None] * 5
    for a in range(2):
        even = float(0.5 * (MAT[a, 0] + MAT[a, 4])) * e0 + float(0.5 * (MAT[a, 1] + MAT[a, 3])) * e1
        odd = float(0.5 * (MAT[a, 0] - MAT[a, 4])) * o0 + float(0.5 * (MAT[a, 1] - MAT[a, 3])) * o1
        out[a] = odd + even
        out[4 - a] = odd - even
    out[2] = float(MAT[2, 0]) * o0 + float(MAT[2, 1]) * o1
    return out


def sub_iota():
    return lax.broadcasted_iota(jnp.int32, (SUBS, LANES), 0)


def half_of():
    return sub_iota() >> 2


def swap_halves(x):
    return pltpu.roll(x, SUBS // 2, axis=0)


def lane_pick(x, idx):
    return jnp.take_along_axis(x, idx, axis=1, mode="promise_in_bounds")


def code_tile(codes_ref, face, slots):
    base = face * slots
    rows = []
    for h in range(2):
        at = base + h * LANES
        at = at if isinstance(at, int) else pl.multiple_of(at, LANES)
        rows.append(jnp.broadcast_to(codes_ref[0:1, pl.ds(at, LANES)], (SUBS, LANES)))
    first, second = rows
    return jnp.where(half_of() == 0, first, second)


def side_offset(axis, up):
    return up * FACE_OFF[2 * axis + 1]


def pack_side(state, list_ref, out, axis, up, slots):
    half = half_of()
    low = half == 0
    lane_group = lax.broadcasted_iota(jnp.int32, (SUBS, LANES), 1) >> 5
    masks = [lane_group == q for q in range(1, 4)]
    side = 2 * axis
    row = jnp.where(up > 0, list_ref[0, side + 1 : side + 2, :], list_ref[0, side : side + 1, :])
    listed = jnp.broadcast_to(jnp.concatenate([row] * 4, axis=1), (SUBS, LANES))
    idx = listed & (LANES - 1)
    here = (listed < slots) & ((listed >> 7) == half)
    start = side_offset(axis, up)

    def combine(parts):
        picked = [lane_pick(part, idx) for part in parts]
        groups = []
        for x in range(2):
            four = picked[4 * x : 4 * x + 4]
            tile = four[0]
            for q in range(1, len(four)):
                tile = jnp.where(masks[q - 1], four[q], tile)
            tile = jnp.where(here, tile, 0.0)
            groups.append(tile + swap_halves(tile))
        return jnp.where(low, groups[0], groups[1])

    for p in range(FACE):
        node = start + FACE_U[side] * (p // ORDER) + FACE_V[side] * (p % ORDER)
        out[p] = combine([state[k * NODES + node] for k in range(8)])
    for g in range(4):
        parts = []
        for w in range(8):
            p = min(8 * g + w, FACE - 1)
            node = start + FACE_U[side] * (p // ORDER) + FACE_V[side] * (p % ORDER)
            parts.append(state[8 * NODES + node])
        out[FACE + g] = combine(parts)


def add_rows(acc, node, jumps, coef, direction, sign):
    lam, mu, buoy, speed = coef
    a, b, c = direction, (direction + 1) % 3, (direction + 2) % 3
    s_aa, s_bb, s_cc = 3 + a, 3 + b, 3 + c
    s_ab, s_ac, s_bc = 6 + c, 6 + b, 6 + a
    across = lam * jumps[a]
    flux = {
        a: buoy * jumps[s_aa],
        b: buoy * jumps[s_ab],
        c: buoy * jumps[s_ac],
        s_aa: across + (mu + mu) * jumps[a],
        s_bb: across,
        s_cc: across,
        s_ab: mu * jumps[b],
        s_ac: mu * jumps[c],
    }
    for k in range(FIELDS):
        row = k * NODES + node
        total = speed * jumps[k]
        if k in flux:
            total = total + flux[k] if sign > 0 else total - flux[k]
        acc[row] = acc[row] + total


def coefs(med, node):
    return [med[m * NODES + node] for m in range(4)]


def volume_pass(state, acc, med, products, average, scaled):
    def x_lines(j, carry):
        for k in range(5):
            for field, row in ((0, 3), (1, 8), (2, 7), (3, 0), (8, 1), (7, 2)):
                out = derivative([state[field * NODES + 25 * i + 5 * j + k] for i in range(5)])
                for i in range(5):
                    acc[row * NODES + 25 * i + 5 * j + k] = out[i]
        return carry

    lax.fori_loop(0, ORDER, x_lines, 0, unroll=True)

    def y_lines(i, carry):
        for k in range(5):
            for field, row, more in ((0, 8, 1), (1, 4, 0), (2, 6, 0), (8, 0, 1), (4, 1, 1), (6, 2, 1)):
                out = derivative([state[field * NODES + 25 * i + 5 * j + k] for j in range(5)])
                for j in range(5):
                    at = row * NODES + 25 * i + 5 * j + k
                    acc[at] = acc[at] + out[j] if more else out[j]
        return carry

    lax.fori_loop(0, ORDER, y_lines, 0, unroll=True)

    def z_line(first):
        parts = {}
        for field in (0, 1, 2, 7, 6, 5):
            parts[field] = derivative([state[field * NODES + first + k] for k in range(5)])
        for k in range(5):
            node = first + k
            lam, mu, buoy = (scaled(value) for value in coefs(med, node)[:3])
            old = [acc[row * NODES + node] for row in range(FIELDS) if row != 5]
            sdiv = [old[0] + parts[7][k], old[1] + parts[6][k], old[2] + parts[5][k]]
            g11, g22, g33 = old[3], old[4], parts[2][k]
            r23 = old[5] + parts[1][k]
            r13 = old[6] + parts[0][k]
            r12 = old[7]
            div = g11 + g22 + g33
            spread = lam * div
            mu2 = mu + mu
            volume = [buoy * s for s in sdiv]
            volume += [spread + mu2 * g for g in (g11, g22, g33)]
            volume += [mu * r for r in (r23, r13, r12)]
            own = [state[row * NODES + node] for row in range(FIELDS)]
            for row in range(FIELDS):
                acc[row * NODES + node] = average(own[row], row * NODES + node) + volume[row]
            dual = [pltpu.roll(x, SUBS - 2, axis=0) for x in own]
            pressure = div * (dual[3] + dual[4] + dual[5])
            normal = g11 * dual[3] + g22 * dual[4] + g33 * dual[5]
            shear = normal + normal + (r23 * dual[6] + r13 * dual[7] + r12 * dual[8])
            light = sdiv[0] * dual[0] + sdiv[1] * dual[1] + sdiv[2] * dual[2]
            for m, value in enumerate((pressure, shear, light)):
                products[pl.ds((m * LANES + node) * SUBS, SUBS), :] = value

    def z_lines(i, carry):
        for j in range(5):
            z_line(25 * i + 5 * j)
        return carry

    lax.fori_loop(0, ORDER, z_lines, 0, unroll=True)


def shot_sums(products, emit):
    for m in range(3):
        for g in range((NODES + 7) // 8):
            rows = min(8, NODES - 8 * g)
            base = (m * LANES + 8 * g) * SUBS
            for h in range(2):
                first = products[pl.ds(base + 4 * h, 8, stride=SUBS), :]
                second = products[pl.ds(base + 4 * h + 1, 8, stride=SUBS), :]
                emit(m, 8 * g, rows, h, (first + second)[:rows])


def local_pass(state, acc, med, codes_ref, slots, weight):
    half = half_of()
    low = half == 0
    free_code = 6 * slots + 4 * 32
    for face in range(6):
        codes = code_tile(codes_ref, face, slots)
        idx = codes & (LANES - 1)
        match = (codes >> 8) == (face ^ 1)
        same = match & (((codes >> 7) & 1) == half)
        cross = match & (((codes >> 7) & 1) != half)
        free = codes == free_code
        factor_v = jnp.where(free, 0.0, weight)
        factor_s = jnp.where(free, 2.0 * weight, weight)
        other = face ^ 1

        def body(u, carry, face=face, other=other, idx=idx, same=same, cross=cross,
                 factor_v=factor_v, factor_s=factor_s):
            for v in range(ORDER):
                shift = FACE_U[face] * u + FACE_V[face] * v
                node = FACE_OFF[face] + shift
                source = FACE_OFF[other] + shift
                jumps = []
                for k in range(FIELDS):
                    there = state[k * NODES + source]
                    outer = jnp.where(same, lane_pick(there, idx), 0.0)
                    outer = jnp.where(cross, lane_pick(swap_halves(there), idx), outer)
                    jump = outer - state[k * NODES + node]
                    jumps.append(jump * (factor_v if k < 3 else factor_s))
                add_rows(acc, node, jumps, coefs(med, node), face // 2, 2 * (face % 2) - 1)
            return carry

        lax.fori_loop(0, ORDER, body, 0, unroll=True)


def ghost_tiles(ghost, p, low):
    tile = ghost[p]
    turned = swap_halves(tile)
    tile9 = ghost[FACE + (p >> 3)]
    turned9 = swap_halves(tile9)
    chosen = half_of() == ((p >> 2) & 1)
    return jnp.where(low, tile, turned), jnp.where(low, turned, tile), jnp.where(chosen, tile9, turned9)


def ghost_pass(acc, med, codes_ref, ghost, axis, up, paired, slots, scale):
    low = half_of() == 0
    face = 2 * axis + up
    sign = (2 * up - 1).astype(jnp.float32)
    codes = code_tile(codes_ref, face, slots) - (6 * slots + 32 * face)
    inside = (codes >= 0) & (codes < 32)
    weight = jnp.where(inside, jnp.where(paired, scale, 0.0), 0.0)
    idx = codes & 31
    shifted = [idx + 32 * q for q in range(4)]
    start = side_offset(axis, up)

    def body(u, carry):
        for v in range(ORDER):
            p = ORDER * u + v
            node = start + FACE_U[2 * axis] * u + FACE_V[2 * axis] * v
            first, second, nine = ghost_tiles(ghost, p, low)
            jumps = []
            for k in range(8):
                jumps.append(lane_pick(first if k < 4 else second, shifted[k % 4]) * weight)
            jumps.append(lane_pick(nine, idx + 32 * (p & 3)) * weight)
            lam, mu, buoy, speed = coefs(med, node)
            add_rows(acc, node, jumps, (sign * lam, sign * mu, sign * buoy, speed), axis, 1)
        return carry

    lax.fori_loop(0, ORDER, body, 0, unroll=True)


def other_sources(state, acc, med, codes_ref, ghosts, ups, paired, axes, outer, slots, scale):
    half = half_of()
    low = half == 0
    first_ghost = 6 * slots

    def codes_of(face):
        return code_tile(codes_ref, face, slots)

    left = jnp.zeros((SUBS, LANES), jnp.int32)
    for face in range(6):
        codes = codes_of(face)
        source = jnp.where(codes < first_ghost, codes >> 8, 6 + ((codes - first_ghost) >> 5))
        usual = (source == (face ^ 1)) | (source >= 10)
        if face < 4:
            usual = usual | (source == 6 + face)
        left = left | jnp.where(usual, 0, 1)
    remaining = jnp.max(left)

    @pl.when(remaining > 0)
    def _():
        def pair(t, carry):
            face, origin = t // 10, t % 10
            codes = code_tile(codes_ref, face, slots)
            source = jnp.where(codes < first_ghost, codes >> 8, 6 + ((codes - first_ghost) >> 5))
            mine = source == origin
            done = (origin == (face ^ 1)) | ((face < 4) & (origin == 6 + face))
            count = jnp.max(jnp.where(mine, 1, 0))

            @pl.when((count > 0) & jnp.logical_not(done))
            def _():
                weight = jnp.where(mine, scale, 0.0)
                axis, sign = face >> 1, (2 * (face & 1) - 1).astype(jnp.float32)

                def strides(which):
                    line = which >> 1
                    off = (which & 1) * jnp.where(line == 0, 100, jnp.where(line == 1, 20, 4))
                    return off, jnp.where(line == 0, 5, 25), jnp.where(line == 2, 5, 1)

                off, du, dv = strides(face)
                off2, du2, dv2 = strides(jnp.minimum(origin, 5))

                def at_node(p, carry):
                    u, v = p // ORDER, p % ORDER
                    node = off + du * u + dv * v

                    @pl.when(origin < 6)
                    def _():
                        there_node = off2 + du2 * u + dv2 * v
                        idx = codes & (LANES - 1)
                        same = ((codes >> 7) & 1) == half
                        for k in range(FIELDS):
                            there = state[k * NODES + there_node]
                            turned = swap_halves(there)
                            outer[k] = jnp.where(same, lane_pick(there, idx), lane_pick(turned, idx)) * weight

                    @pl.when(origin >= 6)
                    def _():
                        for k in range(FIELDS):
                            outer[k] = jnp.zeros((SUBS, LANES), jnp.float32)

                    for ghost, up, pair_here, line in zip(ghosts, ups, paired, axes):

                        @pl.when((origin == 6 + 2 * line + up) & pair_here)
                        def _(ghost=ghost):
                            idx = (codes - first_ghost) & 31
                            first, second, nine = ghost_tiles(ghost, p, low)
                            for k in range(8):
                                tile = first if k < 4 else second
                                outer[k] = lane_pick(tile, idx + 32 * (k % 4)) * weight
                            outer[8] = lane_pick(nine, idx + 32 * (p & 3)) * weight

                    lam, mu, buoy, speed = coefs(med, node)
                    a = axis
                    b, c = lax.rem(axis + 1, 3), lax.rem(axis + 2, 3)
                    across = lam * outer[a]
                    flux = (
                        (a, buoy * outer[3 + a]),
                        (b, buoy * outer[6 + c]),
                        (c, buoy * outer[6 + b]),
                        (3 + a, across + (mu + mu) * outer[a]),
                        (3 + b, across),
                        (3 + c, across),
                        (6 + c, mu * outer[b]),
                        (6 + b, mu * outer[c]),
                        (6 + a, None),
                    )
                    for k, value in flux:
                        row = k * NODES + node
                        total = speed * outer[k]
                        if value is not None:
                            total = total + sign * value
                        acc[row] = acc[row] + total
                    return carry

                lax.fori_loop(0, FACE, at_node, 0)

            return carry

        lax.fori_loop(0, 60, pair, 0)


def link_ups(place_ref, links):
    return [1 - ((lax.div(place_ref[0], stride) + parity) & 1) for _, stride, parity, _ in links]


def link_paired(place_ref, links, ups):
    others = [place_ref[0] + (2 * up - 1) * link[1] for up, link in zip(ups, links)]
    return [(other >= 0) & (other < link[3]) for other, link in zip(others, links)]


def load_kernel(slots, links, mat_hbm, fwd_hbm, adj_hbm, state_ref, med_ref, mat_ref, sems, mat_sem):
    mat_copy = pltpu.make_async_copy(mat_hbm, mat_ref, mat_sem)
    mat_copy.start()
    copies = []
    for k in range(FIELDS):
        span = pl.ds(k * NODES, NODES)
        for n, far in enumerate((fwd_hbm, adj_hbm)):
            copies.append(pltpu.make_async_copy(far.at[span], state_ref.at[span, :, n], sems.at[n, k]))
            copies[-1].start()
    mat_copy.wait()
    spread_material(mat_ref, med_ref)
    for copy in copies:
        copy.wait()


def pack_links(slots, links, place_ref, state_ref, list_ref, sends, line):
    ups = link_ups(place_ref, links)
    chosen = [n for n, link in enumerate(links) if link[0] == line]
    for n, send in zip(chosen, sends):
        pack_side(state_ref, list_ref, send, line, ups[n], slots)


def pack_kernel(line, slots, links, place_ref, state_ref, list_ref, *sends):
    pack_links(slots, links, place_ref, state_ref, list_ref, sends, line)


def late_pack_kernel(slots, links, place_ref, state_ref, list_ref, grad_ref, *sends):
    across = sum(link[0] == 0 for link in links)
    pack_links(slots, links, place_ref, state_ref, list_ref, sends[:across], 0)
    pack_links(slots, links, place_ref, state_ref, list_ref, sends[across:], 1)


def spread_material(mat_ref, med_ref):
    low = half_of() == 0
    for node in range(NODES):
        rows = []
        for m in range(3):
            first = jnp.broadcast_to(mat_ref[m, node : node + 1, 0:LANES], (SUBS, LANES))
            second = jnp.broadcast_to(mat_ref[m, node : node + 1, LANES : 2 * LANES], (SUBS, LANES))
            rows.append(jnp.where(low, first, second))
        lam, mu, buoy = rows
        speed = jnp.sqrt((lam + 2.0 * mu) * buoy)
        for m, value in enumerate((lam, mu, buoy, speed)):
            med_ref[m * NODES + node] = step_size * value


def first_kernel(slots, links, counts_ref, state_ref, med_ref, codes_ref, acc_ref, grad_ref, live_ref, products):
    lane = lax.broadcasted_iota(jnp.int32, (SUBS, LANES), 1)
    count = jnp.broadcast_to(counts_ref[...].reshape(1, 1), (SUBS, LANES))
    live_ref[...] = jnp.where(half_of() * LANES + lane < count, 1.0, 0.0)
    volume_pass(state_ref, acc_ref, med_ref, products, lambda own, row: own, lambda value: value)
    shot_sums(products, store_gradient(live_ref, [grad_ref], None))
    local_pass(state_ref, acc_ref, med_ref, codes_ref, slots, 0.5 * lift_weight)


def store_gradient(live_ref, grad_refs, earlier_ref):
    alive = [jnp.broadcast_to(live_ref[4 * h : 4 * h + 1, :], (SUBS, LANES)) > 0.0 for h in range(2)]

    def emit(m, start, rows, h, value):
        at = (m, slice(start, start + rows), slice(h * LANES, (h + 1) * LANES))
        if earlier_ref is not None:
            value = (0.5 * step_size) * (earlier_ref[at] + value)
        value = jnp.where(alive[h][:rows], value, 0.0)
        for grad_ref in grad_refs:
            size = grad_ref.shape[1]
            if 0 <= start < size:
                grad_ref[m, start : start + rows, h * LANES : (h + 1) * LANES] = value
            start -= size

    return emit


def add_ghosts(links, place_ref, acc_ref, med_ref, codes_ref, ghosts, slots, scale):
    ups = link_ups(place_ref, links)
    paired = link_paired(place_ref, links, ups)
    for link, up, pair_here, ghost in zip(links, ups, paired, ghosts):
        ghost_pass(acc_ref, med_ref, codes_ref, ghost, link[0], up, pair_here, slots, scale)


def add_others(links, place_ref, state_ref, acc_ref, med_ref, codes_ref, ghosts, outer, slots, scale):
    ups = link_ups(place_ref, links)
    paired = link_paired(place_ref, links, ups)
    axes = [link[0] for link in links]
    other_sources(state_ref, acc_ref, med_ref, codes_ref, ghosts, ups, paired, axes, outer, slots, scale)


def middle_kernel(slots, links, place_ref, acc_in, state_ref, med_ref, codes_ref, *rest):
    ghosts, (mid_ref, outer) = rest[: len(links)], rest[len(links) :]
    add_ghosts(links, place_ref, mid_ref, med_ref, codes_ref, ghosts, slots, 0.5 * lift_weight)
    add_others(links, place_ref, state_ref, mid_ref, med_ref, codes_ref, ghosts, outer, slots, 0.5 * lift_weight)


def second_volume_kernel(
    slots, links, live_ref, mid_ref, state_ref, med_ref, first_ref, acc_ref, near_ref, far_ref, products
):
    share = 0.5 * live_ref[...]
    volume_pass(
        mid_ref, acc_ref, med_ref, products,
        lambda own, row: share * (own + state_ref[row]), lambda value: share * value,
    )
    shot_sums(products, store_gradient(live_ref, [near_ref, far_ref], first_ref))


def second_faces_kernel(slots, links, live_ref, acc_in, mid_ref, med_ref, codes_ref, acc_ref):
    weight = (0.25 * lift_weight) * live_ref[...]
    local_pass(mid_ref, acc_ref, med_ref, codes_ref, slots, weight)


def second_ghosts_kernel(slots, links, place_ref, acc_in, mid_ref, med_ref, codes_ref, *rest):
    ghosts, (acc_ref, outer) = rest[: len(links)], rest[len(links) :]
    add_ghosts(links, place_ref, acc_ref, med_ref, codes_ref, ghosts, slots, 0.25 * lift_weight)
    add_others(links, place_ref, mid_ref, acc_ref, med_ref, codes_ref, ghosts, outer, slots, 0.25 * lift_weight)


def partial_kernel(slots, links, acc_in, a_ref, b_ref, near_ref, far_ref, acc_ref, first_ref, second_ref):
    first_ref[...] = a_ref[...] + near_ref[...]
    second_ref[...] = b_ref[...] + far_ref[...]


def store_copies(acc_ref, fwd_hbm, adj_hbm, sems):
    copies = []
    for k in range(FIELDS):
        span = pl.ds(k * NODES, NODES)
        for n, far in enumerate((fwd_hbm, adj_hbm)):
            copies.append(pltpu.make_async_copy(acc_ref.at[span, :, n], far.at[span], sems.at[n, k]))
            copies[-1].start()
    return copies


def store_kernel(slots, links, acc_ref, fwd_hbm, adj_hbm, sems):
    for copy in store_copies(acc_ref, fwd_hbm, adj_hbm, sems):
        copy.wait()


def store_and_sum_kernel(
    slots, links, acc_ref, a_ref, b_ref, c_ref, d_ref, fwd_hbm, adj_hbm, grad_hbm, sems, grad_ref, grad_sem
):
    copies = store_copies(acc_ref, fwd_hbm, adj_hbm, sems)
    cut = a_ref.shape[1]
    grad_ref[:, :cut] = a_ref[...] + c_ref[...]
    grad_ref[:, cut:] = b_ref[...] + d_ref[...]
    copies.append(pltpu.make_async_copy(grad_ref, grad_hbm, grad_sem))
    copies[-1].start()
    for copy in copies:
        copy.wait()


def tree_links(devices):
    links = []
    for axis, stride in ((0, DEV_Y), (1, 1)):
        for parity in range(2):
            pairs = [(d, d + stride) for d in range(devices - stride) if (d // stride) % 2 == parity]
            if pairs:
                alone = set(range(devices)) - {d for pair in pairs for d in pair}
                route = pairs + [(b, a) for a, b in pairs] + [(d, d) for d in sorted(alone)]
                links.append((axis, stride, parity, devices, route))
    return links


def swapped(block, axis, distance):
    route = [(i, i ^ distance) for i in range(lax.axis_size(axis))]
    return lax.ppermute(block, axis, route)


def shards(forward, adjoint, material, counts, send_list, neighbours):
    shots, fields, nodes, slots = forward.shape
    halves = slots // LANES
    rows = fields * nodes
    assert 2 * shots * halves == SUBS and nodes == NODES and fields == FIELDS

    def dense(values):
        cut = values.reshape(shots, fields, nodes, halves, LANES)
        tiles = cut.transpose(1, 2, 3, 0, 4).reshape(rows, halves, shots, LANES)
        return pltpu.with_memory_space_constraint(tiles, pltpu.HBM)

    def restored(values):
        cut = values.reshape(fields, nodes, halves, shots, LANES)
        return cut.transpose(3, 0, 1, 2, 4).reshape(shots, fields, nodes, slots)

    links = tree_links(lax.axis_size("dom"))
    axes = tuple(link[:4] for link in links)
    place = lax.axis_index("dom").astype(jnp.int32).reshape(1)

    def exchange(sends, line):
        routes = [link[4] for link in links if link[0] == line]
        return [lax.ppermute(send, "dom", route) for send, route in zip(sends, routes)]

    vmem = pl.BlockSpec(memory_space=pltpu.VMEM)
    smem = pl.BlockSpec(memory_space=pltpu.SMEM)
    hbm = pl.BlockSpec(memory_space=pltpu.HBM)
    f32 = jnp.float32
    state_shape = pltpu.VMEM((rows, SUBS, LANES), f32)
    send_shape = pltpu.VMEM((FACE + 4, SUBS, LANES), f32)
    med_shape = pltpu.VMEM((4 * nodes, SUBS, LANES), f32)
    grad_shape = pltpu.VMEM(material.shape, f32)
    apart = (rows, halves, 2, shots, LANES)
    part_shape = jax.ShapeDtypeStruct((rows, halves, shots, LANES), f32)
    products = pltpu.VMEM((3 * LANES * SUBS, LANES), f32)
    outer = pltpu.VMEM((FIELDS, SUBS, LANES), f32)
    field_sems = pltpu.SemaphoreType.DMA((2, FIELDS))

    def call(kernel, out_shape, in_specs, name, micros, scratch=(), out_specs=None, aliases=None):
        return pl.pallas_call(
            functools.partial(kernel, slots, axes),
            out_shape=out_shape,
            in_specs=in_specs,
            out_specs=out_specs or [vmem] * len(out_shape),
            scratch_shapes=list(scratch),
            input_output_aliases=aliases or {},
            compiler_params=pltpu.CompilerParams(vmem_limit_bytes=VMEM_BYTES),
            cost_estimate=pl.CostEstimate(flops=int(micros * 10**9), bytes_accessed=0, transcendentals=0),
            name=name,
        )

    count = len(links)
    state, med = call(
        load_kernel, [pltpu.VMEM(apart, f32), med_shape], [hbm] * 3, "load", 4,
        [pltpu.VMEM(material.shape, f32), field_sems, pltpu.SemaphoreType.DMA],
    )(
        pltpu.with_memory_space_constraint(material, pltpu.HBM), dense(forward), dense(adjoint),
    )
    state = state.reshape(rows, SUBS, LANES)
    by_line = [[send_shape for link in links if link[0] == line] for line in range(2)]
    across = len(by_line[0])
    ghosts = []
    for line in range(2):
        sends = call(functools.partial(pack_kernel, line), by_line[line], [smem, vmem, vmem], "pack", 0)(
            place, state, send_list
        )
        ghosts += exchange(sends, line)
    acc, grad_first, live = call(
        first_kernel, [state_shape, grad_shape, pltpu.VMEM((SUBS, LANES), f32)], [vmem] + [vmem] * 3, "first_section", 8, [products]
    )(counts, state, med, neighbours)
    (mid,) = call(
        middle_kernel, [state_shape], [smem] + [vmem] * (4 + count), "first_ghosts", 4, [outer], aliases={1: 0}
    )(place, acc, state, med, neighbours, *ghosts)
    cut = (nodes // 2 + SUBS // 2) // SUBS * SUBS
    part_shapes = [pltpu.VMEM((3, size, slots), f32) for size in (cut, nodes - cut)]
    acc, *halved = call(
        second_volume_kernel, [state_shape] + part_shapes, [vmem] + [vmem] * 4, "second_volume", 0, [products]
    )(live, mid, state, med, grad_first)
    sends = call(late_pack_kernel, [send_shape] * count, [smem] + [vmem] * 3, "pack", 0.5)(
        place, mid, send_list, halved[0]
    )
    ghosts = exchange(sends[:across], 0) + exchange(sends[across:], 1)
    doubling = lax.axis_size("shot") == 4
    if doubling:
        pieces = [swapped(halved[0], "shot", 1), swapped(halved[1], "shot", 2)]
    if doubling:
        acc, *parts = call(
            partial_kernel, [state_shape] + part_shapes, [vmem] * 5, "gradient_partial", 0, aliases={0: 0}
        )(acc, *halved, *pieces)
        pieces = [swapped(parts[0], "shot", 2), swapped(parts[1], "shot", 1)]
    else:
        gradient = lax.psum(jnp.concatenate(halved, axis=1), "shot")
    (acc,) = call(
        second_faces_kernel, [state_shape], [vmem] * 5, "second_faces", 0.5, aliases={1: 0}
    )(live, acc, mid, med, neighbours)

    (acc,) = call(
        second_ghosts_kernel, [state_shape], [smem] + [vmem] * (4 + count), "second_ghosts", 1, [outer], aliases={1: 0}
    )(place, acc, mid, med, neighbours, *ghosts)
    if doubling:
        fwd, adj, gradient = call(
            store_and_sum_kernel, [part_shape, part_shape, jax.ShapeDtypeStruct(material.shape, f32)], [vmem] * 5,
            "store", 4, [field_sems, pltpu.VMEM(material.shape, f32), pltpu.SemaphoreType.DMA], [hbm] * 3,
        )(acc.reshape(apart), *parts, *pieces)
    else:
        fwd, adj = call(store_kernel, [part_shape] * 2, [vmem], "store", 4, [field_sems], [hbm] * 2)(
            acc.reshape(apart)
        )
    return restored(fwd), restored(adj), gradient


def solution(mesh):
    placed = (
        P("shot", None, None, "dom"),
        P("shot", None, None, "dom"),
        P(None, None, "dom"),
        P("dom"),
        P("dom", None, None),
        P("dom", None),
    )
    return jax.shard_map(
        shards,
        mesh=mesh,
        in_specs=placed,
        out_specs=(
            P("shot", None, None, "dom"),
            P("shot", None, None, "dom"),
            P(None, None, "dom"),
        ),
        check_vma=False,
    )
```

```python
import functools

import jax
import jax.numpy as jnp
import numpy as np
from jax import lax
from jax.experimental import pallas as pl
from jax.experimental.pallas import tpu as pltpu
from jax.sharding import PartitionSpec as P

DEV_Y = 4
ORDER = 5
NODES = ORDER**3
FACE = ORDER * ORDER
FIELDS = 9
LANES = 128
SUBS = 8
step_size = 0.01
lift_weight = 10.0
VMEM_BYTES = 16 * 1024 * 1024

FACE_OFF = (0, 100, 0, 20, 0, 4)
FACE_U = (5, 5, 25, 25, 25, 25)
FACE_V = (1, 1, 1, 1, 5, 5)


def derivative_matrix():
    points = np.array([-1.0, -np.sqrt(3.0 / 7.0), 0.0, np.sqrt(3.0 / 7.0), 1.0])
    barycentric = np.array(
        [1.0 / np.prod([points[a] - points[b] for b in range(5) if b != a]) for a in range(5)]
    )
    matrix = np.zeros((5, 5))
    for a in range(5):
        for b in range(5):
            if a != b:
                matrix[a, b] = barycentric[b] / barycentric[a] / (points[a] - points[b])
        matrix[a, a] = -np.sum(matrix[a])
    return matrix


MAT = derivative_matrix()


def derivative(u):
    e0, e1 = u[0] + u[4], u[1] + u[3]
    o0, o1 = u[0] - u[4], u[1] - u[3]
    mid = u[2] + u[2]
    e0, e1 = e0 - mid, e1 - mid
    out = [None] * 5
    for a in range(2):
        even = float(0.5 * (MAT[a, 0] + MAT[a, 4])) * e0 + float(0.5 * (MAT[a, 1] + MAT[a, 3])) * e1
        odd = float(0.5 * (MAT[a, 0] - MAT[a, 4])) * o0 + float(0.5 * (MAT[a, 1] - MAT[a, 3])) * o1
        out[a] = odd + even
        out[4 - a] = odd - even
    out[2] = float(MAT[2, 0]) * o0 + float(MAT[2, 1]) * o1
    return out


def sub_iota():
    return lax.broadcasted_iota(jnp.int32, (SUBS, LANES), 0)


def half_of():
    return sub_iota() >> 2


def swap_halves(x):
    return pltpu.roll(x, SUBS // 2, axis=0)


def lane_pick(x, idx):
    return jnp.take_along_axis(x, idx, axis=1, mode="promise_in_bounds")


def code_tile(codes_ref, face, slots):
    base = face * slots
    rows = []
    for h in range(2):
        at = base + h * LANES
        at = at if isinstance(at, int) else pl.multiple_of(at, LANES)
        rows.append(jnp.broadcast_to(codes_ref[0:1, pl.ds(at, LANES)], (SUBS, LANES)))
    first, second = rows
    return jnp.where(half_of() == 0, first, second)


def side_offset(axis, up):
    return up * FACE_OFF[2 * axis + 1]


def pack_side(state, list_ref, out, axis, up, slots):
    half = half_of()
    low = half == 0
    lane_group = lax.broadcasted_iota(jnp.int32, (SUBS, LANES), 1) >> 5
    masks = [lane_group == q for q in range(1, 4)]
    side = 2 * axis
    row = jnp.where(up > 0, list_ref[0, side + 1 : side + 2, :], list_ref[0, side : side + 1, :])
    listed = jnp.broadcast_to(jnp.concatenate([row] * 4, axis=1), (SUBS, LANES))
    idx = listed & (LANES - 1)
    here = (listed < slots) & ((listed >> 7) == half)
    start = side_offset(axis, up)

    def combine(parts):
        picked = [lane_pick(part, idx) for part in parts]
        groups = []
        for x in range(2):
            four = picked[4 * x : 4 * x + 4]
            tile = four[0]
            for q in range(1, len(four)):
                tile = jnp.where(masks[q - 1], four[q], tile)
            tile = jnp.where(here, tile, 0.0)
            groups.append(tile + swap_halves(tile))
        return jnp.where(low, groups[0], groups[1])

    for p in range(FACE):
        node = start + FACE_U[side] * (p // ORDER) + FACE_V[side] * (p % ORDER)
        out[p] = combine([state[k * NODES + node] for k in range(8)])
    for g in range(4):
        parts = []
        for w in range(8):
            p = min(8 * g + w, FACE - 1)
            node = start + FACE_U[side] * (p // ORDER) + FACE_V[side] * (p % ORDER)
            parts.append(state[8 * NODES + node])
        out[FACE + g] = combine(parts)


def add_rows(acc, node, jumps, coef, direction, sign):
    lam, mu, buoy, speed = coef
    a, b, c = direction, (direction + 1) % 3, (direction + 2) % 3
    s_aa, s_bb, s_cc = 3 + a, 3 + b, 3 + c
    s_ab, s_ac, s_bc = 6 + c, 6 + b, 6 + a
    across = lam * jumps[a]
    flux = {
        a: buoy * jumps[s_aa],
        b: buoy * jumps[s_ab],
        c: buoy * jumps[s_ac],
        s_aa: across + (mu + mu) * jumps[a],
        s_bb: across,
        s_cc: across,
        s_ab: mu * jumps[b],
        s_ac: mu * jumps[c],
    }
    for k in range(FIELDS):
        row = k * NODES + node
        total = speed * jumps[k]
        if k in flux:
            total = total + flux[k] if sign > 0 else total - flux[k]
        acc[row] = acc[row] + total


def coefs(med, node):
    return [med[m * NODES + node] for m in range(4)]


def volume_pass(state, acc, med, products, average, scaled):
    def x_lines(j, carry):
        for k in range(5):
            for field, row in ((0, 3), (1, 8), (2, 7), (3, 0), (8, 1), (7, 2)):
                out = derivative([state[field * NODES + 25 * i + 5 * j + k] for i in range(5)])
                for i in range(5):
                    acc[row * NODES + 25 * i + 5 * j + k] = out[i]
        return carry

    lax.fori_loop(0, ORDER, x_lines, 0, unroll=True)

    def y_lines(i, carry):
        for k in range(5):
            for field, row, more in ((0, 8, 1), (1, 4, 0), (2, 6, 0), (8, 0, 1), (4, 1, 1), (6, 2, 1)):
                out = derivative([state[field * NODES + 25 * i + 5 * j + k] for j in range(5)])
                for j in range(5):
                    at = row * NODES + 25 * i + 5 * j + k
                    acc[at] = acc[at] + out[j] if more else out[j]
        return carry

    lax.fori_loop(0, ORDER, y_lines, 0, unroll=True)

    def z_line(first):
        parts = {}
        for field in (0, 1, 2, 7, 6, 5):
            parts[field] = derivative([state[field * NODES + first + k] for k in range(5)])
        for k in range(5):
            node = first + k
            lam, mu, buoy = (scaled(value) for value in coefs(med, node)[:3])
            old = [acc[row * NODES + node] for row in range(FIELDS) if row != 5]
            sdiv = [old[0] + parts[7][k], old[1] + parts[6][k], old[2] + parts[5][k]]
            g11, g22, g33 = old[3], old[4], parts[2][k]
            r23 = old[5] + parts[1][k]
            r13 = old[6] + parts[0][k]
            r12 = old[7]
            div = g11 + g22 + g33
            spread = lam * div
            mu2 = mu + mu
            volume = [buoy * s for s in sdiv]
            volume += [spread + mu2 * g for g in (g11, g22, g33)]
            volume += [mu * r for r in (r23, r13, r12)]
            own = [state[row * NODES + node] for row in range(FIELDS)]
            for row in range(FIELDS):
                acc[row * NODES + node] = average(own[row], row * NODES + node) + volume[row]
            dual = [pltpu.roll(x, SUBS - 2, axis=0) for x in own]
            pressure = div * (dual[3] + dual[4] + dual[5])
            normal = g11 * dual[3] + g22 * dual[4] + g33 * dual[5]
            shear = normal + normal + (r23 * dual[6] + r13 * dual[7] + r12 * dual[8])
            light = sdiv[0] * dual[0] + sdiv[1] * dual[1] + sdiv[2] * dual[2]
            for m, value in enumerate((pressure, shear, light)):
                products[pl.ds((m * LANES + node) * SUBS, SUBS), :] = value

    def z_lines(i, carry):
        for j in range(5):
            z_line(25 * i + 5 * j)
        return carry

    lax.fori_loop(0, ORDER, z_lines, 0, unroll=True)


def shot_sums(products, emit):
    for m in range(3):
        for g in range((NODES + 7) // 8):
            rows = min(8, NODES - 8 * g)
            base = (m * LANES + 8 * g) * SUBS
            for h in range(2):
                first = products[pl.ds(base + 4 * h, 8, stride=SUBS), :]
                second = products[pl.ds(base + 4 * h + 1, 8, stride=SUBS), :]
                emit(m, 8 * g, rows, h, (first + second)[:rows])


def local_pass(state, acc, med, codes_ref, slots, weight):
    half = half_of()
    low = half == 0
    free_code = 6 * slots + 4 * 32
    for face in range(6):
        codes = code_tile(codes_ref, face, slots)
        idx = codes & (LANES - 1)
        match = (codes >> 8) == (face ^ 1)
        same = match & (((codes >> 7) & 1) == half)
        cross = match & (((codes >> 7) & 1) != half)
        free = codes == free_code
        factor_v = jnp.where(free, 0.0, weight)
        factor_s = jnp.where(free, 2.0 * weight, weight)
        other = face ^ 1

        def body(u, carry, face=face, other=other, idx=idx, same=same, cross=cross,
                 factor_v=factor_v, factor_s=factor_s):
            for v in range(ORDER):
                shift = FACE_U[face] * u + FACE_V[face] * v
                node = FACE_OFF[face] + shift
                source = FACE_OFF[other] + shift
                jumps = []
                for k in range(FIELDS):
                    there = state[k * NODES + source]
                    outer = jnp.where(same, lane_pick(there, idx), 0.0)
                    outer = jnp.where(cross, lane_pick(swap_halves(there), idx), outer)
                    jump = outer - state[k * NODES + node]
                    jumps.append(jump * (factor_v if k < 3 else factor_s))
                add_rows(acc, node, jumps, coefs(med, node), face // 2, 2 * (face % 2) - 1)
            return carry

        lax.fori_loop(0, ORDER, body, 0, unroll=True)


def ghost_tiles(ghost, p, low):
    tile = ghost[p]
    turned = swap_halves(tile)
    tile9 = ghost[FACE + (p >> 3)]
    turned9 = swap_halves(tile9)
    chosen = half_of() == ((p >> 2) & 1)
    return jnp.where(low, tile, turned), jnp.where(low, turned, tile), jnp.where(chosen, tile9, turned9)


def ghost_pass(acc, med, codes_ref, ghost, axis, up, paired, slots, scale):
    low = half_of() == 0
    face = 2 * axis + up
    sign = (2 * up - 1).astype(jnp.float32)
    codes = code_tile(codes_ref, face, slots) - (6 * slots + 32 * face)
    inside = (codes >= 0) & (codes < 32)
    weight = jnp.where(inside, jnp.where(paired, scale, 0.0), 0.0)
    idx = codes & 31
    shifted = [idx + 32 * q for q in range(4)]
    start = side_offset(axis, up)

    def body(u, carry):
        for v in range(ORDER):
            p = ORDER * u + v
            node = start + FACE_U[2 * axis] * u + FACE_V[2 * axis] * v
            first, second, nine = ghost_tiles(ghost, p, low)
            jumps = []
            for k in range(8):
                jumps.append(lane_pick(first if k < 4 else second, shifted[k % 4]) * weight)
            jumps.append(lane_pick(nine, idx + 32 * (p & 3)) * weight)
            lam, mu, buoy, speed = coefs(med, node)
            add_rows(acc, node, jumps, (sign * lam, sign * mu, sign * buoy, speed), axis, 1)
        return carry

    lax.fori_loop(0, ORDER, body, 0, unroll=True)


def other_sources(state, acc, med, codes_ref, ghosts, ups, paired, axes, outer, slots, scale):
    half = half_of()
    low = half == 0
    first_ghost = 6 * slots

    def codes_of(face):
        return code_tile(codes_ref, face, slots)

    left = jnp.zeros((SUBS, LANES), jnp.int32)
    for face in range(6):
        codes = codes_of(face)
        source = jnp.where(codes < first_ghost, codes >> 8, 6 + ((codes - first_ghost) >> 5))
        usual = (source == (face ^ 1)) | (source >= 10)
        if face < 4:
            usual = usual | (source == 6 + face)
        left = left | jnp.where(usual, 0, 1)
    remaining = jnp.max(left)

    @pl.when(remaining > 0)
    def _():
        def pair(t, carry):
            face, origin = t // 10, t % 10
            codes = code_tile(codes_ref, face, slots)
            source = jnp.where(codes < first_ghost, codes >> 8, 6 + ((codes - first_ghost) >> 5))
            mine = source == origin
            done = (origin == (face ^ 1)) | ((face < 4) & (origin == 6 + face))
            count = jnp.max(jnp.where(mine, 1, 0))

            @pl.when((count > 0) & jnp.logical_not(done))
            def _():
                weight = jnp.where(mine, scale, 0.0)
                axis, sign = face >> 1, (2 * (face & 1) - 1).astype(jnp.float32)

                def strides(which):
                    line = which >> 1
                    off = (which & 1) * jnp.where(line == 0, 100, jnp.where(line == 1, 20, 4))
                    return off, jnp.where(line == 0, 5, 25), jnp.where(line == 2, 5, 1)

                off, du, dv = strides(face)
                off2, du2, dv2 = strides(jnp.minimum(origin, 5))

                def at_node(p, carry):
                    u, v = p // ORDER, p % ORDER
                    node = off + du * u + dv * v

                    @pl.when(origin < 6)
                    def _():
                        there_node = off2 + du2 * u + dv2 * v
                        idx = codes & (LANES - 1)
                        same = ((codes >> 7) & 1) == half
                        for k in range(FIELDS):
                            there = state[k * NODES + there_node]
                            turned = swap_halves(there)
                            outer[k] = jnp.where(same, lane_pick(there, idx), lane_pick(turned, idx)) * weight

                    @pl.when(origin >= 6)
                    def _():
                        for k in range(FIELDS):
                            outer[k] = jnp.zeros((SUBS, LANES), jnp.float32)

                    for ghost, up, pair_here, line in zip(ghosts, ups, paired, axes):

                        @pl.when((origin == 6 + 2 * line + up) & pair_here)
                        def _(ghost=ghost):
                            idx = (codes - first_ghost) & 31
                            first, second, nine = ghost_tiles(ghost, p, low)
                            for k in range(8):
                                tile = first if k < 4 else second
                                outer[k] = lane_pick(tile, idx + 32 * (k % 4)) * weight
                            outer[8] = lane_pick(nine, idx + 32 * (p & 3)) * weight

                    lam, mu, buoy, speed = coefs(med, node)
                    a = axis
                    b, c = lax.rem(axis + 1, 3), lax.rem(axis + 2, 3)
                    across = lam * outer[a]
                    flux = (
                        (a, buoy * outer[3 + a]),
                        (b, buoy * outer[6 + c]),
                        (c, buoy * outer[6 + b]),
                        (3 + a, across + (mu + mu) * outer[a]),
                        (3 + b, across),
                        (3 + c, across),
                        (6 + c, mu * outer[b]),
                        (6 + b, mu * outer[c]),
                        (6 + a, None),
                    )
                    for k, value in flux:
                        row = k * NODES + node
                        total = speed * outer[k]
                        if value is not None:
                            total = total + sign * value
                        acc[row] = acc[row] + total
                    return carry

                lax.fori_loop(0, FACE, at_node, 0)

            return carry

        lax.fori_loop(0, 60, pair, 0)


def link_ups(place_ref, links):
    return [1 - ((lax.div(place_ref[0], stride) + parity) & 1) for _, stride, parity, _ in links]


def link_paired(place_ref, links, ups):
    others = [place_ref[0] + (2 * up - 1) * link[1] for up, link in zip(ups, links)]
    return [(other >= 0) & (other < link[3]) for other, link in zip(others, links)]


def load_kernel(slots, links, mat_hbm, fwd_hbm, adj_hbm, state_ref, med_ref, mat_ref, sems, mat_sem):
    mat_copy = pltpu.make_async_copy(mat_hbm, mat_ref, mat_sem)
    mat_copy.start()
    copies = []
    for k in range(FIELDS):
        span = pl.ds(k * NODES, NODES)
        for n, far in enumerate((fwd_hbm, adj_hbm)):
            copies.append(pltpu.make_async_copy(far.at[span], state_ref.at[span, :, n], sems.at[n, k]))
            copies[-1].start()
    mat_copy.wait()
    spread_material(mat_ref, med_ref)
    for copy in copies:
        copy.wait()


def pack_links(slots, links, place_ref, state_ref, list_ref, sends, line):
    ups = link_ups(place_ref, links)
    chosen = [n for n, link in enumerate(links) if link[0] == line]
    for n, send in zip(chosen, sends):
        pack_side(state_ref, list_ref, send, line, ups[n], slots)


def pack_kernel(line, slots, links, place_ref, state_ref, list_ref, *sends):
    pack_links(slots, links, place_ref, state_ref, list_ref, sends, line)


def late_pack_kernel(line, slots, links, place_ref, state_ref, list_ref, grad_ref, *sends):
    pack_links(slots, links, place_ref, state_ref, list_ref, sends, line)


def spread_material(mat_ref, med_ref):
    low = half_of() == 0
    for node in range(NODES):
        rows = []
        for m in range(3):
            first = jnp.broadcast_to(mat_ref[m, node : node + 1, 0:LANES], (SUBS, LANES))
            second = jnp.broadcast_to(mat_ref[m, node : node + 1, LANES : 2 * LANES], (SUBS, LANES))
            rows.append(jnp.where(low, first, second))
        lam, mu, buoy = rows
        speed = jnp.sqrt((lam + 2.0 * mu) * buoy)
        for m, value in enumerate((lam, mu, buoy, speed)):
            med_ref[m * NODES + node] = step_size * value


def first_kernel(slots, links, counts_ref, state_ref, med_ref, codes_ref, acc_ref, grad_ref, live_ref, products):
    lane = lax.broadcasted_iota(jnp.int32, (SUBS, LANES), 1)
    count = jnp.broadcast_to(counts_ref[...].reshape(1, 1), (SUBS, LANES))
    live_ref[...] = jnp.where(half_of() * LANES + lane < count, 1.0, 0.0)
    volume_pass(state_ref, acc_ref, med_ref, products, lambda own, row: own, lambda value: value)
    shot_sums(products, store_gradient(live_ref, [grad_ref], None))
    local_pass(state_ref, acc_ref, med_ref, codes_ref, slots, 0.5 * lift_weight)


def store_gradient(live_ref, grad_refs, earlier_ref):
    alive = [jnp.broadcast_to(live_ref[4 * h : 4 * h + 1, :], (SUBS, LANES)) > 0.0 for h in range(2)]

    def emit(m, start, rows, h, value):
        at = (m, slice(start, start + rows), slice(h * LANES, (h + 1) * LANES))
        if earlier_ref is not None:
            value = (0.5 * step_size) * (earlier_ref[at] + value)
        value = jnp.where(alive[h][:rows], value, 0.0)
        for grad_ref in grad_refs:
            size = grad_ref.shape[1]
            if 0 <= start < size:
                grad_ref[m, start : start + rows, h * LANES : (h + 1) * LANES] = value
            start -= size

    return emit


def add_ghosts(links, place_ref, acc_ref, med_ref, codes_ref, ghosts, slots, scale):
    ups = link_ups(place_ref, links)
    paired = link_paired(place_ref, links, ups)
    for link, up, pair_here, ghost in zip(links, ups, paired, ghosts):
        ghost_pass(acc_ref, med_ref, codes_ref, ghost, link[0], up, pair_here, slots, scale)


def add_others(links, place_ref, state_ref, acc_ref, med_ref, codes_ref, ghosts, outer, slots, scale):
    ups = link_ups(place_ref, links)
    paired = link_paired(place_ref, links, ups)
    axes = [link[0] for link in links]
    other_sources(state_ref, acc_ref, med_ref, codes_ref, ghosts, ups, paired, axes, outer, slots, scale)


def middle_kernel(slots, links, place_ref, acc_in, state_ref, med_ref, codes_ref, *rest):
    ghosts, (mid_ref, outer) = rest[: len(links)], rest[len(links) :]
    add_ghosts(links, place_ref, mid_ref, med_ref, codes_ref, ghosts, slots, 0.5 * lift_weight)
    add_others(links, place_ref, state_ref, mid_ref, med_ref, codes_ref, ghosts, outer, slots, 0.5 * lift_weight)


def second_volume_kernel(
    slots, links, live_ref, mid_ref, state_ref, med_ref, first_ref, acc_ref, near_ref, far_ref, products
):
    share = 0.5 * live_ref[...]
    volume_pass(
        mid_ref, acc_ref, med_ref, products,
        lambda own, row: share * (own + state_ref[row]), lambda value: share * value,
    )
    shot_sums(products, store_gradient(live_ref, [near_ref, far_ref], first_ref))


def second_faces_kernel(slots, links, live_ref, acc_in, mid_ref, med_ref, codes_ref, acc_ref):
    weight = (0.25 * lift_weight) * live_ref[...]
    local_pass(mid_ref, acc_ref, med_ref, codes_ref, slots, weight)


def second_ghosts_kernel(slots, links, place_ref, acc_in, mid_ref, med_ref, codes_ref, *rest):
    ghosts, (acc_ref, outer) = rest[: len(links)], rest[len(links) :]
    add_ghosts(links, place_ref, acc_ref, med_ref, codes_ref, ghosts, slots, 0.25 * lift_weight)
    add_others(links, place_ref, mid_ref, acc_ref, med_ref, codes_ref, ghosts, outer, slots, 0.25 * lift_weight)


def partial_kernel(slots, links, acc_in, a_ref, b_ref, near_ref, far_ref, acc_ref, first_ref, second_ref):
    first_ref[...] = a_ref[...] + near_ref[...]
    second_ref[...] = b_ref[...] + far_ref[...]


def store_copies(acc_ref, fwd_hbm, adj_hbm, sems):
    copies = []
    for k in range(FIELDS):
        span = pl.ds(k * NODES, NODES)
        for n, far in enumerate((fwd_hbm, adj_hbm)):
            copies.append(pltpu.make_async_copy(acc_ref.at[span, :, n], far.at[span], sems.at[n, k]))
            copies[-1].start()
    return copies


def store_kernel(slots, links, acc_ref, fwd_hbm, adj_hbm, sems):
    for copy in store_copies(acc_ref, fwd_hbm, adj_hbm, sems):
        copy.wait()


def store_and_sum_kernel(
    slots, links, acc_ref, a_ref, b_ref, c_ref, d_ref, fwd_hbm, adj_hbm, grad_hbm, sems, grad_ref, grad_sem
):
    copies = store_copies(acc_ref, fwd_hbm, adj_hbm, sems)
    cut = a_ref.shape[1]
    grad_ref[:, :cut] = a_ref[...] + c_ref[...]
    grad_ref[:, cut:] = b_ref[...] + d_ref[...]
    copies.append(pltpu.make_async_copy(grad_ref, grad_hbm, grad_sem))
    copies[-1].start()
    for copy in copies:
        copy.wait()


def tree_links(devices):
    links = []
    for axis, stride in ((0, DEV_Y), (1, 1)):
        for parity in range(2):
            pairs = [(d, d + stride) for d in range(devices - stride) if (d // stride) % 2 == parity]
            if pairs:
                alone = set(range(devices)) - {d for pair in pairs for d in pair}
                route = pairs + [(b, a) for a, b in pairs] + [(d, d) for d in sorted(alone)]
                links.append((axis, stride, parity, devices, route))
    return links


def swapped(block, axis, distance):
    route = [(i, i ^ distance) for i in range(lax.axis_size(axis))]
    return lax.ppermute(block, axis, route)


def shards(forward, adjoint, material, counts, send_list, neighbours):
    shots, fields, nodes, slots = forward.shape
    halves = slots // LANES
    rows = fields * nodes
    assert 2 * shots * halves == SUBS and nodes == NODES and fields == FIELDS

    def dense(values):
        cut = values.reshape(shots, fields, nodes, halves, LANES)
        tiles = cut.transpose(1, 2, 3, 0, 4).reshape(rows, halves, shots, LANES)
        return pltpu.with_memory_space_constraint(tiles, pltpu.HBM)

    def restored(values):
        cut = values.reshape(fields, nodes, halves, shots, LANES)
        return cut.transpose(3, 0, 1, 2, 4).reshape(shots, fields, nodes, slots)

    links = tree_links(lax.axis_size("dom"))
    axes = tuple(link[:4] for link in links)
    place = lax.axis_index("dom").astype(jnp.int32).reshape(1)

    def exchange(sends, line):
        routes = [link[4] for link in links if link[0] == line]
        return [lax.ppermute(send, "dom", route) for send, route in zip(sends, routes)]

    vmem = pl.BlockSpec(memory_space=pltpu.VMEM)
    smem = pl.BlockSpec(memory_space=pltpu.SMEM)
    hbm = pl.BlockSpec(memory_space=pltpu.HBM)
    f32 = jnp.float32
    state_shape = pltpu.VMEM((rows, SUBS, LANES), f32)
    send_shape = pltpu.VMEM((FACE + 4, SUBS, LANES), f32)
    med_shape = pltpu.VMEM((4 * nodes, SUBS, LANES), f32)
    grad_shape = pltpu.VMEM(material.shape, f32)
    apart = (rows, halves, 2, shots, LANES)
    part_shape = jax.ShapeDtypeStruct((rows, halves, shots, LANES), f32)
    products = pltpu.VMEM((3 * LANES * SUBS, LANES), f32)
    outer = pltpu.VMEM((FIELDS, SUBS, LANES), f32)
    field_sems = pltpu.SemaphoreType.DMA((2, FIELDS))

    def call(kernel, out_shape, in_specs, name, micros, scratch=(), out_specs=None, aliases=None):
        return pl.pallas_call(
            functools.partial(kernel, slots, axes),
            out_shape=out_shape,
            in_specs=in_specs,
            out_specs=out_specs or [vmem] * len(out_shape),
            scratch_shapes=list(scratch),
            input_output_aliases=aliases or {},
            compiler_params=pltpu.CompilerParams(vmem_limit_bytes=VMEM_BYTES),
            cost_estimate=pl.CostEstimate(flops=int(micros * 10**9), bytes_accessed=0, transcendentals=0),
            name=name,
        )

    count = len(links)
    state, med = call(
        load_kernel, [pltpu.VMEM(apart, f32), med_shape], [hbm] * 3, "load", 4,
        [pltpu.VMEM(material.shape, f32), field_sems, pltpu.SemaphoreType.DMA],
    )(
        pltpu.with_memory_space_constraint(material, pltpu.HBM), dense(forward), dense(adjoint),
    )
    state = state.reshape(rows, SUBS, LANES)
    by_line = [[send_shape for link in links if link[0] == line] for line in range(2)]
    across = len(by_line[0])
    ghosts = []
    for line in range(2):
        sends = call(functools.partial(pack_kernel, line), by_line[line], [smem, vmem, vmem], "pack", 0)(
            place, state, send_list
        )
        ghosts += exchange(sends, line)
    acc, grad_first, live = call(
        first_kernel, [state_shape, grad_shape, pltpu.VMEM((SUBS, LANES), f32)], [vmem] + [vmem] * 3, "first_section", 8, [products]
    )(counts, state, med, neighbours)
    (mid,) = call(
        middle_kernel, [state_shape], [smem] + [vmem] * (4 + count), "first_ghosts", 4, [outer], aliases={1: 0}
    )(place, acc, state, med, neighbours, *ghosts)
    cut = (nodes // 2 + SUBS // 2) // SUBS * SUBS
    part_shapes = [pltpu.VMEM((3, size, slots), f32) for size in (cut, nodes - cut)]
    acc, *halved = call(
        second_volume_kernel, [state_shape] + part_shapes, [vmem] + [vmem] * 4, "second_volume", 0, [products]
    )(live, mid, state, med, grad_first)
    ghosts = []
    for line in range(2):
        sends = call(
            functools.partial(late_pack_kernel, line), by_line[line], [smem] + [vmem] * 3, "pack", 0.25
        )(place, mid, send_list, halved[0])
        ghosts += exchange(sends, line)
    doubling = lax.axis_size("shot") == 4
    if doubling:
        pieces = [swapped(halved[0], "shot", 1), swapped(halved[1], "shot", 2)]
    if doubling:
        acc, *parts = call(
            partial_kernel, [state_shape] + part_shapes, [vmem] * 5, "gradient_partial", 0, aliases={0: 0}
        )(acc, *halved, *pieces)
        pieces = [swapped(parts[0], "shot", 2), swapped(parts[1], "shot", 1)]
    else:
        gradient = lax.psum(jnp.concatenate(halved, axis=1), "shot")
    (acc,) = call(
        second_faces_kernel, [state_shape], [vmem] * 5, "second_faces", 0.5, aliases={1: 0}
    )(live, acc, mid, med, neighbours)

    (acc,) = call(
        second_ghosts_kernel, [state_shape], [smem] + [vmem] * (4 + count), "second_ghosts", 1, [outer], aliases={1: 0}
    )(place, acc, mid, med, neighbours, *ghosts)
    if doubling:
        fwd, adj, gradient = call(
            store_and_sum_kernel, [part_shape, part_shape, jax.ShapeDtypeStruct(material.shape, f32)], [vmem] * 5,
            "store", 4, [field_sems, pltpu.VMEM(material.shape, f32), pltpu.SemaphoreType.DMA], [hbm] * 3,
        )(acc.reshape(apart), *parts, *pieces)
    else:
        fwd, adj = call(store_kernel, [part_shape] * 2, [vmem], "store", 4, [field_sems], [hbm] * 2)(
            acc.reshape(apart)
        )
    return restored(fwd), restored(adj), gradient


def solution(mesh):
    placed = (
        P("shot", None, None, "dom"),
        P("shot", None, None, "dom"),
        P(None, None, "dom"),
        P("dom"),
        P("dom", None, None),
        P("dom", None),
    )
    return jax.shard_map(
        shards,
        mesh=mesh,
        in_specs=placed,
        out_specs=(
            P("shot", None, None, "dom"),
            P("shot", None, None, "dom"),
            P(None, None, "dom"),
        ),
        check_vma=False,
    )
```
